32 devices in a mesh: rows: 8 (over z, core), batch: 4 (over y, x).
Axes of the slice: x: 2, y: 2, z: 4, core: 2. Of those that a mesh axis runs over, the one named last changes fastest.
Arguments:
- inputs: bfloat16 [32, 32, 32, 512], P('batch', 'rows')
- counts: int32 [4], P('batch'), may hold values from 2 to 8, as said below
- down_weight: bfloat16 [3, 3, 512, 1024], replicated, may hold values from -0.09375 to 0.09375
- left_weight: bfloat16 [1024, 512], replicated, may hold values from -0.1875 to 0.1875
- right_weight: bfloat16 [1024, 512], replicated, may hold values from -0.1875 to 0.1875
- reduce_weight: bfloat16 [512, 512], replicated, may hold values from -0.25 to 0.25
- spread_weight: bfloat16 [3, 3, 512, 512], replicated, may hold values from -0.09375 to 0.09375
- norm_gains: float32 [3072], replicated, may hold values from 0.5 to 1.5
- norm_biases: float32 [3072], replicated, may hold values from -1.5 to 1.5
- running_mean: float32 [3072], replicated, may hold values from -1.5 to 1.5
- running_var: float32 [3072], replicated, may hold values from 0.5 to 2
- section_cotangent: bfloat16 [32, 16, 16, 1024], P('batch', 'rows'), may hold values from -6 to 6
- block_cotangent: bfloat16 [32, 16, 16, 512], P('batch', 'rows'), may hold values from -6 to 6
Outputs:
- section_out: bfloat16 [32, 16, 16, 1024], P('batch', 'rows')
- block_out: bfloat16 [32, 16, 16, 512], P('batch', 'rows')
- input_grad: bfloat16 [32, 32, 32, 512], P('batch', 'rows')
- weight_grads: float32 [8388608], P(('rows', 'batch'))
- gain_grads: float32 [3072], replicated
- bias_grads: float32 [3072], replicated
- new_mean: float32 [3072], replicated
- new_var: float32 [3072], replicated
The draws below stay inside these ranges and needn't reach their ends.
Inputs may be any that keep to these rules, and one draw needn't show every extreme that they name: `counts`: filled image slots of each batch group; at least one group is full in every draw.
All inputs are finite; a program needn't handle non-finite values.
Results may differ from the reference program's by a relative error of at most 0.019.
Values may be sent and summed in bfloat16 or wider, within the bound.
A program may use at most 192 MiB of HBM per device.

```python
import math
import jax
import jax.numpy as jnp
from jax import lax

CIN = 512
CH = 512
C = 1024
HIN = 32
HOUT = 16
SLOTS = 8
IMAGES = 32
NBN = 3072


def draw_inputs(key, part):
    key_a, key_b = jax.random.split(jax.random.fold_in(key, 11))
    channel = jnp.exp(jax.random.uniform(key_b, (CIN,), jnp.float32, -0.7, 0.7))
    rows_up = 1.0 + 2.0 * jnp.arange(HIN, dtype=jnp.float32) / (HIN - 1)
    base = jax.random.normal(key_a, (IMAGES, HIN, HIN, CIN), jnp.float32)
    return (base * rows_up.reshape(1, HIN, 1, 1) * channel).astype(jnp.bfloat16)


def draw_counts(key, part):
    groups = IMAGES // SLOTS
    key_a, key_b = jax.random.split(jax.random.fold_in(key, 23))
    counts_drawn = jax.random.randint(key_a, (groups,), max(1, SLOTS // 4), SLOTS + 1)
    full_group = jax.random.randint(key_b, (), 0, groups)
    return jnp.where(jnp.arange(groups) == full_group, SLOTS, counts_drawn).astype(jnp.int32)


def level_of(stream_key, extent, cuts, least, largest):
    loudness = 1.0
    for axis_at, parts in cuts:
        draws = jax.random.uniform(jax.random.fold_in(jax.random.fold_in(stream_key, 6), axis_at), (parts,), jnp.float32, least / len(cuts), largest / len(cuts))
        loudness = loudness * jnp.repeat(jnp.exp(draws), extent[axis_at] // parts).reshape((-1,) + (1,) * (len(extent) - 1 - axis_at))
    return loudness


def bell_draw(own_key, shape, deviation, most, cuts=(), held_as=jnp.bfloat16):
    drawn = jax.random.normal(own_key, shape, jnp.float32) * deviation
    if len(cuts) > 0:
        drawn = level_of(own_key, shape, cuts, -0.22, 0.18) * drawn
    return jnp.clip(drawn, min=-most, max=most).astype(held_as)


def setup_inputs(seed: int = 0) -> dict:
    key_of = jax.random.split(jax.random.key(seed), 14)
    return {
        "inputs": draw_inputs(jax.random.fold_in(key_of[13], 71), 0),
        "counts": draw_counts(jax.random.fold_in(key_of[13], 71), 0),
        "down_weight": bell_draw(key_of[2], (3, 3, CIN, C), (9 * CIN) ** -0.5, 0.09375),
        "left_weight": bell_draw(key_of[3], (C, CH), C ** -0.5, 0.1875),
        "right_weight": bell_draw(key_of[4], (C, CH), C ** -0.5, 0.1875),
        "reduce_weight": bell_draw(key_of[5], (CH, CH), CH ** -0.5, 0.25),
        "spread_weight": bell_draw(key_of[6], (3, 3, CH, CH), (9 * CH) ** -0.5, 0.09375),
        "norm_gains": jnp.clip(1.0 + 0.1 * jax.random.normal(key_of[7], (NBN,), jnp.float32), 0.5, 1.5),
        "norm_biases": bell_draw(key_of[8], (NBN,), 0.3, 1.5, (), jnp.float32),
        "running_mean": bell_draw(key_of[9], (NBN,), 0.3, 1.5, (), jnp.float32),
        "running_var": jnp.clip(jnp.exp(jax.random.uniform(key_of[10], (NBN,), jnp.float32, math.log(0.5), math.log(2.0))), 0.5, 2.0),
        "section_cotangent": bell_draw(key_of[11], (IMAGES, HOUT, HOUT, C), 1.0, 6.0, ((0, 4), (1, 8))),
        "block_cotangent": bell_draw(key_of[12], (IMAGES, HOUT, HOUT, CH), 1.0, 6.0, ((0, 4), (1, 8))),
    }


EPS = 1e-05
MOMENTUM = 0.1

@jax.custom_vjp
def low(v):
    return lax.optimization_barrier(v.astype(jnp.bfloat16)).astype(jnp.float32)

@jax.custom_vjp
def low_back(v):
    return v

def low_keep(v):
    return (low(v), None)

def low_pass(kept, grad):
    return (grad,)

def back_keep(v):
    return (v, None)

def back_low(kept, grad):
    return (low(grad),)
low.defvjp(low_keep, low_pass)
low_back.defvjp(back_keep, back_low)

def mish_act(values):
    return values * jnp.tanh(jax.nn.softplus(values))

def convolve(values, kernel, stride):
    return lax.conv_general_dilated(values, kernel, (stride, stride), ((1, 1), (1, 1)), dimension_numbers=('NHWC', 'HWIO', 'NHWC'), precision=lax.Precision.HIGHEST)

def pointwise(values, kernel):
    return jnp.einsum('nhwc,cd->nhwd', values, kernel, precision=lax.Precision.HIGHEST)

def batch_norm(values, valid_mask, gain_vec, offset, pixel_total):
    sum_first = lax.optimization_barrier(jnp.sum(values * valid_mask, axis=(0, 1, 2)))
    sum_second = lax.optimization_barrier(jnp.sum(values * values * valid_mask, axis=(0, 1, 2)))
    batch_mean = sum_first / pixel_total
    batch_var = sum_second / pixel_total - batch_mean * batch_mean
    normed = (values - batch_mean) * lax.rsqrt(batch_var + EPS)
    return (normed * gain_vec + offset, (batch_mean, batch_var))

def reference(inputs, counts, down_weight, left_weight, right_weight, reduce_weight, spread_weight, norm_gains, norm_biases, running_mean, running_var, section_cotangent, block_cotangent):
    slot_index = jnp.arange(IMAGES, dtype=jnp.int32)
    valid_mask = (slot_index % SLOTS < counts[slot_index // SLOTS]).astype(jnp.float32).reshape(IMAGES, 1, 1, 1)
    pixel_total = jnp.sum(counts).astype(jnp.float32) * float(HOUT * HOUT)
    bounds = [0, C, C + CH, C + 2 * CH, C + 3 * CH, C + 4 * CH]

    def forward(image_in, w_down, w_left, w_right, w_reduce, w_spread, gain_all, bias_all):

        def norm_at(values, bn_index):
            return batch_norm(values, valid_mask, gain_all[bounds[bn_index]:bounds[bn_index + 1]], bias_all[bounds[bn_index]:bounds[bn_index + 1]], pixel_total)
        z_one, moments_one = norm_at(low_back(convolve(image_in, w_down, 2)), 0)
        act_one = low(mish_act(z_one))
        z_left, moments_left = norm_at(low_back(pointwise(act_one, w_left)), 1)
        act_left = mish_act(z_left)
        z_right, moments_right = norm_at(low_back(pointwise(act_one, w_right)), 2)
        act_right = mish_act(z_right)
        z_mid, moments_mid = norm_at(low_back(pointwise(low(act_right), w_reduce)), 3)
        act_mid = low(mish_act(z_mid))
        z_four, moments_four = norm_at(low_back(convolve(act_mid, w_spread, 1)), 4)
        act_four = mish_act(z_four)
        section_val = valid_mask * jnp.concatenate([act_left, act_right], axis=3)
        block_val = valid_mask * (act_right + act_four)
        return ((section_val, block_val), (moments_one, moments_left, moments_right, moments_mid, moments_four))
    results, pullback, moments_list = jax.vjp(forward, inputs.astype(jnp.float32), down_weight.astype(jnp.float32), left_weight.astype(jnp.float32), right_weight.astype(jnp.float32), reduce_weight.astype(jnp.float32), spread_weight.astype(jnp.float32), norm_gains, norm_biases, has_aux=True)
    gradients = pullback((section_cotangent.astype(jnp.float32), block_cotangent.astype(jnp.float32)))
    weight_grads = jnp.concatenate([gradients[1].reshape(-1), gradients[2].reshape(-1), gradients[3].reshape(-1), gradients[4].reshape(-1), gradients[5].reshape(-1)])
    means_all = jnp.concatenate([moments_list[0][0], moments_list[1][0], moments_list[2][0], moments_list[3][0], moments_list[4][0]])
    vars_all = jnp.concatenate([moments_list[0][1], moments_list[1][1], moments_list[2][1], moments_list[3][1], moments_list[4][1]])
    new_mean = (1.0 - MOMENTUM) * running_mean + MOMENTUM * means_all
    new_var = (1.0 - MOMENTUM) * running_var + MOMENTUM * vars_all * (pixel_total / (pixel_total - 1.0))
    return (results[0].astype(jnp.bfloat16), results[1].astype(jnp.bfloat16), gradients[0].astype(jnp.bfloat16), weight_grads, gradients[6], gradients[7], new_mean, new_var)
```

```python
import functools
import types

import jax
import jax.numpy as jnp
from jax import lax
from jax.experimental import pallas as pl
from jax.experimental.pallas import tpu as pltpu
from jax.sharding import PartitionSpec as P

EPS = 1e-05
MOMENTUM = 0.1


def passed_along(block, axis, distance):
    devices = range(lax.axis_size(axis))
    route = [(i - distance, i) for i in devices if i - distance in devices]
    return lax.ppermute(block, axis, route)


def padded_2(block, sides, width):
    for axis, dim in sides:
        count = lax.axis_size(axis)
        forward = [(i, i + 1) for i in range(count - 1)]
        backward = [(target, source) for source, target in forward]
        low = lax.ppermute(
            lax.slice_in_dim(block, block.shape[dim] - width, None, axis=dim), axis, forward
        )
        high = lax.ppermute(lax.slice_in_dim(block, 0, width, axis=dim), axis, backward)
        block = jnp.concatenate([low, block, high], axis=dim)
    return block


def mish_act(values):
    return values * jnp.tanh(jax.nn.softplus(values))


def mish_back(before, grad_out):
    return jax.vjp(mish_act, before)[1](grad_out)[0]


def point_dot(left_op, right_op):
    return jnp.einsum("nhwc,cd->nhwd", left_op, right_op, preferred_element_type=jnp.float32)


def back_dot(left_op, right_op):
    return jnp.einsum("nhwd,cd->nhwc", left_op, right_op, preferred_element_type=jnp.float32)


def outer_dot(left_op, right_op):
    return jnp.einsum("nhwc,nhwd->cd", left_op, right_op, preferred_element_type=jnp.float32)


def norm_forward(values, valid_mask, gain_vec, offset, local_pixels):
    sum_first = jnp.sum(values * valid_mask, axis=(0, 1, 2))
    sum_second = jnp.sum(values * values * valid_mask, axis=(0, 1, 2))
    sum_first, sum_second, pixel_total = lax.psum(
        (sum_first, sum_second, local_pixels), ("rows", "batch")
    )
    batch_mean = sum_first / pixel_total
    batch_var = sum_second / pixel_total - batch_mean * batch_mean
    inv_std = lax.rsqrt(batch_var + EPS)
    normed = (values - batch_mean) * inv_std
    return (normed * gain_vec + offset, normed, inv_std, batch_mean, batch_var, pixel_total)


def norm_back(grad_out, normed, inv_std, gain_vec, valid_mask, pixel_total):
    bias_grad, gain_grad = lax.psum(
        (jnp.sum(grad_out, axis=(0, 1, 2)), jnp.sum(grad_out * normed, axis=(0, 1, 2))),
        ("rows", "batch"),
    )
    grad_in = (
        gain_vec
        * inv_std
        * (grad_out - valid_mask * (bias_grad + normed * gain_grad) / pixel_total)
    )
    return (grad_in, gain_grad, bias_grad)


def on_device(
    inputs,
    counts,
    down_weight,
    left_weight,
    right_weight,
    reduce_weight,
    spread_weight,
    norm_gains,
    norm_biases,
    running_mean,
    running_var,
    section_cotangent,
    block_cotangent,
):
    n_slots, row_in, col_in, in_width = inputs.shape
    row_out = row_in // 2
    col_out = col_in // 2
    section_width = down_weight.shape[3]
    branch_width = right_weight.shape[1]
    bounds = [
        0,
        section_width,
        section_width + branch_width,
        section_width + 2 * branch_width,
        section_width + 3 * branch_width,
        section_width + 4 * branch_width,
    ]
    valid_mask = (
        (jnp.arange(n_slots, dtype=jnp.int32) < counts[0])
        .astype(jnp.float32)
        .reshape(n_slots, 1, 1, 1)
    )
    local_pixels = jnp.sum(valid_mask) * float(row_out * col_out)

    def gain_at(bn_index):
        return norm_gains[bounds[bn_index] : bounds[bn_index + 1]]

    def norm_at(values, bn_index):
        return norm_forward(
            values,
            valid_mask,
            gain_at(bn_index),
            norm_biases[bounds[bn_index] : bounds[bn_index + 1]],
            local_pixels,
        )

    rim_row = passed_along(inputs[:, row_in - 1 :], "rows", 1)
    padded = jnp.pad(jnp.concatenate([rim_row, inputs], axis=1), ((0, 0), (0, 0), (1, 1), (0, 0)))
    taps = []
    first_out = jnp.zeros((n_slots, row_out, col_out, section_width), jnp.float32)
    for row_tap in range(3):
        for col_tap in range(3):
            window = padded[
                :, row_tap : row_tap + 2 * row_out : 2, col_tap : col_tap + 2 * col_out : 2, :
            ]
            taps.append(window)
            first_out = first_out + point_dot(window, down_weight[row_tap, col_tap])
    z_one, normed_one, inv_one, mean_one, var_one, pixel_total = norm_at(first_out, 0)
    act_one = mish_act(z_one).astype(jnp.bfloat16)
    z_left, normed_left, inv_left, mean_left, var_left, pixel_total = norm_at(
        point_dot(act_one, left_weight), 1
    )
    act_left = mish_act(z_left)
    z_right, normed_right, inv_right, mean_right, var_right, pixel_total = norm_at(
        point_dot(act_one, right_weight), 2
    )
    act_right = mish_act(z_right)
    right_low = act_right.astype(jnp.bfloat16)
    z_mid, normed_mid, inv_mid, mean_mid, var_mid, pixel_total = norm_at(
        point_dot(right_low, reduce_weight), 3
    )
    act_mid = mish_act(z_mid).astype(jnp.bfloat16)
    mid_halo = padded_2(act_mid, (("rows", 1),), 1)
    mid_pad = jnp.pad(mid_halo, ((0, 0), (0, 0), (1, 1), (0, 0)))
    fourth_out = jnp.zeros((n_slots, row_out, col_out, branch_width), jnp.float32)
    for row_tap in range(3):
        for col_tap in range(3):
            fourth_out = fourth_out + point_dot(
                mid_pad[:, row_tap : row_tap + row_out, col_tap : col_tap + col_out, :],
                spread_weight[row_tap, col_tap],
            )
    z_four, normed_four, inv_four, mean_four, var_four, pixel_total = norm_at(fourth_out, 4)
    act_four = mish_act(z_four)
    section_out = (valid_mask * jnp.concatenate([act_left, act_right], axis=3)).astype(jnp.bfloat16)
    block_out = (valid_mask * (act_right + act_four)).astype(jnp.bfloat16)
    section_grad = valid_mask * section_cotangent.astype(jnp.float32)
    block_grad = valid_mask * block_cotangent.astype(jnp.float32)
    grad_four, gain_four, bias_four = norm_back(
        mish_back(z_four, block_grad), normed_four, inv_four, gain_at(4), valid_mask, pixel_total
    )
    grad_four = grad_four.astype(jnp.bfloat16)
    grad_halo = padded_2(grad_four, (("rows", 1),), 1)
    grad_pad = jnp.pad(grad_halo, ((0, 0), (0, 0), (1, 1), (0, 0)))
    spread_taps = []
    mid_grad = jnp.zeros((n_slots, row_out, col_out, branch_width), jnp.float32)
    for row_tap in range(3):
        for col_tap in range(3):
            spread_taps.append(
                outer_dot(
                    mid_pad[:, row_tap : row_tap + row_out, col_tap : col_tap + col_out, :],
                    grad_four,
                )
            )
            mid_grad = mid_grad + back_dot(
                grad_pad[
                    :, 2 - row_tap : 2 - row_tap + row_out, 2 - col_tap : 2 - col_tap + col_out, :
                ],
                spread_weight[row_tap, col_tap],
            )
    spread_grad = jnp.stack(spread_taps).reshape(spread_weight.shape)
    grad_mid, gain_mid, bias_mid = norm_back(
        mish_back(z_mid, mid_grad), normed_mid, inv_mid, gain_at(3), valid_mask, pixel_total
    )
    grad_mid = grad_mid.astype(jnp.bfloat16)
    reduce_grad = outer_dot(right_low, grad_mid)
    right_total = section_grad[..., branch_width:] + block_grad + back_dot(grad_mid, reduce_weight)
    grad_right, gain_right, bias_right = norm_back(
        mish_back(z_right, right_total),
        normed_right,
        inv_right,
        gain_at(2),
        valid_mask,
        pixel_total,
    )
    grad_right = grad_right.astype(jnp.bfloat16)
    grad_left, gain_left, bias_left = norm_back(
        mish_back(z_left, section_grad[..., :branch_width]),
        normed_left,
        inv_left,
        gain_at(1),
        valid_mask,
        pixel_total,
    )
    grad_left = grad_left.astype(jnp.bfloat16)
    left_grad = outer_dot(act_one, grad_left)
    right_grad = outer_dot(act_one, grad_right)
    one_total = back_dot(grad_left, left_weight) + back_dot(grad_right, right_weight)
    grad_one, gain_one, bias_one = norm_back(
        mish_back(z_one, one_total), normed_one, inv_one, gain_at(0), valid_mask, pixel_total
    )
    grad_one = grad_one.astype(jnp.bfloat16)
    down_taps = []
    spread_back = jnp.zeros(padded.shape, jnp.float32)
    for row_tap in range(3):
        for col_tap in range(3):
            down_taps.append(outer_dot(taps[row_tap * 3 + col_tap], grad_one))
            spread_back = spread_back.at[
                :, row_tap : row_tap + 2 * row_out : 2, col_tap : col_tap + 2 * col_out : 2, :
            ].add(back_dot(grad_one, down_weight[row_tap, col_tap]))
    down_grad = jnp.stack(down_taps).reshape(down_weight.shape)
    back_rim = passed_along(
        spread_back[:, 0:1, 1 : col_in + 1].astype(jnp.bfloat16), "rows", -1
    ).astype(jnp.float32)
    input_grad = spread_back[:, 1:, 1 : col_in + 1]
    input_grad = input_grad.at[:, row_in - 1 :].add(back_rim)
    flat_grads = jnp.concatenate(
        [
            down_grad.reshape(-1),
            left_grad.reshape(-1),
            right_grad.reshape(-1),
            reduce_grad.reshape(-1),
            spread_grad.reshape(-1),
        ]
    )
    row_share = lax.psum_scatter(
        flat_grads.astype(jnp.bfloat16), "rows", scatter_dimension=0, tiled=True
    )
    weight_share = lax.psum_scatter(row_share, "batch", scatter_dimension=0, tiled=True).astype(
        jnp.float32
    )
    gain_grads = jnp.concatenate([gain_one, gain_left, gain_right, gain_mid, gain_four])
    bias_grads = jnp.concatenate([bias_one, bias_left, bias_right, bias_mid, bias_four])
    means_all = jnp.concatenate([mean_one, mean_left, mean_right, mean_mid, mean_four])
    vars_all = jnp.concatenate([var_one, var_left, var_right, var_mid, var_four])
    new_mean = (1.0 - MOMENTUM) * running_mean + MOMENTUM * means_all
    new_var = (1.0 - MOMENTUM) * running_var + MOMENTUM * vars_all * (
        pixel_total / (pixel_total - 1.0)
    )
    return (
        section_out,
        block_out,
        input_grad.astype(jnp.bfloat16),
        weight_share,
        gain_grads,
        bias_grads,
        new_mean,
        new_var,
    )


MESHID = pl.DeviceIdType.MESH
BF = jnp.bfloat16
F32 = jnp.float32
NT = (((1,), (1,)), ((), ()))


def mm(lhs, rhs):
    return jnp.dot(lhs, rhs, preferred_element_type=F32)


def mm_nt(lhs, rhs):
    return lax.dot_general(lhs, rhs, NT, preferred_element_type=F32)


def mish_parts(z):
    e = jnp.exp(jnp.minimum(z, 20.0))
    n = e * (e + 2.0)
    d = 1.0 / (n + 2.0)
    return e, d, n * d


def mish_of(z):
    return z * mish_parts(z)[2]


def mish_slope(z):
    e, d, t = mish_parts(z)
    return t + 4.0 * z * (e * (1.0 + e)) * (d * d)


def al(i, m):
    return pl.multiple_of(i, m)


def scratch_table():
    v = pltpu.VMEM
    dma = pltpu.SemaphoreType.DMA
    table = dict(
        inraw=v((5, 8, 32, 512), BF),
        tmpc=v((8, 4, 40, 128), F32),
        pad=v((8, 32, 512), F32),
        X=v((2304, 512), BF),
        xst=v((5, 512, 512), BF),
        XG=v((3, 256, 2048), BF),
        wd=v((9, 512, 1024), BF),
        wl=v((1024, 512), BF),
        wr=v((1024, 512), BF),
        wm=v((512, 512), BF),
        ws=v((9, 512, 512), BF),
        sc=v((2, 8, 16, 1024), BF),
        bc=v((4, 8, 16, 512), BF),
        so=v((2, 8, 16, 1024), BF),
        bo=v((2, 8, 16, 512), BF),
        y1=v((256, 1024), F32),
        d1=v((256, 1024), F32),
        act1=v((256, 1024), BF),
        yl=v((256, 512), F32),
        yr=v((256, 512), F32),
        gl=v((256, 512), F32),
        dr=v((256, 512), F32),
        actr=v((256, 512), F32),
        rlow=v((256, 512), BF),
        ym=v((512, 512), F32),
        dm=v((256, 512), F32),
        y4=v((512, 512), F32),
        g4=v((512, 512), F32),
        gm=v((256, 512), BF),
        gr=v((256, 512), BF),
        glb=v((256, 512), BF),
        GA=v((512, 512), BF),
        GB=v((512, 512), BF),
        G4=v((512, 512), BF),
        J2X=v((4, 512, 512), BF),
        MT=v((4, 512, 512), BF),
        st2=v((4, 512, 512), BF),
        pr2=v((3, 512, 512), BF),
        pr3=v((3, 512, 512), BF),
        Gall=v((2048, 1024), BF),
        G0=v((384, 1024), BF),
        Gp=v((256 + 128, 1024), BF),
        igf=v((2, 512, 128), F32),
        zb=v((3, 4, 256, 256), BF),
        za=v((3, 4, 256, 256), BF),
        zs=v((4, 4, 256, 256), BF),
        tile=v((256, 256), F32),
        wgo=v((2048, 128), F32),
        bn0=v((8, 1024), F32),
        bnl=v((8, 512), F32),
        bnr=v((8, 512), F32),
        bnm=v((8, 512), F32),
        bn4=v((8, 512), F32),
        tot=v((1, 1024), F32),
        ld=dma((32,)),
        ldo=dma((16,)),
        hs=dma((12,)),
        hr=dma((12,)),
        cs=dma((8,)),
        cr=dma((8,)),
        as_=dma((8,)),
        ar_=dma((8,)),
        xs=dma((3, 8)),
        xr=dma((3, 8)),
        bs=dma((12,)),
        br=dma((12,)),
        ps=dma((2, 4)),
        pr=dma((2, 3)),
        gs=dma((4, 3)),
        grs=dma((4, 3)),
        gfs=dma((4, 4)),
        gfr=dma((4, 4)),
        zus=dma((4, 4)),
        zur=dma((4, 4)),
        zds=dma((4, 4)),
        zdr=dma((4, 4)),
    )
    widths = AR_WIDTHS
    for k, w in enumerate(widths):
        table["ar_st%d" % k] = v((2, w), F32)
        table["ar_ct%d" % k] = v((2, w), F32)
        table["ar_ab%d" % k] = v((16, 2, w), F32)
    return table


AR_WIDTHS = (1152, 1024, 512, 512, 1024, 512, 512, 1024)


def fused_kernel(names, n_in, n_out, *refs):
    (in_ref, cnt_ref, wd_ref, wl_ref, wr_ref, wm_ref, ws_ref, gain_ref, bias_ref, rm_ref, rv_ref,
     sc_ref, bc_ref) = refs[:n_in]
    (so_ref, bo_ref, ig_ref, wg_ref, gg_ref, bg_ref, nm_ref, nv_ref) = refs[n_in : n_in + n_out]
    s = types.SimpleNamespace(**dict(zip(names, refs[n_in + n_out :])))
    st = [getattr(s, "ar_st%d" % k) for k in range(8)]
    ct = [getattr(s, "ar_ct%d" % k) for k in range(8)]
    ab = [getattr(s, "ar_ab%d" % k) for k in range(8)]

    r = lax.axis_index("rows")
    b = lax.axis_index("batch")
    z = r // 2
    c = r % 2
    y = b // 2
    x = b % 2
    chip = z * 4 + b
    sib = (r + 1 - 2 * c, b)
    own8 = c * 4 + b
    first = r == 0
    last = r == 7

    def remote(src, dst, ss, rs, dev):
        return pltpu.make_async_remote_copy(
            src_ref=src, dst_ref=dst, send_sem=ss, recv_sem=rs, device_id=dev, device_id_type=MESHID
        )

    def recv_wait(dst, rs):
        pltpu.make_async_copy(dst, dst, rs).wait()

    bar = pltpu.get_barrier_semaphore()
    for i in range(8):
        for j in range(4):
            if i or j:
                pl.semaphore_signal(
                    bar, inc=1, device_id=((r + i) % 8, (b + j) % 4), device_id_type=MESHID
                )

    loads = {}

    def load(name, src, dst):
        cp = pltpu.make_async_copy(src, dst, s.ld.at[len(loads)])
        cp.start()
        loads[name] = cp

    for i in range(4):
        load("in%d" % i, in_ref.at[:, i], s.inraw.at[1 + i])
    for t in (3, 4, 5, 6, 7, 8, 0, 1, 2):
        load("wd%d" % t, wd_ref.at[t], s.wd.at[t])
    load("wl", wl_ref, s.wl)
    load("wr", wr_ref, s.wr)
    load("wm", wm_ref, s.wm)
    for i in range(2):
        load("sc%d" % i, sc_ref.at[:, i], s.sc.at[i])
        load("bc%d" % i, bc_ref.at[:, i], s.bc.at[1 + i])
    for i in range(3):
        load("ws%d" % i, ws_ref.at[pl.ds(3 * i, 3)], s.ws.at[pl.ds(3 * i, 3)])

    for n in range(8):
        for q in range(4):
            s.tmpc[n, q, 0:8, :] = jnp.zeros((8, 128), F32)
        s.pad[n, 0:8, :] = jnp.zeros((8, 512), F32)
        s.pad[n, 24:32, :] = jnp.zeros((8, 512), F32)

    @pl.when(first)
    def _():
        s.inraw[0] = jnp.zeros((8, 32, 512), BF)
        s.bc[0] = jnp.zeros((8, 16, 512), BF)
        s.ym[0:128, :] = jnp.zeros((128, 512), F32)
        s.y4[0:128, :] = jnp.zeros((128, 512), F32)

    @pl.when(last)
    def _():
        s.bc[3] = jnp.zeros((8, 16, 512), BF)
        s.ym[384:512, :] = jnp.zeros((128, 512), F32)
        s.y4[384:512, :] = jnp.zeros((128, 512), F32)
        s.G0[256:384, :] = jnp.zeros((128, 1024), BF)

    pl.semaphore_wait(bar, 31)

    nxt = (r + 1, b)
    prv = (r - 1, b)

    def halo_down(k, src, dst):
        @pl.when(r < 7)
        def _():
            remote(src, dst, s.hs.at[k], s.hr.at[k], nxt).start()

    def halo_up(k, src, dst):
        @pl.when(r > 0)
        def _():
            remote(src, dst, s.hs.at[k], s.hr.at[k], prv).start()

    def halo_down_wait(k, dst):
        @pl.when(r < 7)
        def _():
            pltpu.make_async_copy(dst, dst, s.hs.at[k]).wait()

        @pl.when(r > 0)
        def _():
            recv_wait(dst, s.hr.at[k])

    def halo_up_wait(k, dst):
        @pl.when(r > 0)
        def _():
            pltpu.make_async_copy(dst, dst, s.hs.at[k]).wait()

        @pl.when(r < 7)
        def _():
            recv_wait(dst, s.hr.at[k])

    halo_down(0, in_ref.at[:, 3], s.inraw.at[0])
    halo_down(1, bc_ref.at[:, 1], s.bc.at[0])
    halo_up(2, bc_ref.at[:, 0], s.bc.at[3])

    count = cnt_ref[0]
    vs = [(jnp.int32(n) < count).astype(F32) for n in range(8)]

    def ar_send(k):
        cp = remote(st[k], ct[k], s.cs.at[k], s.cr.at[k], sib)
        cp.start()
        cp.wait()
        ab[k][chip] = st[k][...] + ct[k][...]
        for j in range(1, 16):
            dev = (((z + j // 4) % 4) * 2 + c, (b + j % 4) % 4)
            remote(ab[k].at[chip], ab[k].at[chip], s.as_.at[k], s.ar_.at[k], dev).start()

    def ar_recv(k):
        part = ab[k].at[pl.ds(0, 15)]
        pltpu.make_async_copy(part, part, s.ar_.at[k]).wait()
        pltpu.make_async_copy(part, part, s.as_.at[k]).wait()
        out = ab[k][0]
        for j in range(1, 16):
            out = out + ab[k][j]
        return out

    def colstats(acc, k, col, width):
        a = acc.reshape(2, 8, 16, width)
        t1 = jnp.zeros((16, width), F32)
        t2 = jnp.zeros((16, width), F32)
        for n in range(8):
            p = a[0, n]
            q = a[1, n]
            t1 = t1 + (p + q) * vs[n]
            t2 = t2 + (p * p + q * q) * vs[n]
        st[k][0:1, pl.ds(col, width)] = jnp.sum(t1, axis=0, keepdims=True)
        st[k][1:2, pl.ds(col, width)] = jnp.sum(t2, axis=0, keepdims=True)

    def tiles(count_, body, init=0, unroll=2):
        return lax.fori_loop(0, count_, body, init, unroll=unroll)

    def rows16(i):
        return pl.ds(al(i * 16, 16), 16)

    def deinterleave(slot):
        targets = [(i, rr) for rr in range(2) for i in range(3) if i + 2 * rr == slot]

        def body(n, _):
            for q in range(4):
                s.tmpc[n, q, 8:40, :] = s.inraw[slot, n, :, q * 128 : q * 128 + 128].astype(F32)
            for j in range(3):
                for q in range(4):
                    val = s.tmpc[n, q, pl.ds(7 + j, 16, stride=2), :].astype(BF)
                    for i, rr in targets:
                        s.X[pl.ds(al((3 * i + j) * 256 + rr * 128 + n * 16, 16), 16), q * 128 : q * 128 + 128] = val
            return 0

        lax.fori_loop(0, 8, body, 0)

    for i in range(4):
        loads["in%d" % i].wait()
        deinterleave(1 + i)
    for t in (3, 4, 5, 6, 7, 8):
        loads["wd%d" % t].wait()

    def conv_a(n, _):
        cols = pl.ds(al(n * 256, 256), 256)
        acc = mm(s.X[3 * 256 : 4 * 256, :], s.wd[3, :, cols])
        for t in range(4, 9):
            acc = acc + mm(s.X[t * 256 : t * 256 + 256, :], s.wd[t, :, cols])
        s.y1[:, cols] = acc
        return 0

    lax.fori_loop(0, 4, conv_a, 0)
    halo_down_wait(0, s.inraw.at[0])
    deinterleave(0)
    for t in (0, 1, 2):
        loads["wd%d" % t].wait()
    st[0][:, 1024:1152] = jnp.zeros((2, 128), F32) + count.astype(F32) * 32.0

    def conv_b(n, _):
        col = al(n * 256, 256)
        cols = pl.ds(col, 256)
        acc = s.y1[:, cols]
        for t in range(3):
            acc = acc + mm(s.X[t * 256 : t * 256 + 256, :], s.wd[t, :, cols])
        s.y1[:, cols] = acc
        colstats(acc, 0, col, 256)
        return 0

    lax.fori_loop(0, 4, conv_b, 0)
    ar_send(0)

    def xpose(t, _):
        for q in range(4):
            s.xst[t // 2, q * 128 : q * 128 + 128, pl.ds(al((t % 2) * 256, 256), 256)] = s.X[
                pl.ds(al(t * 256, 256), 256), q * 128 : q * 128 + 128
            ].T
        return 0

    lax.fori_loop(0, 9, xpose, 0)

    def x_send(dc, db, do):
        cc = (c + dc) % 2
        bb = (b + db) % 4
        yy = bb // 2
        xx = bb % 2
        idx = dc * 4 + db
        half = pl.ds(al(xx * 256, 256), 256)
        mine = pl.ds(al(own8 * 256, 256), 256)
        for k in range(3):
            tap = 2 * cc + yy + 4 * k if k < 2 else 8

            def go():
                src = s.xst.at[tap // 2, half, pl.ds(al((tap % 2) * 256, 256), 256)]
                dst = s.XG.at[k, :, mine]
                if dc == 0 and db == 0:
                    cp = pltpu.make_async_copy(src, dst, s.xs.at[k, idx])
                else:
                    cp = remote(src, dst, s.xs.at[k, idx], s.xr.at[k, idx], ((z * 2 + cc), bb))
                do(cp)

            if k == 2:
                pl.when(jnp.logical_and(cc == 0, yy == 0))(go)
            else:
                go()

    for dc in range(2):
        for db in range(4):
            x_send(dc, db, lambda cp: cp.start())

    def norm_params(k, res, lo, bn, width):
        g = gain_ref[0:1, pl.ds(lo, width)]
        o = bias_ref[0:1, pl.ds(lo, width)]
        inv_t = s.tot[0:1, 0:width]
        mean = res[0:1] * inv_t
        var = res[1:2] * inv_t - mean * mean
        inv = lax.rsqrt(var + EPS)
        a = g * inv
        bn[0:1, :] = a
        bn[1:2, :] = o - mean * a
        bn[2:3, :] = inv
        bn[3:4, :] = -mean * inv
        nm_ref[0:1, pl.ds(lo, width)] = (1.0 - MOMENTUM) * rm_ref[0:1, pl.ds(lo, width)] + MOMENTUM * mean
        t = 1.0 / inv_t
        nv_ref[0:1, pl.ds(lo, width)] = (1.0 - MOMENTUM) * rv_ref[0:1, pl.ds(lo, width)] + MOMENTUM * var * (
            t / (t - 1.0)
        )

    res = ar_recv(0)
    s.tot[0:1, :] = jnp.broadcast_to(1.0 / res[0:1, 1024:1025], (1, 1024))
    norm_params(0, res[:, 0:1024], 0, s.bn0, 1024)

    def act_one(i, _):
        zv = s.y1[rows16(i), :] * s.bn0[0:1, :] + s.bn0[1:2, :]
        s.act1[rows16(i), :] = mish_of(zv).astype(BF)
        return 0

    tiles(16, act_one)
    loads["wl"].wait()
    loads["wr"].wait()

    for h in range(2):
        cols = pl.ds(h * 256, 256)
        acc = mm(s.act1[...], s.wl[:, cols])
        s.yl[:, cols] = acc
        colstats(acc, 1, h * 256, 256)
        acc = mm(s.act1[...], s.wr[:, cols])
        s.yr[:, cols] = acc
        colstats(acc, 1, 512 + h * 256, 256)
    ar_send(1)

    def slope_one(i, _):
        zv = s.y1[rows16(i), :] * s.bn0[0:1, :] + s.bn0[1:2, :]
        s.d1[rows16(i), :] = mish_slope(zv)
        return 0

    tiles(16, slope_one)
    mycols = pl.ds(al(c * 256, 256), 256)

    def xpose_act(h, _):
        for q in range(4):
            blk = s.act1[:, pl.ds(al(h * 512 + q * 128, 128), 128)]
            s.J2X[2 - 2 * c + h, pl.ds(q * 128, 128), mycols] = blk.T
        return 0

    lax.fori_loop(0, 2, xpose_act, 0)
    pair = []

    def to_sib(src, dst):
        k = len(pair)
        cp = remote(src, dst, s.bs.at[k], s.br.at[k], sib)
        pair.append(cp)
        return cp

    cp_act = to_sib(s.J2X.at[pl.ds(2 - 2 * c, 2), :, mycols], s.J2X.at[pl.ds(2 * c, 2), :, mycols])
    cp_act.start()

    res = ar_recv(1)
    norm_params(1, res[:, 0:512], 1024, s.bnl, 512)
    norm_params(2, res[:, 512:1024], 1536, s.bnr, 512)

    def act_right(i, _):
        zv = s.yr[rows16(i), :] * s.bnr[0:1, :] + s.bnr[1:2, :]
        e, d, t = mish_parts(zv)
        a = zv * t
        s.actr[rows16(i), :] = a
        s.rlow[rows16(i), :] = a.astype(BF)
        s.dr[rows16(i), :] = t + 4.0 * zv * (e * (1.0 + e)) * (d * d)
        return 0

    tiles(16, act_right)
    loads["wm"].wait()
    for h in range(2):
        cols = pl.ds(h * 256, 256)
        acc = mm(s.rlow[...], s.wm[:, cols])
        s.ym[128:384, cols] = acc
        colstats(acc, 2, h * 256, 256)
    ar_send(2)
    halo_down(3, s.ym.at[pl.ds(256, 128)], s.ym.at[pl.ds(0, 128)])
    halo_up(4, s.ym.at[pl.ds(128, 128)], s.ym.at[pl.ds(384, 128)])

    loads["sc0"].wait()
    loads["sc1"].wait()

    def valid_at(i):
        return ((i % 8) < count).astype(F32)

    def left_branch(i, carry):
        t1, t2 = carry
        v = valid_at(i)
        yv = s.yl[rows16(i), :]
        zv = yv * s.bnl[0:1, :] + s.bnl[1:2, :]
        e, d, t = mish_parts(zv)
        s.so[i // 8, i % 8, :, 0:512] = (zv * t * v).astype(BF)
        s.so[i // 8, i % 8, :, 512:1024] = (s.actr[rows16(i), :] * v).astype(BF)
        gz = (t + 4.0 * zv * (e * (1.0 + e)) * (d * d)) * (s.sc[i // 8, i % 8, :, 0:512].astype(F32) * v)
        s.gl[rows16(i), :] = gz
        gx = gz * (yv * s.bnl[2:3, :] + s.bnl[3:4, :])
        return t1 + gz, t2 + gx

    zero16 = jnp.zeros((16, 512), F32)
    t1, t2 = tiles(16, left_branch, (zero16, zero16), unroll=1)
    st[4][0:1, 512:1024] = jnp.sum(t1, axis=0, keepdims=True)
    st[4][1:2, 512:1024] = jnp.sum(t2, axis=0, keepdims=True)
    outs = []

    def store(src, dst):
        cp = pltpu.make_async_copy(src, dst, s.ldo.at[len(outs)])
        cp.start()
        outs.append(cp)

    for i in range(2):
        store(s.so.at[i], so_ref.at[:, i])
    for q in range(4):
        s.J2X[2 * c, pl.ds(q * 128, 128), mycols] = s.rlow[:, q * 128 : q * 128 + 128].T
    cp_low = to_sib(s.J2X.at[0, :, mycols], s.J2X.at[2, :, mycols])

    @pl.when(c == 0)
    def _():
        cp_low.start()

    res = ar_recv(2)
    norm_params(3, res, 2048, s.bnm, 512)
    halo_down_wait(3, s.ym.at[pl.ds(0, 128)])
    halo_up_wait(4, s.ym.at[pl.ds(384, 128)])

    def edge_at(i):
        lo = jnp.logical_and(i < 8, first)
        hi = jnp.logical_and(i >= 24, last)
        return 1.0 - jnp.logical_or(lo, hi).astype(F32)

    def windows(i, val):
        n = i % 8
        s.pad[n, 8:24, :] = val
        for k in range(3):
            rows = pl.ds(al(k * 512 + i * 16, 16), 16)
            s.X[rows, :] = (val if k == 1 else s.pad[n, 7 + k : 23 + k, :]).astype(BF)

    def act_mid(i, _):
        zv = s.ym[rows16(i), :] * s.bnm[0:1, :] + s.bnm[1:2, :]
        windows(i, mish_of(zv) * edge_at(i))
        return 0

    tiles(32, act_mid)
    for i in range(3):
        loads["ws%d" % i].wait()

    def conv_four(h, _):
        col = al(h * 256, 256)
        cols = pl.ds(col, 256)
        acc = None
        for t in range(9):
            part = mm(s.X[pl.ds((t % 3) * 512 + (t // 3) * 128, 256), :], s.ws[t, :, cols])
            acc = part if acc is None else acc + part
        s.y4[pl.ds(128, 256), cols] = acc
        colstats(acc, 3, col, 256)
        return 0

    lax.fori_loop(0, 2, conv_four, 0)
    ar_send(3)
    halo_down(5, s.y4.at[pl.ds(256, 128)], s.y4.at[pl.ds(0, 128)])
    halo_up(6, s.y4.at[pl.ds(128, 128)], s.y4.at[pl.ds(384, 128)])

    def slope_mid(i, _):
        zv = s.ym[pl.ds(al(128 + i * 16, 16), 16), :] * s.bnm[0:1, :] + s.bnm[1:2, :]
        s.dm[rows16(i), :] = mish_slope(zv)
        return 0

    tiles(16, slope_mid)

    def window_t(tap, dst, k):
        base = pl.ds(al((tap % 3) * 512 + (tap // 3) * 128, 128), 256)
        for q in range(4):
            dst[k, pl.ds(q * 128, 128), mycols] = s.X[base, q * 128 : q * 128 + 128].T

    def xpose_mid(k, _):
        window_t(1 + 4 * c + k, s.MT, k)
        window_t(5 - 4 * c + k, s.st2, k)
        return 0

    lax.fori_loop(0, 4, xpose_mid, 0)
    window_t(0 * c, s.J2X, 1 + 2 * c)
    cp_mt = to_sib(s.st2.at[:, :, mycols], s.MT.at[:, :, mycols])
    cp_mt.start()
    cp_m0 = to_sib(s.J2X.at[1, :, mycols], s.J2X.at[3, :, mycols])

    @pl.when(c == 0)
    def _():
        cp_m0.start()

    loads["bc0"].wait()
    loads["bc1"].wait()
    halo_down_wait(1, s.bc.at[0])
    halo_up_wait(2, s.bc.at[3])

    res = ar_recv(3)
    norm_params(4, res, 2560, s.bn4, 512)

    def norm_four(i, carry):
        t1, t2 = carry
        v = valid_at(i)
        rows = pl.ds(al(128 + i * 16, 16), 16)
        yv = s.y4[rows, :]
        zv = yv * s.bn4[0:1, :] + s.bn4[1:2, :]
        e, d, t = mish_parts(zv)
        s.bo[i // 8, i % 8] = ((zv * t + s.actr[rows16(i), :]) * v).astype(BF)
        gz = (t + 4.0 * zv * (e * (1.0 + e)) * (d * d)) * (s.bc[1 + i // 8, i % 8].astype(F32) * v)
        s.g4[rows, :] = gz
        gx = gz * (yv * s.bn4[2:3, :] + s.bn4[3:4, :])
        return t1 + gz, t2 + gx

    t1, t2 = tiles(16, norm_four, (zero16, zero16), unroll=1)
    st[4][0:1, 0:512] = jnp.sum(t1, axis=0, keepdims=True)
    st[4][1:2, 0:512] = jnp.sum(t2, axis=0, keepdims=True)
    ar_send(4)
    for i in range(2):
        store(s.bo.at[i], bo_ref.at[:, i])

    halo_down_wait(5, s.y4.at[pl.ds(0, 128)])
    halo_up_wait(6, s.y4.at[pl.ds(384, 128)])

    def halo_four(k, _):
        i = k + 16 * (k // 8)
        v = valid_at(i)
        zv = s.y4[rows16(i), :] * s.bn4[0:1, :] + s.bn4[1:2, :]
        s.g4[rows16(i), :] = mish_slope(zv) * (s.bc[i // 8, i % 8].astype(F32) * v)
        return 0

    tiles(16, halo_four)

    def back_params(res, lo, bn, width):
        inv_t = s.tot[0:1, 0:width]
        bg_ref[0:1, pl.ds(lo, width)] = res[0:1]
        gg_ref[0:1, pl.ds(lo, width)] = res[1:2]
        bn[4:5, :] = res[0:1] * inv_t
        bn[5:6, :] = res[1:2] * inv_t

    def grad_of(gz, yv, bn, v):
        xh = yv * bn[2:3, :] + bn[3:4, :]
        return bn[0:1, :] * (gz - v * (bn[4:5, :] + xh * bn[5:6, :]))

    res = ar_recv(4)
    back_params(res[:, 0:512], 2560, s.bn4, 512)
    back_params(res[:, 512:1024], 1024, s.bnl, 512)

    def grad_four(i, _):
        v = valid_at(i) * edge_at(i)
        windows(i, grad_of(s.g4[rows16(i), :], s.y4[rows16(i), :], s.bn4, v).astype(BF).astype(F32))
        return 0

    tiles(32, grad_four)

    def back_four(h, _):
        col = al(h * 256, 256)
        acc = None
        for t in range(9):
            part = mm_nt(
                s.X[pl.ds((2 - t % 3) * 512 + (2 - t // 3) * 128, 256), :], s.ws[t, pl.ds(col, 256), :]
            )
            acc = part if acc is None else acc + part
        cols = pl.ds(col, 256)
        gz = s.dm[:, cols] * acc
        s.dm[:, cols] = gz
        xh = s.ym[pl.ds(128, 256), cols] * s.bnm[2:3, cols] + s.bnm[3:4, cols]
        st[5][0:1, cols] = jnp.sum(gz, axis=0, keepdims=True)
        st[5][1:2, cols] = jnp.sum(gz * xh, axis=0, keepdims=True)
        return 0

    lax.fori_loop(0, 2, back_four, 0)
    ar_send(5)

    def grad_left(i, _):
        val = grad_of(s.gl[rows16(i), :], s.yl[rows16(i), :], s.bnl, valid_at(i)).astype(BF)
        s.glb[rows16(i), :] = val
        s.GA[pl.ds(al(c * 256 + i * 16, 16), 16), :] = val
        return 0

    tiles(16, grad_left)
    myrows = pl.ds(al(c * 256, 256), 256)
    s.G4[myrows, :] = s.X[640:896, :]
    cp_g4 = to_sib(s.G4.at[myrows], s.G4.at[myrows])
    cp_g4.start()
    cp_ga = to_sib(s.glb, s.GA.at[myrows])

    @pl.when(c == 1)
    def _():
        cp_ga.start()

    def both_waits(cp, sender):
        pl.when(c == sender)(cp.wait_send)
        pl.when(c != sender)(cp.wait_recv)

    cp_act.wait()
    both_waits(cp_low, 0)
    cp_mt.wait()
    both_waits(cp_m0, 0)
    cp_g4.wait()

    def plane_send(job, stage, k, slots):
        rel = (k - b + 4) % 4

        @pl.when(rel > 0)
        def _():
            remote(
                stage.at[k], slots.at[rel - 1], s.ps.at[job, k], s.pr.at[job, rel - 1], (r, k)
            ).start()

    def piece(lhs, k, rhs, stage):
        def body(i, _):
            rows = pl.ds(al((i // 2) * 256, 256), 256)
            cols = pl.ds(al((i % 2) * 256, 256), 256)
            stage[k, rows, cols] = mm(lhs[k, rows, :], rhs[:, cols]).astype(BF)
            return 0

        lax.fori_loop(0, 4, body, 0)

    for dc in range(2):
        for db in range(4):
            x_wait = lambda cp, me=(dc == 0 and db == 0): cp.wait() if me else cp.wait_send()
            x_send(dc, db, x_wait)
    st3 = s.xst
    for k in range(4):
        piece(s.MT, k, s.G4, st3)
        plane_send(0, st3, k, s.pr3)

    both_waits(cp_ga, 1)

    @pl.when(c == 0)
    def _():
        for k in (2, 3):
            piece(s.J2X, k, s.GA, s.st2)
            plane_send(1, s.st2, k, s.pr2)

    @pl.when(c == 1)
    def _():
        piece(s.J2X, 3, s.G4, s.st2)
        plane_send(1, s.st2, 3, s.pr2)

    res = ar_recv(5)
    back_params(res, 2048, s.bnm, 512)

    def grad_mid(i, _):
        val = grad_of(
            s.dm[rows16(i), :], s.ym[pl.ds(al(128 + i * 16, 16), 16), :], s.bnm, valid_at(i)
        ).astype(BF)
        s.gm[rows16(i), :] = val
        s.GB[pl.ds(al(c * 256 + i * 16, 16), 16), :] = val
        return 0

    tiles(16, grad_mid)

    def back_mid(h, _):
        col = al(h * 256, 256)
        cols = pl.ds(col, 256)
        acc = mm_nt(s.gm[...], s.wm[cols, :]).reshape(2, 8, 16, 256)
        t1 = jnp.zeros((16, 256), F32)
        t2 = jnp.zeros((16, 256), F32)
        for rr in range(2):
            for n in range(8):
                rows = pl.ds(rr * 128 + n * 16, 16)
                cot = s.sc[rr, n, :, pl.ds(al(512 + h * 256, 256), 256)].astype(F32) + s.bc[
                    1 + rr, n, :, cols
                ].astype(F32)
                gz = s.dr[rows, cols] * (acc[rr, n] + cot * vs[n])
                s.dr[rows, cols] = gz
                t1 = t1 + gz
                t2 = t2 + gz * (s.yr[rows, cols] * s.bnr[2:3, cols] + s.bnr[3:4, cols])
        st[6][0:1, cols] = jnp.sum(t1, axis=0, keepdims=True)
        st[6][1:2, cols] = jnp.sum(t2, axis=0, keepdims=True)
        return 0

    lax.fori_loop(0, 2, back_mid, 0)
    ar_send(6)

    cp_gb = to_sib(s.gm, s.GB.at[myrows])

    @pl.when(c == 0)
    def _():
        cp_gb.start()

    both_waits(cp_gb, 0)

    @pl.when(c == 1)
    def _():
        piece(s.J2X, 2, s.GB, s.st2)
        plane_send(1, s.st2, 2, s.pr2)

    res = ar_recv(6)
    back_params(res, 1536, s.bnr, 512)

    def grad_right(i, _):
        val = grad_of(s.dr[rows16(i), :], s.yr[rows16(i), :], s.bnr, valid_at(i)).astype(BF)
        s.gr[rows16(i), :] = val

        return 0

    tiles(16, grad_right)

    def back_one(h, _):
        cols = pl.ds(al(h * 256, 256), 256)
        acc = mm_nt(s.glb[...], s.wl[cols, :]) + mm_nt(s.gr[...], s.wr[cols, :])
        gz = s.d1[:, cols] * acc
        s.d1[:, cols] = gz
        xh = s.y1[:, cols] * s.bn0[2:3, cols] + s.bn0[3:4, cols]
        st[7][0:1, cols] = jnp.sum(gz, axis=0, keepdims=True)
        st[7][1:2, cols] = jnp.sum(gz * xh, axis=0, keepdims=True)
        return 0

    lax.fori_loop(0, 4, back_one, 0)
    ar_send(7)

    @pl.when(c == 1)
    def _():
        s.GA[myrows, :] = s.gr[...]

    cp_gr = to_sib(s.gr, s.GA.at[myrows])

    @pl.when(c == 0)
    def _():
        cp_gr.start()

    both_waits(cp_gr, 0)

    @pl.when(c == 1)
    def _():
        for k in (0, 1):
            piece(s.J2X, k, s.GA, s.st2)
            plane_send(1, s.st2, k, s.pr2)

    res = ar_recv(7)
    back_params(res, 0, s.bn0, 1024)

    def grad_one(i, _):
        val = grad_of(s.d1[rows16(i), :], s.y1[rows16(i), :], s.bn0, valid_at(i))
        low = val.astype(BF)
        s.G0[rows16(i), :] = low
        s.Gall[pl.ds(al(own8 * 256 + i * 16, 16), 16), :] = low
        return 0

    tiles(16, grad_one)

    halo_up(7, s.G0.at[pl.ds(0, 128)], s.G0.at[pl.ds(256, 128)])

    def g_block(core, batch, q):
        return s.Gall.at[pl.ds(al((core * 4 + batch) * 256, 256), 256), pl.ds(q * 256, 256)]

    def g_direct(q, j):
        return remote(
            g_block(c, b, q), g_block(c, b, q), s.gs.at[q, j - 1], s.grs.at[q, j - 1], (r, (b + j) % 4)
        )

    def g_forward(q, j):
        blk = g_block(c, (b - j + 4) % 4, q)
        return remote(blk, blk, s.gfs.at[q, j], s.gfr.at[q, j], sib)

    for q in range(4):
        for j in (1, 2, 3):
            g_direct(q, j).start()
    for q in range(4):
        g_forward(q, 0).start()

    for dc in range(2):
        for db in range(4):
            if dc or db:
                idx = dc * 4 + db
                src8 = ((c + dc) % 2) * 4 + (b - db + 4) % 4
                for k in range(3):
                    dst = s.XG.at[k, :, pl.ds(al(src8 * 256, 256), 256)]
                    if k < 2:
                        recv_wait(dst, s.xr.at[k, idx])
                    else:

                        @pl.when(jnp.logical_and(c == 0, y == 0))
                        def _():
                            recv_wait(dst, s.xr.at[k, idx])

    def chain(zp, q, own, down_job):
        up_to = (r + 2, b)
        down_to = (r - 2, b)
        own()

        if zp > 0:

            @pl.when(jnp.logical_and(z > 0, z <= zp))
            def _():
                slot = s.zb.at[zp - 1, q]
                recv_wait(slot, s.zur.at[zp, q])
                s.tile[...] = s.tile[...] + slot[...].astype(F32)

        if zp < 3:

            @pl.when(jnp.logical_and(z < 3, z >= zp))
            def _():
                slot = s.za.at[zp, q]
                recv_wait(slot, s.zdr.at[zp, q])
                s.tile[...] = s.tile[...] + slot[...].astype(F32)

        if zp > 0:

            @pl.when(z < zp)
            def _():
                s.zs[zp, q] = s.tile[...].astype(BF)
                remote(s.zs.at[zp, q], s.zb.at[zp - 1, q], s.zus.at[zp, q], s.zur.at[zp, q], up_to).start()

        if zp < 3:

            @pl.when(z > zp)
            def _():
                s.zs[zp, q] = s.tile[...].astype(BF)
                remote(s.zs.at[zp, q], s.za.at[zp, q], s.zds.at[zp, q], s.zdr.at[zp, q], down_to).start()

        def final_down():
            for h in range(2):
                s.wgo[pl.ds(2 * q + h, 256, stride=8), :] = s.tile[:, h * 128 : h * 128 + 128]

        def final_tile():
            mi, ni = q // 2, q % 2
            for h in range(2):
                s.wgo[pl.ds(mi * 1024 + ni * 2 + h, 256, stride=4), :] = s.tile[:, h * 128 : h * 128 + 128]

        @pl.when(z == zp)
        def _():
            if down_job is True:
                final_down()
            elif down_job is False:
                final_tile()
            else:
                pl.when(down_job)(final_down)
                pl.when(jnp.logical_not(down_job))(final_tile)

    def chain_drain(zp, q):
        if zp > 0:

            @pl.when(z < zp)
            def _():
                pltpu.make_async_copy(s.zs.at[zp, q], s.zs.at[zp, q], s.zus.at[zp, q]).wait()

        if zp < 3:

            @pl.when(z > zp)
            def _():
                pltpu.make_async_copy(s.zs.at[zp, q], s.zs.at[zp, q], s.zds.at[zp, q]).wait()

    def own_plane(stage, slots, q):
        rows = pl.ds((q // 2) * 256, 256)
        cols = pl.ds((q % 2) * 256, 256)

        def go():
            v = stage[b, rows, cols].astype(F32)
            for j in range(3):
                v = v + slots[j, rows, cols].astype(F32)
            s.tile[...] = v

        return go

    def own_down(k, q):
        def go():
            s.tile[...] = mm(s.XG[k], s.Gall[:, pl.ds(q * 256, 256)])

        return go

    for j in range(3):
        recv_wait(s.pr3.at[j], s.pr.at[0, j])
    for q in range(4):
        chain(3, q, own_plane(st3, s.pr3, q), False)

    is_tap8 = jnp.logical_and(c == 0, y == 0)
    has_plane2 = jnp.logical_not(is_tap8)

    @pl.when(has_plane2)
    def _():
        for j in range(3):
            recv_wait(s.pr2.at[j], s.pr.at[1, j])

    for q in range(4):
        for j in (1, 2, 3):
            recv_wait(g_block(c, (b - j + 4) % 4, q), s.grs.at[q, j - 1])
            g_forward(q, j).start()
        for j in range(4):
            recv_wait(g_block(1 - c, (b - j + 4) % 4, q), s.gfr.at[q, j])
        chain(0, q, own_down(0, q), True)
        chain(1, q, own_down(1, q), True)

        def own_two():
            pl.when(is_tap8)(own_down(2, q))
            pl.when(has_plane2)(own_plane(s.st2, s.pr2, q))

        chain(2, q, own_two, is_tap8)

    store(s.wgo, wg_ref)

    halo_up_wait(7, s.G0.at[pl.ds(256, 128)])

    def shift_one(i, _):
        n = i % 8
        for h in range(2):
            cols = pl.ds(h * 512, 512)
            s.pad[n, 8:24, :] = s.G0[rows16(i), cols].astype(F32)
            s.Gp[rows16(i), cols] = s.pad[n, 9:25, :].astype(BF)
        return 0

    lax.fori_loop(0, 24, shift_one, 0)

    def back_conv(h, _):
        ch = pl.ds(al(h * 256, 256), 256)

        def part(src, row, tap):
            return mm_nt(src[pl.ds(row * 128, 256), :], s.wd[tap, ch, :])

        for par in range(2):
            if par == 0:
                even = part(s.G0, 0, 4)
                odd = part(s.G0, 0, 5) + part(s.Gp, 0, 3)
            else:
                even = part(s.G0, 0, 7) + part(s.G0, 1, 1)
                odd = (part(s.G0, 0, 8) + part(s.Gp, 0, 6)) + (part(s.G0, 1, 2) + part(s.Gp, 1, 0))
            for q in range(2):
                s.igf[q, pl.ds(0, 256, stride=2), :] = even[:, q * 128 : q * 128 + 128]
                s.igf[q, pl.ds(1, 256, stride=2), :] = odd[:, q * 128 : q * 128 + 128]
            for rr in range(2):
                for q in range(2):
                    s.inraw[2 * rr + par, :, :, pl.ds(al(h * 256 + q * 128, 128), 128)] = (
                        s.igf[q, rr * 256 : rr * 256 + 256, :].astype(BF).reshape(8, 32, 128)
                    )
        return 0

    lax.fori_loop(0, 2, back_conv, 0)
    for i in range(4):
        store(s.inraw.at[i], ig_ref.at[:, i])

    for q in range(4):
        for zp in range(4):
            chain_drain(zp, q)
        for j in (1, 2, 3):
            g_direct(q, j).wait_send()
        for j in range(4):
            g_forward(q, j).wait_send()
    for k in range(4):

        @pl.when(k != b)
        def _():
            pltpu.make_async_copy(st3.at[k], st3.at[k], s.ps.at[0, k]).wait()

            @pl.when(jnp.logical_or(c == 1, k >= 2))
            def _():
                pltpu.make_async_copy(s.st2.at[k], s.st2.at[k], s.ps.at[1, k]).wait()

    for cp in outs:
        cp.wait()


def fused_step(
    inputs, counts, down_weight, left_weight, right_weight, reduce_weight, spread_weight,
    norm_gains, norm_biases, running_mean, running_var, section_cotangent, block_cotangent,
):
    table = scratch_table()
    names = tuple(table)
    sds = jax.ShapeDtypeStruct
    row = (1, 3072)
    vmem = pl.BlockSpec(memory_space=pltpu.VMEM)
    smem = pl.BlockSpec(memory_space=pltpu.SMEM)
    hbm = pl.BlockSpec(memory_space=pl.ANY)
    outs = pl.pallas_call(
        functools.partial(fused_kernel, names, 13, 8),
        out_shape=(
            sds((8, 2, 16, 1024), BF),
            sds((8, 2, 16, 512), BF),
            sds((8, 4, 32, 512), BF),
            sds((2048, 128), F32),
            sds(row, F32),
            sds(row, F32),
            sds(row, F32),
            sds(row, F32),
        ),
        in_specs=[hbm, smem, hbm, hbm, hbm, hbm, hbm, vmem, vmem, vmem, vmem, hbm, hbm],
        out_specs=(hbm, hbm, hbm, hbm, vmem, vmem, vmem, vmem),
        scratch_shapes=list(table.values()),
        compiler_params=pltpu.CompilerParams(
            collective_id=0, has_side_effects=True, vmem_limit_bytes=64 * 2**20 - 2**16
        ),
        cost_estimate=pl.CostEstimate(flops=13 * 10**9, bytes_accessed=21 * 10**6, transcendentals=10**6),
    )(
        inputs, counts, down_weight.reshape((9,) + down_weight.shape[2:]), left_weight, right_weight,
        reduce_weight, spread_weight.reshape((9,) + spread_weight.shape[2:]),
        norm_gains.reshape(row), norm_biases.reshape(row), running_mean.reshape(row), running_var.reshape(row),
        section_cotangent, block_cotangent,
    )
    so, bo, ig, wg, gg, bg, nm, nv = outs
    return (so, bo, ig, wg.reshape(-1), gg.reshape(-1), bg.reshape(-1), nm.reshape(-1), nv.reshape(-1))


def fits_fused(mesh):
    return dict(mesh.shape) == {"rows": 8, "batch": 4}


def solution(mesh):
    placed = (
        P("batch", "rows", None, None),
        P("batch"),
        P(),
        P(),
        P(),
        P(),
        P(),
        P(),
        P(),
        P(),
        P(),
        P("batch", "rows", None, None),
        P("batch", "rows", None, None),
    )
    return jax.shard_map(
        fused_step if fits_fused(mesh) else on_device,
        mesh=mesh,
        in_specs=placed,
        out_specs=(
            P("batch", "rows", None, None),
            P("batch", "rows", None, None),
            P("batch", "rows", None, None),
            P(("rows", "batch")),
            P(),
            P(),
            P(),
            P(),
        ),
        check_vma=False,
    )
```

```python
import functools
import types

import jax
import jax.numpy as jnp
from jax import lax
from jax.experimental import pallas as pl
from jax.experimental.pallas import tpu as pltpu
from jax.sharding import PartitionSpec as P

EPS = 1e-05
MOMENTUM = 0.1


def passed_along(block, axis, distance):
    devices = range(lax.axis_size(axis))
    route = [(i - distance, i) for i in devices if i - distance in devices]
    return lax.ppermute(block, axis, route)


def padded_2(block, sides, width):
    for axis, dim in sides:
        count = lax.axis_size(axis)
        forward = [(i, i + 1) for i in range(count - 1)]
        backward = [(target, source) for source, target in forward]
        low = lax.ppermute(
            lax.slice_in_dim(block, block.shape[dim] - width, None, axis=dim), axis, forward
        )
        high = lax.ppermute(lax.slice_in_dim(block, 0, width, axis=dim), axis, backward)
        block = jnp.concatenate([low, block, high], axis=dim)
    return block


def mish_act(values):
    return values * jnp.tanh(jax.nn.softplus(values))


def mish_back(before, grad_out):
    return jax.vjp(mish_act, before)[1](grad_out)[0]


def point_dot(left_op, right_op):
    return jnp.einsum("nhwc,cd->nhwd", left_op, right_op, preferred_element_type=jnp.float32)


def back_dot(left_op, right_op):
    return jnp.einsum("nhwd,cd->nhwc", left_op, right_op, preferred_element_type=jnp.float32)


def outer_dot(left_op, right_op):
    return jnp.einsum("nhwc,nhwd->cd", left_op, right_op, preferred_element_type=jnp.float32)


def norm_forward(values, valid_mask, gain_vec, offset, local_pixels):
    sum_first = jnp.sum(values * valid_mask, axis=(0, 1, 2))
    sum_second = jnp.sum(values * values * valid_mask, axis=(0, 1, 2))
    sum_first, sum_second, pixel_total = lax.psum(
        (sum_first, sum_second, local_pixels), ("rows", "batch")
    )
    batch_mean = sum_first / pixel_total
    batch_var = sum_second / pixel_total - batch_mean * batch_mean
    inv_std = lax.rsqrt(batch_var + EPS)
    normed = (values - batch_mean) * inv_std
    return (normed * gain_vec + offset, normed, inv_std, batch_mean, batch_var, pixel_total)


def norm_back(grad_out, normed, inv_std, gain_vec, valid_mask, pixel_total):
    bias_grad, gain_grad = lax.psum(
        (jnp.sum(grad_out, axis=(0, 1, 2)), jnp.sum(grad_out * normed, axis=(0, 1, 2))),
        ("rows", "batch"),
    )
    grad_in = (
        gain_vec
        * inv_std
        * (grad_out - valid_mask * (bias_grad + normed * gain_grad) / pixel_total)
    )
    return (grad_in, gain_grad, bias_grad)


def on_device(
    inputs,
    counts,
    down_weight,
    left_weight,
    right_weight,
    reduce_weight,
    spread_weight,
    norm_gains,
    norm_biases,
    running_mean,
    running_var,
    section_cotangent,
    block_cotangent,
):
    n_slots, row_in, col_in, in_width = inputs.shape
    row_out = row_in // 2
    col_out = col_in // 2
    section_width = down_weight.shape[3]
    branch_width = right_weight.shape[1]
    bounds = [
        0,
        section_width,
        section_width + branch_width,
        section_width + 2 * branch_width,
        section_width + 3 * branch_width,
        section_width + 4 * branch_width,
    ]
    valid_mask = (
        (jnp.arange(n_slots, dtype=jnp.int32) < counts[0])
        .astype(jnp.float32)
        .reshape(n_slots, 1, 1, 1)
    )
    local_pixels = jnp.sum(valid_mask) * float(row_out * col_out)

    def gain_at(bn_index):
        return norm_gains[bounds[bn_index] : bounds[bn_index + 1]]

    def norm_at(values, bn_index):
        return norm_forward(
            values,
            valid_mask,
            gain_at(bn_index),
            norm_biases[bounds[bn_index] : bounds[bn_index + 1]],
            local_pixels,
        )

    rim_row = passed_along(inputs[:, row_in - 1 :], "rows", 1)
    padded = jnp.pad(jnp.concatenate([rim_row, inputs], axis=1), ((0, 0), (0, 0), (1, 1), (0, 0)))
    taps = []
    first_out = jnp.zeros((n_slots, row_out, col_out, section_width), jnp.float32)
    for row_tap in range(3):
        for col_tap in range(3):
            window = padded[
                :, row_tap : row_tap + 2 * row_out : 2, col_tap : col_tap + 2 * col_out : 2, :
            ]
            taps.append(window)
            first_out = first_out + point_dot(window, down_weight[row_tap, col_tap])
    z_one, normed_one, inv_one, mean_one, var_one, pixel_total = norm_at(first_out, 0)
    act_one = mish_act(z_one).astype(jnp.bfloat16)
    z_left, normed_left, inv_left, mean_left, var_left, pixel_total = norm_at(
        point_dot(act_one, left_weight), 1
    )
    act_left = mish_act(z_left)
    z_right, normed_right, inv_right, mean_right, var_right, pixel_total = norm_at(
        point_dot(act_one, right_weight), 2
    )
    act_right = mish_act(z_right)
    right_low = act_right.astype(jnp.bfloat16)
    z_mid, normed_mid, inv_mid, mean_mid, var_mid, pixel_total = norm_at(
        point_dot(right_low, reduce_weight), 3
    )
    act_mid = mish_act(z_mid).astype(jnp.bfloat16)
    mid_halo = padded_2(act_mid, (("rows", 1),), 1)
    mid_pad = jnp.pad(mid_halo, ((0, 0), (0, 0), (1, 1), (0, 0)))
    fourth_out = jnp.zeros((n_slots, row_out, col_out, branch_width), jnp.float32)
    for row_tap in range(3):
        for col_tap in range(3):
            fourth_out = fourth_out + point_dot(
                mid_pad[:, row_tap : row_tap + row_out, col_tap : col_tap + col_out, :],
                spread_weight[row_tap, col_tap],
            )
    z_four, normed_four, inv_four, mean_four, var_four, pixel_total = norm_at(fourth_out, 4)
    act_four = mish_act(z_four)
    section_out = (valid_mask * jnp.concatenate([act_left, act_right], axis=3)).astype(jnp.bfloat16)
    block_out = (valid_mask * (act_right + act_four)).astype(jnp.bfloat16)
    section_grad = valid_mask * section_cotangent.astype(jnp.float32)
    block_grad = valid_mask * block_cotangent.astype(jnp.float32)
    grad_four, gain_four, bias_four = norm_back(
        mish_back(z_four, block_grad), normed_four, inv_four, gain_at(4), valid_mask, pixel_total
    )
    grad_four = grad_four.astype(jnp.bfloat16)
    grad_halo = padded_2(grad_four, (("rows", 1),), 1)
    grad_pad = jnp.pad(grad_halo, ((0, 0), (0, 0), (1, 1), (0, 0)))
    spread_taps = []
    mid_grad = jnp.zeros((n_slots, row_out, col_out, branch_width), jnp.float32)
    for row_tap in range(3):
        for col_tap in range(3):
            spread_taps.append(
                outer_dot(
                    mid_pad[:, row_tap : row_tap + row_out, col_tap : col_tap + col_out, :],
                    grad_four,
                )
            )
            mid_grad = mid_grad + back_dot(
                grad_pad[
                    :, 2 - row_tap : 2 - row_tap + row_out, 2 - col_tap : 2 - col_tap + col_out, :
                ],
                spread_weight[row_tap, col_tap],
            )
    spread_grad = jnp.stack(spread_taps).reshape(spread_weight.shape)
    grad_mid, gain_mid, bias_mid = norm_back(
        mish_back(z_mid, mid_grad), normed_mid, inv_mid, gain_at(3), valid_mask, pixel_total
    )
    grad_mid = grad_mid.astype(jnp.bfloat16)
    reduce_grad = outer_dot(right_low, grad_mid)
    right_total = section_grad[..., branch_width:] + block_grad + back_dot(grad_mid, reduce_weight)
    grad_right, gain_right, bias_right = norm_back(
        mish_back(z_right, right_total),
        normed_right,
        inv_right,
        gain_at(2),
        valid_mask,
        pixel_total,
    )
    grad_right = grad_right.astype(jnp.bfloat16)
    grad_left, gain_left, bias_left = norm_back(
        mish_back(z_left, section_grad[..., :branch_width]),
        normed_left,
        inv_left,
        gain_at(1),
        valid_mask,
        pixel_total,
    )
    grad_left = grad_left.astype(jnp.bfloat16)
    left_grad = outer_dot(act_one, grad_left)
    right_grad = outer_dot(act_one, grad_right)
    one_total = back_dot(grad_left, left_weight) + back_dot(grad_right, right_weight)
    grad_one, gain_one, bias_one = norm_back(
        mish_back(z_one, one_total), normed_one, inv_one, gain_at(0), valid_mask, pixel_total
    )
    grad_one = grad_one.astype(jnp.bfloat16)
    down_taps = []
    spread_back = jnp.zeros(padded.shape, jnp.float32)
    for row_tap in range(3):
        for col_tap in range(3):
            down_taps.append(outer_dot(taps[row_tap * 3 + col_tap], grad_one))
            spread_back = spread_back.at[
                :, row_tap : row_tap + 2 * row_out : 2, col_tap : col_tap + 2 * col_out : 2, :
            ].add(back_dot(grad_one, down_weight[row_tap, col_tap]))
    down_grad = jnp.stack(down_taps).reshape(down_weight.shape)
    back_rim = passed_along(
        spread_back[:, 0:1, 1 : col_in + 1].astype(jnp.bfloat16), "rows", -1
    ).astype(jnp.float32)
    input_grad = spread_back[:, 1:, 1 : col_in + 1]
    input_grad = input_grad.at[:, row_in - 1 :].add(back_rim)
    flat_grads = jnp.concatenate(
        [
            down_grad.reshape(-1),
            left_grad.reshape(-1),
            right_grad.reshape(-1),
            reduce_grad.reshape(-1),
            spread_grad.reshape(-1),
        ]
    )
    row_share = lax.psum_scatter(
        flat_grads.astype(jnp.bfloat16), "rows", scatter_dimension=0, tiled=True
    )
    weight_share = lax.psum_scatter(row_share, "batch", scatter_dimension=0, tiled=True).astype(
        jnp.float32
    )
    gain_grads = jnp.concatenate([gain_one, gain_left, gain_right, gain_mid, gain_four])
    bias_grads = jnp.concatenate([bias_one, bias_left, bias_right, bias_mid, bias_four])
    means_all = jnp.concatenate([mean_one, mean_left, mean_right, mean_mid, mean_four])
    vars_all = jnp.concatenate([var_one, var_left, var_right, var_mid, var_four])
    new_mean = (1.0 - MOMENTUM) * running_mean + MOMENTUM * means_all
    new_var = (1.0 - MOMENTUM) * running_var + MOMENTUM * vars_all * (
        pixel_total / (pixel_total - 1.0)
    )
    return (
        section_out,
        block_out,
        input_grad.astype(jnp.bfloat16),
        weight_share,
        gain_grads,
        bias_grads,
        new_mean,
        new_var,
    )


MESHID = pl.DeviceIdType.MESH
BF = jnp.bfloat16
F32 = jnp.float32
NT = (((1,), (1,)), ((), ()))


def mm(lhs, rhs):
    return jnp.dot(lhs, rhs, preferred_element_type=F32)


def mm_nt(lhs, rhs):
    return lax.dot_general(lhs, rhs, NT, preferred_element_type=F32)


def mish_parts(z):
    e = jnp.exp(jnp.minimum(z, 20.0))
    n = e * (e + 2.0)
    d = 1.0 / (n + 2.0)
    return e, d, n * d


def mish_of(z):
    return z * mish_parts(z)[2]


def mish_slope(z):
    e, d, t = mish_parts(z)
    return t + 4.0 * z * (e * (1.0 + e)) * (d * d)


def al(i, m):
    return pl.multiple_of(i, m)


def scratch_table():
    v = pltpu.VMEM
    dma = pltpu.SemaphoreType.DMA
    table = dict(
        inraw=v((5, 8, 32, 512), BF),
        tmpc=v((8, 4, 40, 128), F32),
        pad=v((8, 32, 512), F32),
        X=v((2304, 512), BF),
        xst=v((5, 512, 512), BF),
        XG=v((3, 256, 2048), BF),
        wd=v((9, 512, 1024), BF),
        wl=v((1024, 512), BF),
        wr=v((1024, 512), BF),
        wm=v((512, 512), BF),
        ws=v((9, 512, 512), BF),
        sc=v((2, 8, 16, 1024), BF),
        bc=v((4, 8, 16, 512), BF),
        so=v((2, 8, 16, 1024), BF),
        bo=v((2, 8, 16, 512), BF),
        y1=v((256, 1024), F32),
        d1=v((256, 1024), F32),
        act1=v((256, 1024), BF),
        yl=v((256, 512), F32),
        yr=v((256, 512), F32),
        gl=v((256, 512), F32),
        dr=v((256, 512), F32),
        actr=v((256, 512), F32),
        rlow=v((256, 512), BF),
        ym=v((512, 512), F32),
        dm=v((256, 512), F32),
        y4=v((512, 512), F32),
        g4=v((512, 512), F32),
        gm=v((256, 512), BF),
        gr=v((256, 512), BF),
        glb=v((256, 512), BF),
        GA=v((512, 512), BF),
        GB=v((512, 512), BF),
        G4=v((512, 512), BF),
        J2X=v((4, 512, 512), BF),
        MT=v((4, 512, 512), BF),
        st2=v((4, 512, 512), BF),
        pr2=v((3, 512, 512), BF),
        pr3=v((3, 512, 512), BF),
        Gall=v((2048, 1024), BF),
        G0=v((384, 1024), BF),
        Gp=v((256 + 128, 1024), BF),
        igf=v((2, 512, 128), F32),
        zb=v((3, 4, 256, 256), BF),
        za=v((3, 4, 256, 256), BF),
        zs=v((4, 4, 256, 256), BF),
        tile=v((256, 256), F32),
        wgo=v((2048, 128), F32),
        bn0=v((8, 1024), F32),
        bnl=v((8, 512), F32),
        bnr=v((8, 512), F32),
        bnm=v((8, 512), F32),
        bn4=v((8, 512), F32),
        tot=v((1, 1024), F32),
        ld=dma((32,)),
        ldo=dma((16,)),
        hs=dma((12,)),
        hr=dma((12,)),
        cs=dma((8,)),
        cr=dma((8,)),
        as_=dma((8,)),
        ar_=dma((8,)),
        xs=dma((3, 8)),
        xr=dma((3, 8)),
        bs=dma((12,)),
        br=dma((12,)),
        ps=dma((2, 3, 2)),
        pr=dma((2, 3, 2)),
        gs=dma((4, 3)),
        grs=dma((4, 3)),
        gfs=dma((4, 4)),
        gfr=dma((4, 4)),
        zus=dma((4, 4)),
        zur=dma((4, 4)),
        zds=dma((4, 4)),
        zdr=dma((4, 4)),
    )
    widths = AR_WIDTHS
    for k, w in enumerate(widths):
        table["ar_st%d" % k] = v((2, w), F32)
        table["ar_ct%d" % k] = v((2, w), F32)
        table["ar_ab%d" % k] = v((16, 2, w), F32)
    return table


AR_WIDTHS = (1152, 1024, 512, 512, 1024, 512, 512, 1024)


def fused_kernel(names, n_in, n_out, *refs):
    (in_ref, cnt_ref, wd_ref, wl_ref, wr_ref, wm_ref, ws_ref, gain_ref, bias_ref, rm_ref, rv_ref,
     sc_ref, bc_ref) = refs[:n_in]
    (so_ref, bo_ref, ig_ref, wg_ref, gg_ref, bg_ref, nm_ref, nv_ref) = refs[n_in : n_in + n_out]
    s = types.SimpleNamespace(**dict(zip(names, refs[n_in + n_out :])))
    st = [getattr(s, "ar_st%d" % k) for k in range(8)]
    ct = [getattr(s, "ar_ct%d" % k) for k in range(8)]
    ab = [getattr(s, "ar_ab%d" % k) for k in range(8)]

    r = lax.axis_index("rows")
    b = lax.axis_index("batch")
    z = r // 2
    c = r % 2
    y = b // 2
    x = b % 2
    chip = z * 4 + b
    sib = (r + 1 - 2 * c, b)
    own8 = c * 4 + b
    first = r == 0
    last = r == 7
    plane = [b, b + 1 - 2 * x, b + 2 - 4 * y, 3 - b]

    def remote(src, dst, ss, rs, dev):
        return pltpu.make_async_remote_copy(
            src_ref=src, dst_ref=dst, send_sem=ss, recv_sem=rs, device_id=dev, device_id_type=MESHID
        )

    def recv_wait(dst, rs):
        pltpu.make_async_copy(dst, dst, rs).wait()

    bar = pltpu.get_barrier_semaphore()
    for i in range(8):
        for j in range(4):
            if i or j:
                pl.semaphore_signal(
                    bar, inc=1, device_id=((r + i) % 8, (b + j) % 4), device_id_type=MESHID
                )

    loads = {}

    def load(name, src, dst):
        cp = pltpu.make_async_copy(src, dst, s.ld.at[len(loads)])
        cp.start()
        loads[name] = cp

    for i in range(4):
        load("in%d" % i, in_ref.at[:, i], s.inraw.at[1 + i])
    for t in (3, 4, 5, 6, 7, 8, 0, 1, 2):
        load("wd%d" % t, wd_ref.at[t], s.wd.at[t])
    load("wl", wl_ref, s.wl)
    load("wr", wr_ref, s.wr)
    load("wm", wm_ref, s.wm)
    for i in range(2):
        load("sc%d" % i, sc_ref.at[:, i], s.sc.at[i])
        load("bc%d" % i, bc_ref.at[:, i], s.bc.at[1 + i])
    for i in range(3):
        load("ws%d" % i, ws_ref.at[pl.ds(3 * i, 3)], s.ws.at[pl.ds(3 * i, 3)])

    for n in range(8):
        for q in range(4):
            s.tmpc[n, q, 0:8, :] = jnp.zeros((8, 128), F32)
        s.pad[n, 0:8, :] = jnp.zeros((8, 512), F32)
        s.pad[n, 24:32, :] = jnp.zeros((8, 512), F32)

    @pl.when(first)
    def _():
        s.inraw[0] = jnp.zeros((8, 32, 512), BF)
        s.bc[0] = jnp.zeros((8, 16, 512), BF)
        s.ym[0:128, :] = jnp.zeros((128, 512), F32)
        s.y4[0:128, :] = jnp.zeros((128, 512), F32)

    @pl.when(last)
    def _():
        s.bc[3] = jnp.zeros((8, 16, 512), BF)
        s.ym[384:512, :] = jnp.zeros((128, 512), F32)
        s.y4[384:512, :] = jnp.zeros((128, 512), F32)
        s.G0[256:384, :] = jnp.zeros((128, 1024), BF)

    pl.semaphore_wait(bar, 31)

    nxt = (r + 1, b)
    prv = (r - 1, b)

    def halo_down(k, src, dst):
        @pl.when(r < 7)
        def _():
            remote(src, dst, s.hs.at[k], s.hr.at[k], nxt).start()

    def halo_up(k, src, dst):
        @pl.when(r > 0)
        def _():
            remote(src, dst, s.hs.at[k], s.hr.at[k], prv).start()

    def halo_down_wait(k, dst):
        @pl.when(r < 7)
        def _():
            pltpu.make_async_copy(dst, dst, s.hs.at[k]).wait()

        @pl.when(r > 0)
        def _():
            recv_wait(dst, s.hr.at[k])

    def halo_up_wait(k, dst):
        @pl.when(r > 0)
        def _():
            pltpu.make_async_copy(dst, dst, s.hs.at[k]).wait()

        @pl.when(r < 7)
        def _():
            recv_wait(dst, s.hr.at[k])

    halo_down(0, in_ref.at[:, 3], s.inraw.at[0])
    halo_down(1, bc_ref.at[:, 1], s.bc.at[0])
    halo_up(2, bc_ref.at[:, 0], s.bc.at[3])

    count = cnt_ref[0]
    vs = [(jnp.int32(n) < count).astype(F32) for n in range(8)]

    def ar_send(k):
        cp = remote(st[k], ct[k], s.cs.at[k], s.cr.at[k], sib)
        cp.start()
        cp.wait()
        ab[k][chip] = st[k][...] + ct[k][...]
        for j in range(1, 16):
            dev = (((z + j // 4) % 4) * 2 + c, (b + j % 4) % 4)
            remote(ab[k].at[chip], ab[k].at[chip], s.as_.at[k], s.ar_.at[k], dev).start()

    def ar_recv(k):
        part = ab[k].at[pl.ds(0, 15)]
        pltpu.make_async_copy(part, part, s.ar_.at[k]).wait()
        pltpu.make_async_copy(part, part, s.as_.at[k]).wait()
        out = ab[k][0]
        for j in range(1, 16):
            out = out + ab[k][j]
        return out

    def colstats(acc, k, col, width):
        a = acc.reshape(2, 8, 16, width)
        t1 = jnp.zeros((16, width), F32)
        t2 = jnp.zeros((16, width), F32)
        for n in range(8):
            p = a[0, n]
            q = a[1, n]
            t1 = t1 + (p + q) * vs[n]
            t2 = t2 + (p * p + q * q) * vs[n]
        st[k][0:1, pl.ds(col, width)] = jnp.sum(t1, axis=0, keepdims=True)
        st[k][1:2, pl.ds(col, width)] = jnp.sum(t2, axis=0, keepdims=True)

    def tiles(count_, body, init=0, unroll=2):
        return lax.fori_loop(0, count_, body, init, unroll=unroll)

    def rows16(i):
        return pl.ds(al(i * 16, 16), 16)

    def deinterleave(slot):
        targets = [(i, rr) for rr in range(2) for i in range(3) if i + 2 * rr == slot]

        def body(n, _):
            for q in range(4):
                s.tmpc[n, q, 8:40, :] = s.inraw[slot, n, :, q * 128 : q * 128 + 128].astype(F32)
            for j in range(3):
                for q in range(4):
                    val = s.tmpc[n, q, pl.ds(7 + j, 16, stride=2), :].astype(BF)
                    for i, rr in targets:
                        s.X[pl.ds(al((3 * i + j) * 256 + rr * 128 + n * 16, 16), 16), q * 128 : q * 128 + 128] = val
            return 0

        lax.fori_loop(0, 8, body, 0)

    for i in range(4):
        loads["in%d" % i].wait()
        deinterleave(1 + i)
    for t in (3, 4, 5, 6, 7, 8):
        loads["wd%d" % t].wait()

    def conv_a(n, _):
        cols = pl.ds(al(n * 256, 256), 256)
        acc = mm(s.X[3 * 256 : 4 * 256, :], s.wd[3, :, cols])
        for t in range(4, 9):
            acc = acc + mm(s.X[t * 256 : t * 256 + 256, :], s.wd[t, :, cols])
        s.y1[:, cols] = acc
        return 0

    lax.fori_loop(0, 4, conv_a, 0)
    halo_down_wait(0, s.inraw.at[0])
    deinterleave(0)
    for t in (0, 1, 2):
        loads["wd%d" % t].wait()
    st[0][:, 1024:1152] = jnp.zeros((2, 128), F32) + count.astype(F32) * 32.0

    def conv_b(n, _):
        col = al(n * 256, 256)
        cols = pl.ds(col, 256)
        acc = s.y1[:, cols]
        for t in range(3):
            acc = acc + mm(s.X[t * 256 : t * 256 + 256, :], s.wd[t, :, cols])
        s.y1[:, cols] = acc
        colstats(acc, 0, col, 256)
        return 0

    lax.fori_loop(0, 4, conv_b, 0)
    ar_send(0)

    def xpose(t, _):
        for q in range(4):
            s.xst[t // 2, q * 128 : q * 128 + 128, pl.ds(al((t % 2) * 256, 256), 256)] = s.X[
                pl.ds(al(t * 256, 256), 256), q * 128 : q * 128 + 128
            ].T
        return 0

    lax.fori_loop(0, 9, xpose, 0)

    def x_copy(dc, j, k):
        cc = (c + dc) % 2
        bb = plane[j]
        yy = bb // 2
        xx = bb % 2
        half = pl.ds(al(xx * 256, 256), 256)
        mine = pl.ds(al(own8 * 256, 256), 256)
        tap = 2 * cc + yy + 4 * k if k < 2 else 8
        src = s.xst.at[tap // 2, half, pl.ds(al((tap % 2) * 256, 256), 256)]
        dst = s.XG.at[k, :, mine]
        idx = dc * 4 + j
        if dc == 0 and j == 0:
            return pltpu.make_async_copy(src, dst, s.xs.at[k, idx])
        return remote(src, dst, s.xs.at[k, idx], s.xr.at[k, idx], (z * 2 + cc, bb))

    def x_when(dc, j, k, do):
        if k < 2:
            do()
        else:
            pl.when(jnp.logical_and((c + dc) % 2 == 0, plane[j] // 2 == 0))(do)

    def x_start(js, ks):
        for k in ks:
            for dc in range(2):
                for j in js:
                    x_when(dc, j, k, lambda: x_copy(dc, j, k).start())

    x_start((1, 2), (0,))
    x_start((0,), (0, 1, 2))

    def norm_params(k, res, lo, bn, width):
        g = gain_ref[0:1, pl.ds(lo, width)]
        o = bias_ref[0:1, pl.ds(lo, width)]
        inv_t = s.tot[0:1, 0:width]
        mean = res[0:1] * inv_t
        var = res[1:2] * inv_t - mean * mean
        inv = lax.rsqrt(var + EPS)
        a = g * inv
        bn[0:1, :] = a
        bn[1:2, :] = o - mean * a
        bn[2:3, :] = inv
        bn[3:4, :] = -mean * inv
        nm_ref[0:1, pl.ds(lo, width)] = (1.0 - MOMENTUM) * rm_ref[0:1, pl.ds(lo, width)] + MOMENTUM * mean
        t = 1.0 / inv_t
        nv_ref[0:1, pl.ds(lo, width)] = (1.0 - MOMENTUM) * rv_ref[0:1, pl.ds(lo, width)] + MOMENTUM * var * (
            t / (t - 1.0)
        )

    res = ar_recv(0)
    s.tot[0:1, :] = jnp.broadcast_to(1.0 / res[0:1, 1024:1025], (1, 1024))
    norm_params(0, res[:, 0:1024], 0, s.bn0, 1024)

    def act_one(i, _):
        zv = s.y1[rows16(i), :] * s.bn0[0:1, :] + s.bn0[1:2, :]
        s.act1[rows16(i), :] = mish_of(zv).astype(BF)
        return 0

    tiles(16, act_one)
    loads["wl"].wait()
    loads["wr"].wait()

    for h in range(2):
        cols = pl.ds(h * 256, 256)
        acc = mm(s.act1[...], s.wl[:, cols])
        s.yl[:, cols] = acc
        colstats(acc, 1, h * 256, 256)
        acc = mm(s.act1[...], s.wr[:, cols])
        s.yr[:, cols] = acc
        colstats(acc, 1, 512 + h * 256, 256)
    ar_send(1)

    def slope_one(i, _):
        zv = s.y1[rows16(i), :] * s.bn0[0:1, :] + s.bn0[1:2, :]
        s.d1[rows16(i), :] = mish_slope(zv)
        return 0

    tiles(16, slope_one)
    mycols = pl.ds(al(c * 256, 256), 256)

    def xpose_act(h, _):
        for q in range(4):
            blk = s.act1[:, pl.ds(al(h * 512 + q * 128, 128), 128)]
            s.J2X[2 - 2 * c + h, pl.ds(q * 128, 128), mycols] = blk.T
        return 0

    lax.fori_loop(0, 2, xpose_act, 0)
    pair = []

    def to_sib(src, dst):
        k = len(pair)
        cp = remote(src, dst, s.bs.at[k], s.br.at[k], sib)
        pair.append(cp)
        return cp

    cp_act = to_sib(s.J2X.at[pl.ds(2 - 2 * c, 2), :, mycols], s.J2X.at[pl.ds(2 * c, 2), :, mycols])
    cp_act.start()
    x_start((1, 2), (1,))

    res = ar_recv(1)
    norm_params(1, res[:, 0:512], 1024, s.bnl, 512)
    norm_params(2, res[:, 512:1024], 1536, s.bnr, 512)

    def act_right(i, _):
        zv = s.yr[rows16(i), :] * s.bnr[0:1, :] + s.bnr[1:2, :]
        e, d, t = mish_parts(zv)
        a = zv * t
        s.actr[rows16(i), :] = a
        s.rlow[rows16(i), :] = a.astype(BF)
        s.dr[rows16(i), :] = t + 4.0 * zv * (e * (1.0 + e)) * (d * d)
        return 0

    tiles(16, act_right)
    loads["wm"].wait()
    for h in range(2):
        cols = pl.ds(h * 256, 256)
        acc = mm(s.rlow[...], s.wm[:, cols])
        s.ym[128:384, cols] = acc
        colstats(acc, 2, h * 256, 256)
    ar_send(2)
    halo_down(3, s.ym.at[pl.ds(256, 128)], s.ym.at[pl.ds(0, 128)])
    halo_up(4, s.ym.at[pl.ds(128, 128)], s.ym.at[pl.ds(384, 128)])
    x_start((3,), (0,))

    loads["sc0"].wait()
    loads["sc1"].wait()

    def valid_at(i):
        return ((i % 8) < count).astype(F32)

    def left_branch(i, carry):
        t1, t2 = carry
        v = valid_at(i)
        yv = s.yl[rows16(i), :]
        zv = yv * s.bnl[0:1, :] + s.bnl[1:2, :]
        e, d, t = mish_parts(zv)
        s.so[i // 8, i % 8, :, 0:512] = (zv * t * v).astype(BF)
        s.so[i // 8, i % 8, :, 512:1024] = (s.actr[rows16(i), :] * v).astype(BF)
        gz = (t + 4.0 * zv * (e * (1.0 + e)) * (d * d)) * (s.sc[i // 8, i % 8, :, 0:512].astype(F32) * v)
        s.gl[rows16(i), :] = gz
        gx = gz * (yv * s.bnl[2:3, :] + s.bnl[3:4, :])
        return t1 + gz, t2 + gx

    zero16 = jnp.zeros((16, 512), F32)
    t1, t2 = tiles(16, left_branch, (zero16, zero16), unroll=1)
    st[4][0:1, 512:1024] = jnp.sum(t1, axis=0, keepdims=True)
    st[4][1:2, 512:1024] = jnp.sum(t2, axis=0, keepdims=True)
    outs = []

    def store(src, dst):
        cp = pltpu.make_async_copy(src, dst, s.ldo.at[len(outs)])
        cp.start()
        outs.append(cp)

    for i in range(2):
        store(s.so.at[i], so_ref.at[:, i])
    for q in range(4):
        s.J2X[2 * c, pl.ds(q * 128, 128), mycols] = s.rlow[:, q * 128 : q * 128 + 128].T
    cp_low = to_sib(s.J2X.at[0, :, mycols], s.J2X.at[2, :, mycols])

    @pl.when(c == 0)
    def _():
        cp_low.start()

    res = ar_recv(2)
    norm_params(3, res, 2048, s.bnm, 512)
    halo_down_wait(3, s.ym.at[pl.ds(0, 128)])
    halo_up_wait(4, s.ym.at[pl.ds(384, 128)])

    def edge_at(i):
        lo = jnp.logical_and(i < 8, first)
        hi = jnp.logical_and(i >= 24, last)
        return 1.0 - jnp.logical_or(lo, hi).astype(F32)

    def windows(i, val):
        n = i % 8
        s.pad[n, 8:24, :] = val
        for k in range(3):
            rows = pl.ds(al(k * 512 + i * 16, 16), 16)
            s.X[rows, :] = (val if k == 1 else s.pad[n, 7 + k : 23 + k, :]).astype(BF)

    def act_mid(i, _):
        zv = s.ym[rows16(i), :] * s.bnm[0:1, :] + s.bnm[1:2, :]
        windows(i, mish_of(zv) * edge_at(i))
        return 0

    tiles(32, act_mid)
    for i in range(3):
        loads["ws%d" % i].wait()

    def conv_four(h, _):
        col = al(h * 256, 256)
        cols = pl.ds(col, 256)
        acc = None
        for t in range(9):
            part = mm(s.X[pl.ds((t % 3) * 512 + (t // 3) * 128, 256), :], s.ws[t, :, cols])
            acc = part if acc is None else acc + part
        s.y4[pl.ds(128, 256), cols] = acc
        colstats(acc, 3, col, 256)
        return 0

    lax.fori_loop(0, 2, conv_four, 0)
    ar_send(3)
    halo_down(5, s.y4.at[pl.ds(256, 128)], s.y4.at[pl.ds(0, 128)])
    halo_up(6, s.y4.at[pl.ds(128, 128)], s.y4.at[pl.ds(384, 128)])
    x_start((3,), (1,))

    def slope_mid(i, _):
        zv = s.ym[pl.ds(al(128 + i * 16, 16), 16), :] * s.bnm[0:1, :] + s.bnm[1:2, :]
        s.dm[rows16(i), :] = mish_slope(zv)
        return 0

    tiles(16, slope_mid)

    def window_t(tap, dst, k):
        base = pl.ds(al((tap % 3) * 512 + (tap // 3) * 128, 128), 256)
        for q in range(4):
            dst[k, pl.ds(q * 128, 128), mycols] = s.X[base, q * 128 : q * 128 + 128].T

    def xpose_mid(k, _):
        window_t(1 + 4 * c + k, s.MT, k)
        window_t(5 - 4 * c + k, s.st2, k)
        return 0

    lax.fori_loop(0, 4, xpose_mid, 0)
    window_t(0 * c, s.J2X, 1 + 2 * c)
    cp_mt = to_sib(s.st2.at[:, :, mycols], s.MT.at[:, :, mycols])
    cp_mt.start()
    cp_m0 = to_sib(s.J2X.at[1, :, mycols], s.J2X.at[3, :, mycols])

    @pl.when(c == 0)
    def _():
        cp_m0.start()

    loads["bc0"].wait()
    loads["bc1"].wait()
    halo_down_wait(1, s.bc.at[0])
    halo_up_wait(2, s.bc.at[3])

    res = ar_recv(3)
    norm_params(4, res, 2560, s.bn4, 512)

    def norm_four(i, carry):
        t1, t2 = carry
        v = valid_at(i)
        rows = pl.ds(al(128 + i * 16, 16), 16)
        yv = s.y4[rows, :]
        zv = yv * s.bn4[0:1, :] + s.bn4[1:2, :]
        e, d, t = mish_parts(zv)
        s.bo[i // 8, i % 8] = ((zv * t + s.actr[rows16(i), :]) * v).astype(BF)
        gz = (t + 4.0 * zv * (e * (1.0 + e)) * (d * d)) * (s.bc[1 + i // 8, i % 8].astype(F32) * v)
        s.g4[rows, :] = gz
        gx = gz * (yv * s.bn4[2:3, :] + s.bn4[3:4, :])
        return t1 + gz, t2 + gx

    t1, t2 = tiles(16, norm_four, (zero16, zero16), unroll=1)
    st[4][0:1, 0:512] = jnp.sum(t1, axis=0, keepdims=True)
    st[4][1:2, 0:512] = jnp.sum(t2, axis=0, keepdims=True)
    ar_send(4)
    x_start((1, 2, 3), (2,))
    for i in range(2):
        store(s.bo.at[i], bo_ref.at[:, i])

    halo_down_wait(5, s.y4.at[pl.ds(0, 128)])
    halo_up_wait(6, s.y4.at[pl.ds(384, 128)])

    def halo_four(k, _):
        i = k + 16 * (k // 8)
        v = valid_at(i)
        zv = s.y4[rows16(i), :] * s.bn4[0:1, :] + s.bn4[1:2, :]
        s.g4[rows16(i), :] = mish_slope(zv) * (s.bc[i // 8, i % 8].astype(F32) * v)
        return 0

    tiles(16, halo_four)

    def back_params(res, lo, bn, width):
        inv_t = s.tot[0:1, 0:width]
        bg_ref[0:1, pl.ds(lo, width)] = res[0:1]
        gg_ref[0:1, pl.ds(lo, width)] = res[1:2]
        bn[4:5, :] = res[0:1] * inv_t
        bn[5:6, :] = res[1:2] * inv_t

    def grad_of(gz, yv, bn, v):
        xh = yv * bn[2:3, :] + bn[3:4, :]
        return bn[0:1, :] * (gz - v * (bn[4:5, :] + xh * bn[5:6, :]))

    res = ar_recv(4)
    back_params(res[:, 0:512], 2560, s.bn4, 512)
    back_params(res[:, 512:1024], 1024, s.bnl, 512)

    def grad_four(i, _):
        v = valid_at(i) * edge_at(i)
        windows(i, grad_of(s.g4[rows16(i), :], s.y4[rows16(i), :], s.bn4, v).astype(BF).astype(F32))
        return 0

    tiles(32, grad_four)

    def back_four(h, _):
        col = al(h * 256, 256)
        acc = None
        for t in range(9):
            part = mm_nt(
                s.X[pl.ds((2 - t % 3) * 512 + (2 - t // 3) * 128, 256), :], s.ws[t, pl.ds(col, 256), :]
            )
            acc = part if acc is None else acc + part
        cols = pl.ds(col, 256)
        gz = s.dm[:, cols] * acc
        s.dm[:, cols] = gz
        xh = s.ym[pl.ds(128, 256), cols] * s.bnm[2:3, cols] + s.bnm[3:4, cols]
        st[5][0:1, cols] = jnp.sum(gz, axis=0, keepdims=True)
        st[5][1:2, cols] = jnp.sum(gz * xh, axis=0, keepdims=True)
        return 0

    lax.fori_loop(0, 2, back_four, 0)
    ar_send(5)

    def grad_left(i, _):
        val = grad_of(s.gl[rows16(i), :], s.yl[rows16(i), :], s.bnl, valid_at(i)).astype(BF)
        s.glb[rows16(i), :] = val
        s.GA[pl.ds(al(c * 256 + i * 16, 16), 16), :] = val
        return 0

    tiles(16, grad_left)
    myrows = pl.ds(al(c * 256, 256), 256)
    s.G4[myrows, :] = s.X[640:896, :]
    cp_g4 = to_sib(s.G4.at[myrows], s.G4.at[myrows])
    cp_g4.start()
    cp_ga = to_sib(s.glb, s.GA.at[myrows])

    @pl.when(c == 1)
    def _():
        cp_ga.start()

    def both_waits(cp, sender):
        pl.when(c == sender)(cp.wait_send)
        pl.when(c != sender)(cp.wait_recv)

    cp_act.wait()
    both_waits(cp_low, 0)
    cp_mt.wait()
    both_waits(cp_m0, 0)
    cp_g4.wait()

    def half_of(ref, k, hf):
        return ref.at[k, pl.ds(hf * 256, 256)]

    def plane_copy(job, j, hf):
        stage, slots = ((st3, s.pr3), (s.st2, s.pr2))[job]
        return remote(
            half_of(stage, plane[j], hf), half_of(slots, j - 1, hf),
            s.ps.at[job, j - 1, hf], s.pr.at[job, j - 1, hf], (r, plane[j]),
        )

    def piece(lhs, k, rhs, stage):
        def body(i, _):
            rows = pl.ds(al((i // 2) * 256, 256), 256)
            cols = pl.ds(al((i % 2) * 256, 256), 256)
            stage[k, rows, cols] = mm(lhs[k, rows, :], rhs[:, cols]).astype(BF)
            return 0

        lax.fori_loop(0, 4, body, 0)

    for k in range(3):
        for dc in range(2):
            for j in range(4):
                cp = x_copy(dc, j, k)
                x_when(dc, j, k, cp.wait if dc == 0 and j == 0 else cp.wait_send)
    st3 = s.xst

    def piece3(j):
        piece(s.MT, plane[j], s.G4, st3)

    piece3(1)
    piece3(2)
    for j in (1, 2):
        plane_copy(0, j, 0).start()
    piece3(3)
    piece3(0)

    res = ar_recv(5)
    back_params(res, 2048, s.bnm, 512)

    def grad_mid(i, _):
        val = grad_of(
            s.dm[rows16(i), :], s.ym[pl.ds(al(128 + i * 16, 16), 16), :], s.bnm, valid_at(i)
        ).astype(BF)
        s.gm[rows16(i), :] = val
        s.GB[pl.ds(al(c * 256 + i * 16, 16), 16), :] = val
        return 0

    tiles(16, grad_mid)

    def back_mid(h, _):
        col = al(h * 256, 256)
        cols = pl.ds(col, 256)
        acc = mm_nt(s.gm[...], s.wm[cols, :]).reshape(2, 8, 16, 256)
        t1 = jnp.zeros((16, 256), F32)
        t2 = jnp.zeros((16, 256), F32)
        for rr in range(2):
            for n in range(8):
                rows = pl.ds(rr * 128 + n * 16, 16)
                cot = s.sc[rr, n, :, pl.ds(al(512 + h * 256, 256), 256)].astype(F32) + s.bc[
                    1 + rr, n, :, cols
                ].astype(F32)
                gz = s.dr[rows, cols] * (acc[rr, n] + cot * vs[n])
                s.dr[rows, cols] = gz
                t1 = t1 + gz
                t2 = t2 + gz * (s.yr[rows, cols] * s.bnr[2:3, cols] + s.bnr[3:4, cols])
        st[6][0:1, cols] = jnp.sum(t1, axis=0, keepdims=True)
        st[6][1:2, cols] = jnp.sum(t2, axis=0, keepdims=True)
        return 0

    lax.fori_loop(0, 2, back_mid, 0)
    ar_send(6)

    cp_gb = to_sib(s.gm, s.GB.at[myrows])

    @pl.when(c == 0)
    def _():
        cp_gb.start()

    for j in (1, 2):
        plane_copy(0, j, 1).start()
    both_waits(cp_ga, 1)
    both_waits(cp_gb, 0)

    @pl.when(c == 0)
    def _():
        for k in (2, 3):
            piece(s.J2X, k, s.GA, s.st2)

    @pl.when(c == 1)
    def _():
        piece(s.J2X, 3, s.G4, s.st2)
        piece(s.J2X, 2, s.GB, s.st2)

    res = ar_recv(6)
    back_params(res, 1536, s.bnr, 512)

    def grad_right(i, _):
        val = grad_of(s.dr[rows16(i), :], s.yr[rows16(i), :], s.bnr, valid_at(i)).astype(BF)
        s.gr[rows16(i), :] = val

        return 0

    tiles(16, grad_right)

    def back_one(h, _):
        cols = pl.ds(al(h * 256, 256), 256)
        acc = mm_nt(s.glb[...], s.wl[cols, :]) + mm_nt(s.gr[...], s.wr[cols, :])
        gz = s.d1[:, cols] * acc
        s.d1[:, cols] = gz
        xh = s.y1[:, cols] * s.bn0[2:3, cols] + s.bn0[3:4, cols]
        st[7][0:1, cols] = jnp.sum(gz, axis=0, keepdims=True)
        st[7][1:2, cols] = jnp.sum(gz * xh, axis=0, keepdims=True)
        return 0

    lax.fori_loop(0, 4, back_one, 0)
    ar_send(7)

    @pl.when(c == 1)
    def _():
        s.GA[myrows, :] = s.gr[...]

    cp_gr = to_sib(s.gr, s.GA.at[myrows])

    @pl.when(c == 0)
    def _():
        cp_gr.start()

    for hf in range(2):
        plane_copy(0, 3, hf).start()
    both_waits(cp_gr, 0)

    @pl.when(c == 1)
    def _():
        for k in (0, 1):
            piece(s.J2X, k, s.GA, s.st2)

    res = ar_recv(7)
    back_params(res, 0, s.bn0, 1024)

    def grad_one(i, _):
        val = grad_of(s.d1[rows16(i), :], s.y1[rows16(i), :], s.bn0, valid_at(i))
        low = val.astype(BF)
        s.G0[rows16(i), :] = low
        s.Gall[pl.ds(al(own8 * 256 + i * 16, 16), 16), :] = low
        return 0

    tiles(16, grad_one)

    halo_up(7, s.G0.at[pl.ds(0, 128)], s.G0.at[pl.ds(256, 128)])

    def g_block(core, batch, q):
        return s.Gall.at[pl.ds(al((core * 4 + batch) * 256, 256), 256), pl.ds(al(q * 256, 256), 256)]

    def g_direct(q, j):
        blk = g_block(c, b, q)
        return remote(blk, blk, s.gs.at[q, j - 1], s.grs.at[q, j - 1], (r, plane[j]))

    def g_forward(q, j):
        blk = g_block(c, plane[j], q)
        return remote(blk, blk, s.gfs.at[q, j], s.gfr.at[q, j], sib)

    is_tap8 = jnp.logical_and(c == 0, y == 0)
    has_plane2 = jnp.logical_not(is_tap8)

    def to_piece_owner(j):
        return jnp.logical_or(c == 1, plane[j] // 2 == 1)

    for q in range(4):
        for j in (1, 2, 3):
            g_direct(q, j).start()
        g_forward(q, 0).start()
    for j in (1, 2, 3):

        @pl.when(to_piece_owner(j))
        def _():
            for hf in range(2):
                plane_copy(1, j, hf).start()

    for dc in range(2):
        for j in range(4):
            if dc or j:
                idx = dc * 4 + j
                src8 = ((c + dc) % 2) * 4 + plane[j]
                for k in range(3):
                    dst = s.XG.at[k, :, pl.ds(al(src8 * 256, 256), 256)]
                    x_got = lambda: recv_wait(dst, s.xr.at[k, idx])
                    if k < 2:
                        x_got()
                    else:
                        pl.when(is_tap8)(x_got)

    def chain(zp, slot, own, down_job):
        far = max(zp, 3 - zp)
        lag = jnp.where(z < zp, z, jnp.where(z > zp, 3 - z, far))
        q = slot - lag

        @pl.when(jnp.logical_and(q >= 0, q < 4))
        def _():
            own(q)
            if zp > 0:

                @pl.when(jnp.logical_and(z > 0, z <= zp))
                def _():
                    got = s.zb.at[zp - 1, q]
                    recv_wait(got, s.zur.at[zp, q])
                    s.tile[...] = s.tile[...] + got[...].astype(F32)

            if zp < 3:

                @pl.when(jnp.logical_and(z < 3, z >= zp))
                def _():
                    got = s.za.at[zp, q]
                    recv_wait(got, s.zdr.at[zp, q])
                    s.tile[...] = s.tile[...] + got[...].astype(F32)

            if zp > 0:

                @pl.when(z < zp)
                def _():
                    s.zs[zp, q] = s.tile[...].astype(BF)
                    remote(
                        s.zs.at[zp, q], s.zb.at[zp - 1, q], s.zus.at[zp, q], s.zur.at[zp, q], (r + 2, b)
                    ).start()

            if zp < 3:

                @pl.when(z > zp)
                def _():
                    s.zs[zp, q] = s.tile[...].astype(BF)
                    remote(
                        s.zs.at[zp, q], s.za.at[zp, q], s.zds.at[zp, q], s.zdr.at[zp, q], (r - 2, b)
                    ).start()

            def final_down():
                for h in range(2):
                    s.wgo[pl.ds(2 * q + h, 256, stride=8), :] = s.tile[:, h * 128 : h * 128 + 128]

            def final_tile():
                for h in range(2):
                    s.wgo[pl.ds((q // 2) * 1024 + (q % 2) * 2 + h, 256, stride=4), :] = s.tile[
                        :, h * 128 : h * 128 + 128
                    ]

            @pl.when(z == zp)
            def _():
                if down_job is True:
                    final_down()
                elif down_job is False:
                    final_tile()
                else:
                    pl.when(down_job)(final_down)
                    pl.when(jnp.logical_not(down_job))(final_tile)

    def chain_drain(zp, q):
        if zp > 0:

            @pl.when(z < zp)
            def _():
                pltpu.make_async_copy(s.zs.at[zp, q], s.zs.at[zp, q], s.zus.at[zp, q]).wait()

        if zp < 3:

            @pl.when(z > zp)
            def _():
                pltpu.make_async_copy(s.zs.at[zp, q], s.zs.at[zp, q], s.zds.at[zp, q]).wait()

    def own_plane(stage, slots, q):
        rows = pl.ds(al((q // 2) * 256, 256), 256)
        cols = pl.ds(al((q % 2) * 256, 256), 256)
        v = stage[b, rows, cols].astype(F32)
        for j in range(3):
            v = v + slots[j, rows, cols].astype(F32)
        s.tile[...] = v

    def own_down(k, q):
        s.tile[...] = mm(s.XG[k], s.Gall[:, pl.ds(al(q * 256, 256), 256)])

    def own_two(q):
        pl.when(is_tap8)(lambda: own_down(2, q))
        pl.when(has_plane2)(lambda: own_plane(s.st2, s.pr2, q))

    def shift_one(i, _):
        n = i % 8
        for h in range(2):
            cols = pl.ds(h * 512, 512)
            s.pad[n, 8:24, :] = s.G0[rows16(i), cols].astype(F32)
            s.Gp[rows16(i), cols] = s.pad[n, 9:25, :].astype(BF)
        return 0

    lax.fori_loop(0, 16, shift_one, 0)

    def back_conv(h, par):
        ch = pl.ds(al(h * 256, 256), 256)

        def part(src, row, tap):
            return mm_nt(src[pl.ds(row * 128, 256), :], s.wd[tap, ch, :])

        if par == 0:
            even = part(s.G0, 0, 4)
            odd = part(s.G0, 0, 5) + part(s.Gp, 0, 3)
        else:
            even = part(s.G0, 0, 7) + part(s.G0, 1, 1)
            odd = (part(s.G0, 0, 8) + part(s.Gp, 0, 6)) + (part(s.G0, 1, 2) + part(s.Gp, 1, 0))
        for q in range(2):
            s.igf[q, pl.ds(0, 256, stride=2), :] = even[:, q * 128 : q * 128 + 128]
            s.igf[q, pl.ds(1, 256, stride=2), :] = odd[:, q * 128 : q * 128 + 128]
        for rr in range(2):
            for q in range(2):
                s.inraw[2 * rr + par, :, :, pl.ds(al(h * 256 + q * 128, 128), 128)] = (
                    s.igf[q, rr * 256 : rr * 256 + 256, :].astype(BF).reshape(8, 32, 128)
                )

    def step(slot, _):
        pl.when(slot < 2)(lambda: back_conv(slot, 0))

        @pl.when(slot == 2)
        def _():
            halo_up_wait(7, s.G0.at[pl.ds(256, 128)])
            lax.fori_loop(16, 24, shift_one, 0)

        pl.when(jnp.logical_and(slot >= 2, slot < 4))(lambda: back_conv(slot - 2, 1))

        @pl.when(slot < 4)
        def _():
            for j in (1, 2, 3):
                recv_wait(g_block(c, plane[j], slot), s.grs.at[slot, j - 1])
                g_forward(slot, j).start()
            for j in range(4):
                recv_wait(g_block(1 - c, plane[j], slot), s.gfr.at[slot, j])

        chain(0, slot, lambda q: own_down(0, q), True)
        chain(1, slot, lambda q: own_down(1, q), True)

        @pl.when(slot == LATE3)
        def _():
            for j in (1, 2, 3):
                for hf in range(2):
                    recv_wait(half_of(s.pr3, j - 1, hf), s.pr.at[0, j - 1, hf])

        chain(3, slot - LATE3, lambda q: own_plane(st3, s.pr3, q), False)

        @pl.when(jnp.logical_and(slot == LATE2, has_plane2))
        def _():
            for j in (1, 2, 3):
                for hf in range(2):
                    recv_wait(half_of(s.pr2, j - 1, hf), s.pr.at[1, j - 1, hf])

        chain(2, slot - jnp.where(is_tap8, 0, LATE2), own_two, is_tap8)
        return 0

    lax.fori_loop(0, 7 + max(LATE2 - 1, LATE3), step, 0)
    store(s.wgo, wg_ref)
    for i in range(4):
        store(s.inraw.at[i], ig_ref.at[:, i])

    for q in range(4):
        for zp in range(4):
            chain_drain(zp, q)
        for j in (1, 2, 3):
            g_direct(q, j).wait_send()
        for j in range(4):
            g_forward(q, j).wait_send()
    for j in (1, 2, 3):
        for hf in range(2):
            plane_copy(0, j, hf).wait_send()
            pl.when(to_piece_owner(j))(lambda: plane_copy(1, j, hf).wait_send())
    for cp in outs:
        cp.wait()


LATE3 = 1
LATE2 = 4


def hand_over(n, *refs):
    ins, outs, held = refs[:n], refs[n : 2 * n], refs[2 * n : 3 * n]
    sems = refs[3 * n]
    got = [pltpu.make_async_copy(ins[i], held[i], sems.at[0, i]) for i in range(n)]
    put = [pltpu.make_async_copy(held[i], outs[i], sems.at[1, i]) for i in range(n)]
    for cp in got:
        cp.start()
    for i in range(n):
        got[i].wait()
        put[i].start()
    for cp in put:
        cp.wait()


def fused_step(
    inputs, counts, down_weight, left_weight, right_weight, reduce_weight, spread_weight,
    norm_gains, norm_biases, running_mean, running_var, section_cotangent, block_cotangent,
):
    table = scratch_table()
    names = tuple(table)
    sds = jax.ShapeDtypeStruct
    row = (1, 3072)
    vmem = pl.BlockSpec(memory_space=pltpu.VMEM)
    smem = pl.BlockSpec(memory_space=pltpu.SMEM)
    hbm = pl.BlockSpec(memory_space=pl.ANY)
    outs = pl.pallas_call(
        functools.partial(fused_kernel, names, 13, 8),
        out_shape=(
            sds((8, 2, 16, 1024), BF),
            sds((8, 2, 16, 512), BF),
            sds((8, 4, 32, 512), BF),
            sds((2048, 128), F32),
            sds(row, F32),
            sds(row, F32),
            sds(row, F32),
            sds(row, F32),
        ),
        in_specs=[hbm, smem, hbm, hbm, hbm, hbm, hbm, vmem, vmem, vmem, vmem, hbm, hbm],
        out_specs=(hbm, hbm, hbm, hbm, vmem, vmem, vmem, vmem),
        scratch_shapes=list(table.values()),
        compiler_params=pltpu.CompilerParams(
            collective_id=0, has_side_effects=True, vmem_limit_bytes=64 * 2**20 - 2**16
        ),
        cost_estimate=pl.CostEstimate(flops=13 * 10**9, bytes_accessed=21 * 10**6, transcendentals=10**6),
    )(
        inputs, counts, down_weight.reshape((9,) + down_weight.shape[2:]), left_weight, right_weight,
        reduce_weight, spread_weight.reshape((9,) + spread_weight.shape[2:]),
        norm_gains.reshape(row), norm_biases.reshape(row), running_mean.reshape(row), running_var.reshape(row),
        section_cotangent, block_cotangent,
    )
    n = len(outs)
    so, bo, ig, wg, gg, bg, nm, nv = pl.pallas_call(
        functools.partial(hand_over, n),
        out_shape=tuple(sds(o.shape, o.dtype) for o in outs),
        in_specs=[hbm] * n,
        out_specs=(hbm,) * n,
        scratch_shapes=[pltpu.VMEM(o.shape, o.dtype) for o in outs] + [pltpu.SemaphoreType.DMA((2, n))],
        cost_estimate=pl.CostEstimate(flops=0, bytes_accessed=6 * 10**6, transcendentals=0),
    )(*outs)
    return (so, bo, ig, wg.reshape(-1), gg.reshape(-1), bg.reshape(-1), nm.reshape(-1), nv.reshape(-1))


def fits_fused(mesh):
    return dict(mesh.shape) == {"rows": 8, "batch": 4}


def solution(mesh):
    placed = (
        P("batch", "rows", None, None),
        P("batch"),
        P(),
        P(),
        P(),
        P(),
        P(),
        P(),
        P(),
        P(),
        P(),
        P("batch", "rows", None, None),
        P("batch", "rows", None, None),
    )
    return jax.shard_map(
        fused_step if fits_fused(mesh) else on_device,
        mesh=mesh,
        in_specs=placed,
        out_specs=(
            P("batch", "rows", None, None),
            P("batch", "rows", None, None),
            P("batch", "rows", None, None),
            P(("rows", "batch")),
            P(),
            P(),
            P(),
            P(),
        ),
        check_vma=False,
    )
```

```python
import functools
import types

import jax
import jax.numpy as jnp
from jax import lax
from jax.experimental import pallas as pl
from jax.experimental.pallas import tpu as pltpu
from jax.sharding import PartitionSpec as P

EPS = 1e-05
MOMENTUM = 0.1


def passed_along(block, axis, distance):
    devices = range(lax.axis_size(axis))
    route = [(i - distance, i) for i in devices if i - distance in devices]
    return lax.ppermute(block, axis, route)


def padded_2(block, sides, width):
    for axis, dim in sides:
        count = lax.axis_size(axis)
        forward = [(i, i + 1) for i in range(count - 1)]
        backward = [(target, source) for source, target in forward]
        low = lax.ppermute(
            lax.slice_in_dim(block, block.shape[dim] - width, None, axis=dim), axis, forward
        )
        high = lax.ppermute(lax.slice_in_dim(block, 0, width, axis=dim), axis, backward)
        block = jnp.concatenate([low, block, high], axis=dim)
    return block


def mish_act(values):
    return values * jnp.tanh(jax.nn.softplus(values))


def mish_back(before, grad_out):
    return jax.vjp(mish_act, before)[1](grad_out)[0]


def point_dot(left_op, right_op):
    return jnp.einsum("nhwc,cd->nhwd", left_op, right_op, preferred_element_type=jnp.float32)


def back_dot(left_op, right_op):
    return jnp.einsum("nhwd,cd->nhwc", left_op, right_op, preferred_element_type=jnp.float32)


def outer_dot(left_op, right_op):
    return jnp.einsum("nhwc,nhwd->cd", left_op, right_op, preferred_element_type=jnp.float32)


def norm_forward(values, valid_mask, gain_vec, offset, local_pixels):
    sum_first = jnp.sum(values * valid_mask, axis=(0, 1, 2))
    sum_second = jnp.sum(values * values * valid_mask, axis=(0, 1, 2))
    sum_first, sum_second, pixel_total = lax.psum(
        (sum_first, sum_second, local_pixels), ("rows", "batch")
    )
    batch_mean = sum_first / pixel_total
    batch_var = sum_second / pixel_total - batch_mean * batch_mean
    inv_std = lax.rsqrt(batch_var + EPS)
    normed = (values - batch_mean) * inv_std
    return (normed * gain_vec + offset, normed, inv_std, batch_mean, batch_var, pixel_total)


def norm_back(grad_out, normed, inv_std, gain_vec, valid_mask, pixel_total):
    bias_grad, gain_grad = lax.psum(
        (jnp.sum(grad_out, axis=(0, 1, 2)), jnp.sum(grad_out * normed, axis=(0, 1, 2))),
        ("rows", "batch"),
    )
    grad_in = (
        gain_vec
        * inv_std
        * (grad_out - valid_mask * (bias_grad + normed * gain_grad) / pixel_total)
    )
    return (grad_in, gain_grad, bias_grad)


def on_device(
    inputs,
    counts,
    down_weight,
    left_weight,
    right_weight,
    reduce_weight,
    spread_weight,
    norm_gains,
    norm_biases,
    running_mean,
    running_var,
    section_cotangent,
    block_cotangent,
):
    n_slots, row_in, col_in, in_width = inputs.shape
    row_out = row_in // 2
    col_out = col_in // 2
    section_width = down_weight.shape[3]
    branch_width = right_weight.shape[1]
    bounds = [
        0,
        section_width,
        section_width + branch_width,
        section_width + 2 * branch_width,
        section_width + 3 * branch_width,
        section_width + 4 * branch_width,
    ]
    valid_mask = (
        (jnp.arange(n_slots, dtype=jnp.int32) < counts[0])
        .astype(jnp.float32)
        .reshape(n_slots, 1, 1, 1)
    )
    local_pixels = jnp.sum(valid_mask) * float(row_out * col_out)

    def gain_at(bn_index):
        return norm_gains[bounds[bn_index] : bounds[bn_index + 1]]

    def norm_at(values, bn_index):
        return norm_forward(
            values,
            valid_mask,
            gain_at(bn_index),
            norm_biases[bounds[bn_index] : bounds[bn_index + 1]],
            local_pixels,
        )

    rim_row = passed_along(inputs[:, row_in - 1 :], "rows", 1)
    padded = jnp.pad(jnp.concatenate([rim_row, inputs], axis=1), ((0, 0), (0, 0), (1, 1), (0, 0)))
    taps = []
    first_out = jnp.zeros((n_slots, row_out, col_out, section_width), jnp.float32)
    for row_tap in range(3):
        for col_tap in range(3):
            window = padded[
                :, row_tap : row_tap + 2 * row_out : 2, col_tap : col_tap + 2 * col_out : 2, :
            ]
            taps.append(window)
            first_out = first_out + point_dot(window, down_weight[row_tap, col_tap])
    z_one, normed_one, inv_one, mean_one, var_one, pixel_total = norm_at(first_out, 0)
    act_one = mish_act(z_one).astype(jnp.bfloat16)
    z_left, normed_left, inv_left, mean_left, var_left, pixel_total = norm_at(
        point_dot(act_one, left_weight), 1
    )
    act_left = mish_act(z_left)
    z_right, normed_right, inv_right, mean_right, var_right, pixel_total = norm_at(
        point_dot(act_one, right_weight), 2
    )
    act_right = mish_act(z_right)
    right_low = act_right.astype(jnp.bfloat16)
    z_mid, normed_mid, inv_mid, mean_mid, var_mid, pixel_total = norm_at(
        point_dot(right_low, reduce_weight), 3
    )
    act_mid = mish_act(z_mid).astype(jnp.bfloat16)
    mid_halo = padded_2(act_mid, (("rows", 1),), 1)
    mid_pad = jnp.pad(mid_halo, ((0, 0), (0, 0), (1, 1), (0, 0)))
    fourth_out = jnp.zeros((n_slots, row_out, col_out, branch_width), jnp.float32)
    for row_tap in range(3):
        for col_tap in range(3):
            fourth_out = fourth_out + point_dot(
                mid_pad[:, row_tap : row_tap + row_out, col_tap : col_tap + col_out, :],
                spread_weight[row_tap, col_tap],
            )
    z_four, normed_four, inv_four, mean_four, var_four, pixel_total = norm_at(fourth_out, 4)
    act_four = mish_act(z_four)
    section_out = (valid_mask * jnp.concatenate([act_left, act_right], axis=3)).astype(jnp.bfloat16)
    block_out = (valid_mask * (act_right + act_four)).astype(jnp.bfloat16)
    section_grad = valid_mask * section_cotangent.astype(jnp.float32)
    block_grad = valid_mask * block_cotangent.astype(jnp.float32)
    grad_four, gain_four, bias_four = norm_back(
        mish_back(z_four, block_grad), normed_four, inv_four, gain_at(4), valid_mask, pixel_total
    )
    grad_four = grad_four.astype(jnp.bfloat16)
    grad_halo = padded_2(grad_four, (("rows", 1),), 1)
    grad_pad = jnp.pad(grad_halo, ((0, 0), (0, 0), (1, 1), (0, 0)))
    spread_taps = []
    mid_grad = jnp.zeros((n_slots, row_out, col_out, branch_width), jnp.float32)
    for row_tap in range(3):
        for col_tap in range(3):
            spread_taps.append(
                outer_dot(
                    mid_pad[:, row_tap : row_tap + row_out, col_tap : col_tap + col_out, :],
                    grad_four,
                )
            )
            mid_grad = mid_grad + back_dot(
                grad_pad[
                    :, 2 - row_tap : 2 - row_tap + row_out, 2 - col_tap : 2 - col_tap + col_out, :
                ],
                spread_weight[row_tap, col_tap],
            )
    spread_grad = jnp.stack(spread_taps).reshape(spread_weight.shape)
    grad_mid, gain_mid, bias_mid = norm_back(
        mish_back(z_mid, mid_grad), normed_mid, inv_mid, gain_at(3), valid_mask, pixel_total
    )
    grad_mid = grad_mid.astype(jnp.bfloat16)
    reduce_grad = outer_dot(right_low, grad_mid)
    right_total = section_grad[..., branch_width:] + block_grad + back_dot(grad_mid, reduce_weight)
    grad_right, gain_right, bias_right = norm_back(
        mish_back(z_right, right_total),
        normed_right,
        inv_right,
        gain_at(2),
        valid_mask,
        pixel_total,
    )
    grad_right = grad_right.astype(jnp.bfloat16)
    grad_left, gain_left, bias_left = norm_back(
        mish_back(z_left, section_grad[..., :branch_width]),
        normed_left,
        inv_left,
        gain_at(1),
        valid_mask,
        pixel_total,
    )
    grad_left = grad_left.astype(jnp.bfloat16)
    left_grad = outer_dot(act_one, grad_left)
    right_grad = outer_dot(act_one, grad_right)
    one_total = back_dot(grad_left, left_weight) + back_dot(grad_right, right_weight)
    grad_one, gain_one, bias_one = norm_back(
        mish_back(z_one, one_total), normed_one, inv_one, gain_at(0), valid_mask, pixel_total
    )
    grad_one = grad_one.astype(jnp.bfloat16)
    down_taps = []
    spread_back = jnp.zeros(padded.shape, jnp.float32)
    for row_tap in range(3):
        for col_tap in range(3):
            down_taps.append(outer_dot(taps[row_tap * 3 + col_tap], grad_one))
            spread_back = spread_back.at[
                :, row_tap : row_tap + 2 * row_out : 2, col_tap : col_tap + 2 * col_out : 2, :
            ].add(back_dot(grad_one, down_weight[row_tap, col_tap]))
    down_grad = jnp.stack(down_taps).reshape(down_weight.shape)
    back_rim = passed_along(
        spread_back[:, 0:1, 1 : col_in + 1].astype(jnp.bfloat16), "rows", -1
    ).astype(jnp.float32)
    input_grad = spread_back[:, 1:, 1 : col_in + 1]
    input_grad = input_grad.at[:, row_in - 1 :].add(back_rim)
    flat_grads = jnp.concatenate(
        [
            down_grad.reshape(-1),
            left_grad.reshape(-1),
            right_grad.reshape(-1),
            reduce_grad.reshape(-1),
            spread_grad.reshape(-1),
        ]
    )
    row_share = lax.psum_scatter(
        flat_grads.astype(jnp.bfloat16), "rows", scatter_dimension=0, tiled=True
    )
    weight_share = lax.psum_scatter(row_share, "batch", scatter_dimension=0, tiled=True).astype(
        jnp.float32
    )
    gain_grads = jnp.concatenate([gain_one, gain_left, gain_right, gain_mid, gain_four])
    bias_grads = jnp.concatenate([bias_one, bias_left, bias_right, bias_mid, bias_four])
    means_all = jnp.concatenate([mean_one, mean_left, mean_right, mean_mid, mean_four])
    vars_all = jnp.concatenate([var_one, var_left, var_right, var_mid, var_four])
    new_mean = (1.0 - MOMENTUM) * running_mean + MOMENTUM * means_all
    new_var = (1.0 - MOMENTUM) * running_var + MOMENTUM * vars_all * (
        pixel_total / (pixel_total - 1.0)
    )
    return (
        section_out,
        block_out,
        input_grad.astype(jnp.bfloat16),
        weight_share,
        gain_grads,
        bias_grads,
        new_mean,
        new_var,
    )


MESHID = pl.DeviceIdType.MESH
BF = jnp.bfloat16
F32 = jnp.float32
NT = (((1,), (1,)), ((), ()))


def mm(lhs, rhs):
    return jnp.dot(lhs, rhs, preferred_element_type=F32)


def mm_nt(lhs, rhs):
    return lax.dot_general(lhs, rhs, NT, preferred_element_type=F32)


def mish_parts(z):
    e = jnp.exp(jnp.minimum(z, 20.0))
    n = e * (e + 2.0)
    d = 1.0 / (n + 2.0)
    return e, d, n * d


def mish_of(z):
    return z * mish_parts(z)[2]


def mish_slope(z):
    e, d, t = mish_parts(z)
    return t + 4.0 * z * (e * (1.0 + e)) * (d * d)


def al(i, m):
    return pl.multiple_of(i, m)


def scratch_table():
    v = pltpu.VMEM
    dma = pltpu.SemaphoreType.DMA
    table = dict(
        inraw=v((5, 8, 32, 512), BF),
        tmpc=v((8, 4, 40, 128), F32),
        pad=v((8, 32, 512), F32),
        X=v((2304, 512), BF),
        xst=v((5, 512, 512), BF),
        XG=v((3, 256, 2048), BF),
        wd=v((9, 512, 1024), BF),
        wl=v((1024, 512), BF),
        wr=v((1024, 512), BF),
        wm=v((512, 512), BF),
        ws=v((9, 512, 512), BF),
        sc=v((2, 8, 16, 1024), BF),
        bc=v((4, 8, 16, 512), BF),
        so=v((2, 8, 16, 1024), BF),
        bo=v((2, 8, 16, 512), BF),
        y1=v((256, 1024), F32),
        d1=v((256, 1024), F32),
        act1=v((256, 1024), BF),
        yl=v((256, 512), F32),
        yr=v((256, 512), F32),
        gl=v((256, 512), F32),
        dr=v((256, 512), F32),
        actr=v((256, 512), F32),
        rlow=v((256, 512), BF),
        ym=v((512, 512), F32),
        dm=v((256, 512), F32),
        y4=v((512, 512), F32),
        g4=v((512, 512), F32),
        gm=v((256, 512), BF),
        gr=v((256, 512), BF),
        glb=v((256, 512), BF),
        GA=v((512, 512), BF),
        GB=v((512, 512), BF),
        G4=v((512, 512), BF),
        J2X=v((4, 512, 512), BF),
        MT=v((4, 512, 512), BF),
        st2=v((4, 512, 512), BF),
        pr2=v((3, 512, 512), BF),
        pr3=v((3, 512, 512), BF),
        Gall=v((2048, 1024), BF),
        G0=v((384, 1024), BF),
        Gp=v((256 + 128, 1024), BF),
        igf=v((2, 512, 128), F32),
        zb=v((3, 4, 256, 256), BF),
        za=v((3, 4, 256, 256), BF),
        zs=v((4, 4, 256, 256), BF),
        wgo=v((2048, 128), F32),
        bn0=v((8, 1024), F32),
        bnl=v((8, 512), F32),
        bnr=v((8, 512), F32),
        bnm=v((8, 512), F32),
        bn4=v((8, 512), F32),
        tot=v((1, 1024), F32),
        ld=dma((32,)),
        ldo=dma((16,)),
        hs=dma((12,)),
        hr=dma((12,)),
        cs=dma((8,)),
        cr=dma((8,)),
        as_=dma((8,)),
        ar_=dma((8,)),
        xs=dma((3, 8)),
        xr=dma((3, 8)),
        bs=dma((12,)),
        br=dma((12,)),
        ps=dma((2, 2, 3)),
        pr=dma((2, 2, 3)),
        gs=dma((4, 3)),
        grs=dma((4, 3)),
        gfs=dma((4, 4)),
        gfr=dma((4, 4)),
        zus=dma((4, 8)),
        zur=dma((4, 8)),
        zds=dma((4, 8)),
        zdr=dma((4, 8)),
    )
    widths = AR_WIDTHS
    for k, w in enumerate(widths):
        table["ar_st%d" % k] = v((2, w), F32)
        table["ar_ct%d" % k] = v((2, w), F32)
        table["ar_ab%d" % k] = v((16, 2, w), F32)
    return table


AR_WIDTHS = (1152, 1024, 512, 1024, 512, 512, 512, 1024)


def fused_kernel(names, n_in, n_out, *refs):
    (in_ref, cnt_ref, wd_ref, wl_ref, wr_ref, wm_ref, ws_ref, gain_ref, bias_ref, rm_ref, rv_ref,
     sc_ref, bc_ref) = refs[:n_in]
    (so_ref, bo_ref, ig_ref, wg_ref, gg_ref, bg_ref, nm_ref, nv_ref) = refs[n_in : n_in + n_out]
    s = types.SimpleNamespace(**dict(zip(names, refs[n_in + n_out :])))
    st = [getattr(s, "ar_st%d" % k) for k in range(8)]
    ct = [getattr(s, "ar_ct%d" % k) for k in range(8)]
    ab = [getattr(s, "ar_ab%d" % k) for k in range(8)]

    r = lax.axis_index("rows")
    b = lax.axis_index("batch")
    z = r // 2
    c = r % 2
    y = b // 2
    x = b % 2
    chip = z * 4 + b
    sib = (r + 1 - 2 * c, b)
    own8 = c * 4 + b
    first = r == 0
    last = r == 7
    plane = [b, b + 1 - 2 * x, b + 2 - 4 * y, 3 - b]

    def remote(src, dst, ss, rs, dev):
        return pltpu.make_async_remote_copy(
            src_ref=src, dst_ref=dst, send_sem=ss, recv_sem=rs, device_id=dev, device_id_type=MESHID
        )

    def recv_wait(dst, rs):
        pltpu.make_async_copy(dst, dst, rs).wait()

    bar = pltpu.get_barrier_semaphore()
    for i in range(8):
        for j in range(4):
            if i or j:
                pl.semaphore_signal(
                    bar, inc=1, device_id=((r + i) % 8, (b + j) % 4), device_id_type=MESHID
                )

    loads = {}

    def load(name, src, dst):
        cp = pltpu.make_async_copy(src, dst, s.ld.at[len(loads)])
        cp.start()
        loads[name] = cp

    for i in range(4):
        load("in%d" % i, in_ref.at[:, i], s.inraw.at[1 + i])
    for t in (3, 4, 5, 6, 7, 8, 0, 1, 2):
        load("wd%d" % t, wd_ref.at[t], s.wd.at[t])
    load("wl", wl_ref, s.wl)
    load("wr", wr_ref, s.wr)
    load("wm", wm_ref, s.wm)
    for i in range(2):
        load("sc%d" % i, sc_ref.at[:, i], s.sc.at[i])
        load("bc%d" % i, bc_ref.at[:, i], s.bc.at[1 + i])
    for i in range(3):
        load("ws%d" % i, ws_ref.at[pl.ds(3 * i, 3)], s.ws.at[pl.ds(3 * i, 3)])

    for n in range(8):
        for q in range(4):
            s.tmpc[n, q, 0:8, :] = jnp.zeros((8, 128), F32)
        s.pad[n, 0:8, :] = jnp.zeros((8, 512), F32)
        s.pad[n, 24:32, :] = jnp.zeros((8, 512), F32)

    @pl.when(first)
    def _():
        s.inraw[0] = jnp.zeros((8, 32, 512), BF)
        s.bc[0] = jnp.zeros((8, 16, 512), BF)
        s.ym[0:128, :] = jnp.zeros((128, 512), F32)
        s.y4[0:128, :] = jnp.zeros((128, 512), F32)

    @pl.when(last)
    def _():
        s.bc[3] = jnp.zeros((8, 16, 512), BF)
        s.ym[384:512, :] = jnp.zeros((128, 512), F32)
        s.y4[384:512, :] = jnp.zeros((128, 512), F32)
        s.G0[256:384, :] = jnp.zeros((128, 1024), BF)

    nxt = (r + 1, b)
    prv = (r - 1, b)

    def halo_down(k, src, dst):
        @pl.when(r < 7)
        def _():
            remote(src, dst, s.hs.at[k], s.hr.at[k], nxt).start()

    def halo_up(k, src, dst):
        @pl.when(r > 0)
        def _():
            remote(src, dst, s.hs.at[k], s.hr.at[k], prv).start()

    def halo_down_wait(k, dst):
        @pl.when(r < 7)
        def _():
            pltpu.make_async_copy(dst, dst, s.hs.at[k]).wait()

        @pl.when(r > 0)
        def _():
            recv_wait(dst, s.hr.at[k])

    def halo_up_wait(k, dst):
        @pl.when(r > 0)
        def _():
            pltpu.make_async_copy(dst, dst, s.hs.at[k]).wait()

        @pl.when(r < 7)
        def _():
            recv_wait(dst, s.hr.at[k])

    count = cnt_ref[0]
    vs = [(jnp.int32(n) < count).astype(F32) for n in range(8)]

    def ar_send(k):
        cp = remote(st[k], ct[k], s.cs.at[k], s.cr.at[k], sib)
        cp.start()
        cp.wait()
        ab[k][chip] = st[k][...] + ct[k][...]
        for j in range(1, 16):
            dev = (((z + j // 4) % 4) * 2 + c, (b + j % 4) % 4)
            remote(ab[k].at[chip], ab[k].at[chip], s.as_.at[k], s.ar_.at[k], dev).start()

    def ar_recv(k):
        part = ab[k].at[pl.ds(0, 15)]
        pltpu.make_async_copy(part, part, s.ar_.at[k]).wait()
        pltpu.make_async_copy(part, part, s.as_.at[k]).wait()
        out = ab[k][0]
        for j in range(1, 16):
            out = out + ab[k][j]
        return out

    def colstats(acc, k, col, width):
        a = acc.reshape(2, 8, 16, width)
        t1 = jnp.zeros((16, width), F32)
        t2 = jnp.zeros((16, width), F32)
        for n in range(8):
            p = a[0, n]
            q = a[1, n]
            t1 = t1 + (p + q) * vs[n]
            t2 = t2 + (p * p + q * q) * vs[n]
        st[k][0:1, pl.ds(col, width)] = jnp.sum(t1, axis=0, keepdims=True)
        st[k][1:2, pl.ds(col, width)] = jnp.sum(t2, axis=0, keepdims=True)

    def tiles(count_, body, init=0, unroll=2):
        return lax.fori_loop(0, count_, body, init, unroll=unroll)

    def rows16(i):
        return pl.ds(al(i * 16, 16), 16)

    def deinterleave(slot):
        targets = [(i, rr) for rr in range(2) for i in range(3) if i + 2 * rr == slot]

        def body(n, _):
            for q in range(4):
                s.tmpc[n, q, 8:40, :] = s.inraw[slot, n, :, q * 128 : q * 128 + 128].astype(F32)
            for j in range(3):
                for q in range(4):
                    val = s.tmpc[n, q, pl.ds(7 + j, 16, stride=2), :].astype(BF)
                    for i, rr in targets:
                        s.X[pl.ds(al((3 * i + j) * 256 + rr * 128 + n * 16, 16), 16), q * 128 : q * 128 + 128] = val
            return 0

        lax.fori_loop(0, 8, body, 0)

    for i in range(4):
        loads["in%d" % i].wait()
        deinterleave(1 + i)
    pl.semaphore_wait(bar, 31)
    halo_down(0, in_ref.at[:, 3], s.inraw.at[0])
    halo_down(1, bc_ref.at[:, 1], s.bc.at[0])
    halo_up(2, bc_ref.at[:, 0], s.bc.at[3])
    for t in (3, 4, 5, 6, 7, 8):
        loads["wd%d" % t].wait()

    def conv_a(n, _):
        cols = pl.ds(al(n * 256, 256), 256)
        acc = mm(s.X[3 * 256 : 4 * 256, :], s.wd[3, :, cols])
        for t in range(4, 9):
            acc = acc + mm(s.X[t * 256 : t * 256 + 256, :], s.wd[t, :, cols])
        s.y1[:, cols] = acc
        return 0

    lax.fori_loop(0, 4, conv_a, 0)
    halo_down_wait(0, s.inraw.at[0])
    deinterleave(0)
    for t in (0, 1, 2):
        loads["wd%d" % t].wait()
    st[0][:, 1024:1152] = jnp.zeros((2, 128), F32) + count.astype(F32) * 32.0

    def conv_b(n, _):
        col = al(n * 256, 256)
        cols = pl.ds(col, 256)
        acc = s.y1[:, cols]
        for t in range(3):
            acc = acc + mm(s.X[t * 256 : t * 256 + 256, :], s.wd[t, :, cols])
        s.y1[:, cols] = acc
        colstats(acc, 0, col, 256)
        return 0

    lax.fori_loop(0, 4, conv_b, 0)
    ar_send(0)

    def xpose(t, _):
        for q in range(4):
            s.xst[t // 2, q * 128 : q * 128 + 128, pl.ds(al((t % 2) * 256, 256), 256)] = s.X[
                pl.ds(al(t * 256, 256), 256), q * 128 : q * 128 + 128
            ].T
        return 0

    lax.fori_loop(0, 9, xpose, 0)

    def x_copy(dc, j, k):
        cc = (c + dc) % 2
        bb = plane[j]
        yy = bb // 2
        xx = bb % 2
        half = pl.ds(al(xx * 256, 256), 256)
        mine = pl.ds(al(own8 * 256, 256), 256)
        tap = 2 * cc + yy + 4 * k if k < 2 else 8
        src = s.xst.at[tap // 2, half, pl.ds(al((tap % 2) * 256, 256), 256)]
        dst = s.XG.at[k, :, mine]
        idx = dc * 4 + j
        if dc == 0 and j == 0:
            return pltpu.make_async_copy(src, dst, s.xs.at[k, idx])
        return remote(src, dst, s.xs.at[k, idx], s.xr.at[k, idx], (z * 2 + cc, bb))

    def x_when(dc, j, k, do):
        if k < 2:
            do()
        else:
            pl.when(jnp.logical_and((c + dc) % 2 == 0, plane[j] // 2 == 0))(do)

    def x_start(js, ks):
        for k in ks:
            for dc in range(2):
                for j in js:
                    x_when(dc, j, k, lambda: x_copy(dc, j, k).start())

    x_start((1, 2), (0,))
    x_start((0,), (0, 1, 2))

    def norm_params(k, res, lo, bn, width):
        g = gain_ref[0:1, pl.ds(lo, width)]
        o = bias_ref[0:1, pl.ds(lo, width)]
        inv_t = s.tot[0:1, 0:width]
        mean = res[0:1] * inv_t
        var = res[1:2] * inv_t - mean * mean
        inv = lax.rsqrt(var + EPS)
        a = g * inv
        bn[0:1, :] = a
        bn[1:2, :] = o - mean * a
        bn[2:3, :] = inv
        bn[3:4, :] = -mean * inv
        nm_ref[0:1, pl.ds(lo, width)] = (1.0 - MOMENTUM) * rm_ref[0:1, pl.ds(lo, width)] + MOMENTUM * mean
        t = 1.0 / inv_t
        nv_ref[0:1, pl.ds(lo, width)] = (1.0 - MOMENTUM) * rv_ref[0:1, pl.ds(lo, width)] + MOMENTUM * var * (
            t / (t - 1.0)
        )

    res = ar_recv(0)
    s.tot[0:1, :] = jnp.broadcast_to(1.0 / res[0:1, 1024:1025], (1, 1024))
    norm_params(0, res[:, 0:1024], 0, s.bn0, 1024)

    def act_one(i, _):
        zv = s.y1[rows16(i), :] * s.bn0[0:1, :] + s.bn0[1:2, :]
        s.act1[rows16(i), :] = mish_of(zv).astype(BF)
        return 0

    tiles(16, act_one)
    loads["wl"].wait()
    loads["wr"].wait()

    for h in range(2):
        cols = pl.ds(h * 256, 256)
        acc = mm(s.act1[...], s.wl[:, cols])
        s.yl[:, cols] = acc
        colstats(acc, 1, h * 256, 256)
        acc = mm(s.act1[...], s.wr[:, cols])
        s.yr[:, cols] = acc
        colstats(acc, 1, 512 + h * 256, 256)
    ar_send(1)

    def slope_one(i, _):
        zv = s.y1[rows16(i), :] * s.bn0[0:1, :] + s.bn0[1:2, :]
        s.d1[rows16(i), :] = mish_slope(zv)
        return 0

    tiles(16, slope_one)
    mycols = pl.ds(al(c * 256, 256), 256)

    def xpose_act(h, _):
        for q in range(4):
            blk = s.act1[:, pl.ds(al(h * 512 + q * 128, 128), 128)]
            s.J2X[2 - 2 * c + h, pl.ds(q * 128, 128), mycols] = blk.T
        return 0

    lax.fori_loop(0, 2, xpose_act, 0)
    pair = []

    def to_sib(src, dst):
        k = len(pair)
        cp = remote(src, dst, s.bs.at[k], s.br.at[k], sib)
        pair.append(cp)
        return cp

    cp_act = to_sib(s.J2X.at[pl.ds(2 - 2 * c, 2), :, mycols], s.J2X.at[pl.ds(2 * c, 2), :, mycols])
    cp_act.start()
    x_start((1, 2), (1,))

    res = ar_recv(1)
    norm_params(1, res[:, 0:512], 1024, s.bnl, 512)
    norm_params(2, res[:, 512:1024], 1536, s.bnr, 512)

    def act_right(i, _):
        zv = s.yr[rows16(i), :] * s.bnr[0:1, :] + s.bnr[1:2, :]
        e, d, t = mish_parts(zv)
        a = zv * t
        s.actr[rows16(i), :] = a
        s.rlow[rows16(i), :] = a.astype(BF)
        s.dr[rows16(i), :] = t + 4.0 * zv * (e * (1.0 + e)) * (d * d)
        return 0

    tiles(16, act_right)
    loads["wm"].wait()
    for h in range(2):
        cols = pl.ds(h * 256, 256)
        acc = mm(s.rlow[...], s.wm[:, cols])
        s.ym[128:384, cols] = acc
        colstats(acc, 2, h * 256, 256)
    ar_send(2)
    halo_down(3, s.ym.at[pl.ds(256, 128)], s.ym.at[pl.ds(0, 128)])
    halo_up(4, s.ym.at[pl.ds(128, 128)], s.ym.at[pl.ds(384, 128)])
    x_start((3,), (0,))

    loads["sc0"].wait()
    loads["sc1"].wait()

    def valid_at(i):
        return ((i % 8) < count).astype(F32)

    def left_branch(i, carry):
        t1, t2 = carry
        v = valid_at(i)
        yv = s.yl[rows16(i), :]
        zv = yv * s.bnl[0:1, :] + s.bnl[1:2, :]
        e, d, t = mish_parts(zv)
        s.so[i // 8, i % 8, :, 0:512] = (zv * t * v).astype(BF)
        s.so[i // 8, i % 8, :, 512:1024] = (s.actr[rows16(i), :] * v).astype(BF)
        gz = (t + 4.0 * zv * (e * (1.0 + e)) * (d * d)) * (s.sc[i // 8, i % 8, :, 0:512].astype(F32) * v)
        s.gl[rows16(i), :] = gz
        gx = gz * (yv * s.bnl[2:3, :] + s.bnl[3:4, :])
        return t1 + gz, t2 + gx

    zero16 = jnp.zeros((16, 512), F32)
    t1, t2 = tiles(16, left_branch, (zero16, zero16), unroll=1)
    st[3][0:1, 512:1024] = jnp.sum(t1, axis=0, keepdims=True)
    st[3][1:2, 512:1024] = jnp.sum(t2, axis=0, keepdims=True)
    outs = []

    def store(src, dst):
        cp = pltpu.make_async_copy(src, dst, s.ldo.at[len(outs)])
        cp.start()
        outs.append(cp)

    for i in range(2):
        store(s.so.at[i], so_ref.at[:, i])
    for q in range(4):
        s.J2X[2 * c, pl.ds(q * 128, 128), mycols] = s.rlow[:, q * 128 : q * 128 + 128].T
    cp_low = to_sib(s.J2X.at[0, :, mycols], s.J2X.at[2, :, mycols])

    @pl.when(c == 0)
    def _():
        cp_low.start()

    res = ar_recv(2)
    norm_params(3, res, 2048, s.bnm, 512)
    halo_down_wait(3, s.ym.at[pl.ds(0, 128)])
    halo_up_wait(4, s.ym.at[pl.ds(384, 128)])

    def edge_at(i):
        lo = jnp.logical_and(i < 8, first)
        hi = jnp.logical_and(i >= 24, last)
        return 1.0 - jnp.logical_or(lo, hi).astype(F32)

    def windows(i, val):
        n = i % 8
        s.pad[n, 8:24, :] = val
        for k in range(3):
            rows = pl.ds(al(k * 512 + i * 16, 16), 16)
            s.X[rows, :] = (val if k == 1 else s.pad[n, 7 + k : 23 + k, :]).astype(BF)

    def act_mid(i, _):
        zv = s.ym[rows16(i), :] * s.bnm[0:1, :] + s.bnm[1:2, :]
        windows(i, mish_of(zv) * edge_at(i))
        return 0

    tiles(32, act_mid)
    for i in range(3):
        loads["ws%d" % i].wait()

    def conv_four(h, _):
        col = al(h * 256, 256)
        cols = pl.ds(col, 256)
        acc = None
        for t in range(9):
            part = mm(s.X[pl.ds((t % 3) * 512 + (t // 3) * 128, 256), :], s.ws[t, :, cols])
            acc = part if acc is None else acc + part
        s.y4[pl.ds(128, 256), cols] = acc
        colstats(acc, 3, col, 256)
        return 0

    lax.fori_loop(0, 2, conv_four, 0)
    ar_send(3)
    halo_down(5, s.y4.at[pl.ds(256, 128)], s.y4.at[pl.ds(0, 128)])
    halo_up(6, s.y4.at[pl.ds(128, 128)], s.y4.at[pl.ds(384, 128)])
    x_start((3,), (1,))

    def slope_mid(i, _):
        zv = s.ym[pl.ds(al(128 + i * 16, 16), 16), :] * s.bnm[0:1, :] + s.bnm[1:2, :]
        s.dm[rows16(i), :] = mish_slope(zv)
        return 0

    tiles(16, slope_mid)

    def window_t(tap, dst, k):
        base = pl.ds(al((tap % 3) * 512 + (tap // 3) * 128, 128), 256)
        for q in range(4):
            dst[k, pl.ds(q * 128, 128), mycols] = s.X[base, q * 128 : q * 128 + 128].T

    def xpose_mid(k, _):
        window_t(1 + 4 * c + k, s.MT, k)
        window_t(5 - 4 * c + k, s.st2, k)
        return 0

    lax.fori_loop(0, 4, xpose_mid, 0)
    window_t(0 * c, s.J2X, 1 + 2 * c)
    cp_mt = to_sib(s.st2.at[:, :, mycols], s.MT.at[:, :, mycols])
    cp_mt.start()
    cp_m0 = to_sib(s.J2X.at[1, :, mycols], s.J2X.at[3, :, mycols])

    @pl.when(c == 0)
    def _():
        cp_m0.start()

    loads["bc0"].wait()
    loads["bc1"].wait()
    halo_down_wait(1, s.bc.at[0])
    halo_up_wait(2, s.bc.at[3])

    def back_params(res, lo, bn, width):
        inv_t = s.tot[0:1, 0:width]
        bg_ref[0:1, pl.ds(lo, width)] = res[0:1]
        gg_ref[0:1, pl.ds(lo, width)] = res[1:2]
        bn[4:5, :] = res[0:1] * inv_t
        bn[5:6, :] = res[1:2] * inv_t

    def grad_of(gz, yv, bn, v):
        xh = yv * bn[2:3, :] + bn[3:4, :]
        return bn[0:1, :] * (gz - v * (bn[4:5, :] + xh * bn[5:6, :]))

    res = ar_recv(3)
    norm_params(4, res[:, 0:512], 2560, s.bn4, 512)
    back_params(res[:, 512:1024], 1024, s.bnl, 512)

    def norm_four(i, carry):
        t1, t2 = carry
        v = valid_at(i)
        rows = pl.ds(al(128 + i * 16, 16), 16)
        yv = s.y4[rows, :]
        zv = yv * s.bn4[0:1, :] + s.bn4[1:2, :]
        e, d, t = mish_parts(zv)
        s.bo[i // 8, i % 8] = ((zv * t + s.actr[rows16(i), :]) * v).astype(BF)
        gz = (t + 4.0 * zv * (e * (1.0 + e)) * (d * d)) * (s.bc[1 + i // 8, i % 8].astype(F32) * v)
        s.g4[rows, :] = gz
        gx = gz * (yv * s.bn4[2:3, :] + s.bn4[3:4, :])
        return t1 + gz, t2 + gx

    t1, t2 = tiles(16, norm_four, (zero16, zero16), unroll=1)
    st[4][0:1, :] = jnp.sum(t1, axis=0, keepdims=True)
    st[4][1:2, :] = jnp.sum(t2, axis=0, keepdims=True)
    ar_send(4)
    x_start((1, 2, 3), (2,))
    myrows = pl.ds(al(c * 256, 256), 256)
    st3 = s.xst

    def grad_left(i, _):
        val = grad_of(s.gl[rows16(i), :], s.yl[rows16(i), :], s.bnl, valid_at(i)).astype(BF)
        s.glb[rows16(i), :] = val
        s.GA[pl.ds(al(c * 256 + i * 16, 16), 16), :] = val
        return 0

    tiles(16, grad_left)
    cp_ga = to_sib(s.glb, s.GA.at[myrows])

    @pl.when(c == 1)
    def _():
        cp_ga.start()

    def both_waits(cp, sender):
        pl.when(c == sender)(cp.wait_send)
        pl.when(c != sender)(cp.wait_recv)

    def half_of(ref, k, hf):
        return ref.at[k, pl.ds(hf * 256, 256)]

    def owned(job, j):
        return True if job == 0 else jnp.logical_or(c == 1, plane[j] // 2 == 1)

    def when_owned(job, j, do):
        if job == 0:
            do()
        else:
            pl.when(owned(job, j))(do)

    def plane_copy(job, hf, m):
        stage, slots = ((st3, s.pr3), (s.st2, s.pr2))[job]
        near, far = ((1, 2), (2, 1))[hf]
        src = (near, 3, far)[m]
        to = (near, near, far)[m]
        cp = remote(
            half_of(stage, plane[src], hf), half_of(slots, m, hf), s.ps.at[job, hf, m], s.pr.at[job, hf, m],
            (r, plane[to]),
        )
        return cp, src, (0, far, 0)[m]

    def plane_start(job, hf, m):
        cp, src, _ = plane_copy(job, hf, m)
        when_owned(job, src, cp.start)

    def plane_got(job, hf, m):
        cp, _, mine_at = plane_copy(job, hf, m)
        when_owned(job, mine_at, cp.wait_recv)

    def plane_sent(job, hf, m):
        cp, src, _ = plane_copy(job, hf, m)
        when_owned(job, src, cp.wait_send)

    def plane_second(job, hf):
        stage, slots = ((st3, s.pr3), (s.st2, s.pr2))[job]
        far = (2, 1)[hf]
        plane_got(job, hf, 1)

        def add():
            def body(i, _):
                rows = pl.ds(al(hf * 256 + i * 16, 16), 16)
                k = plane[far]
                stage[k, rows, :] = (stage[k, rows, :].astype(F32) + slots[1, rows, :].astype(F32)).astype(BF)
                return 0

            lax.fori_loop(0, 16, body, 0)

        when_owned(job, far, add)
        plane_start(job, hf, 2)

    def piece(lhs, k, rhs, stage):
        def body(i, _):
            rows = pl.ds(al((i // 2) * 256, 256), 256)
            cols = pl.ds(al((i % 2) * 256, 256), 256)
            stage[k, rows, cols] = mm(lhs[k, rows, :], rhs[:, cols]).astype(BF)
            return 0

        lax.fori_loop(0, 4, body, 0)

    cp_act.wait()
    cp_mt.wait()
    both_waits(cp_ga, 1)

    @pl.when(c == 0)
    def _():
        for k in (2, 3):
            piece(s.J2X, k, s.GA, s.st2)
        for m in (1, 0):
            for hf in range(2):
                plane_start(1, hf, m)

    for i in range(2):
        store(s.bo.at[i], bo_ref.at[:, i])

    halo_down_wait(5, s.y4.at[pl.ds(0, 128)])
    halo_up_wait(6, s.y4.at[pl.ds(384, 128)])

    def halo_four(k, _):
        i = k + 16 * (k // 8)
        v = valid_at(i)
        zv = s.y4[rows16(i), :] * s.bn4[0:1, :] + s.bn4[1:2, :]
        s.g4[rows16(i), :] = mish_slope(zv) * (s.bc[i // 8, i % 8].astype(F32) * v)
        return 0

    tiles(16, halo_four)

    res = ar_recv(4)
    back_params(res, 2560, s.bn4, 512)

    def grad_four(i, _):
        v = valid_at(i) * edge_at(i)
        windows(i, grad_of(s.g4[rows16(i), :], s.y4[rows16(i), :], s.bn4, v).astype(BF).astype(F32))
        return 0

    tiles(32, grad_four)

    def back_four(h, _):
        col = al(h * 256, 256)
        acc = None
        for t in range(9):
            part = mm_nt(
                s.X[pl.ds((2 - t % 3) * 512 + (2 - t // 3) * 128, 256), :], s.ws[t, pl.ds(col, 256), :]
            )
            acc = part if acc is None else acc + part
        cols = pl.ds(col, 256)
        gz = s.dm[:, cols] * acc
        s.dm[:, cols] = gz
        xh = s.ym[pl.ds(128, 256), cols] * s.bnm[2:3, cols] + s.bnm[3:4, cols]
        st[5][0:1, cols] = jnp.sum(gz, axis=0, keepdims=True)
        st[5][1:2, cols] = jnp.sum(gz * xh, axis=0, keepdims=True)
        return 0

    lax.fori_loop(0, 2, back_four, 0)
    ar_send(5)

    s.G4[myrows, :] = s.X[640:896, :]
    cp_g4 = to_sib(s.G4.at[myrows], s.G4.at[myrows])
    cp_g4.start()
    both_waits(cp_low, 0)
    both_waits(cp_m0, 0)
    cp_g4.wait()

    for k in range(3):
        for dc in range(2):
            for j in range(4):
                cp = x_copy(dc, j, k)
                x_when(dc, j, k, cp.wait if dc == 0 and j == 0 else cp.wait_send)

    def piece3(j):
        piece(s.MT, plane[j], s.G4, st3)

    piece3(3)
    for hf in range(2):
        plane_start(0, hf, 1)

    @pl.when(c == 0)
    def _():
        for hf in range(2):
            plane_second(1, hf)

    piece3(1)
    piece3(2)

    res = ar_recv(5)
    back_params(res, 2048, s.bnm, 512)

    def grad_mid(i, _):
        val = grad_of(
            s.dm[rows16(i), :], s.ym[pl.ds(al(128 + i * 16, 16), 16), :], s.bnm, valid_at(i)
        ).astype(BF)
        s.gm[rows16(i), :] = val
        s.GB[pl.ds(al(c * 256 + i * 16, 16), 16), :] = val
        return 0

    tiles(16, grad_mid)

    def back_mid(h, _):
        col = al(h * 256, 256)
        cols = pl.ds(col, 256)
        acc = mm_nt(s.gm[...], s.wm[cols, :]).reshape(2, 8, 16, 256)
        t1 = jnp.zeros((16, 256), F32)
        t2 = jnp.zeros((16, 256), F32)
        for rr in range(2):
            for n in range(8):
                rows = pl.ds(rr * 128 + n * 16, 16)
                cot = s.sc[rr, n, :, pl.ds(al(512 + h * 256, 256), 256)].astype(F32) + s.bc[
                    1 + rr, n, :, cols
                ].astype(F32)
                gz = s.dr[rows, cols] * (acc[rr, n] + cot * vs[n])
                s.dr[rows, cols] = gz
                t1 = t1 + gz
                t2 = t2 + gz * (s.yr[rows, cols] * s.bnr[2:3, cols] + s.bnr[3:4, cols])
        st[6][0:1, cols] = jnp.sum(t1, axis=0, keepdims=True)
        st[6][1:2, cols] = jnp.sum(t2, axis=0, keepdims=True)
        return 0

    lax.fori_loop(0, 2, back_mid, 0)
    ar_send(6)

    cp_gb = to_sib(s.gm, s.GB.at[myrows])

    @pl.when(c == 0)
    def _():
        cp_gb.start()

    for hf in range(2):
        plane_start(0, hf, 0)
    piece3(0)
    both_waits(cp_gb, 0)

    @pl.when(c == 1)
    def _():
        piece(s.J2X, 3, s.G4, s.st2)
        piece(s.J2X, 2, s.GB, s.st2)

    res = ar_recv(6)
    back_params(res, 1536, s.bnr, 512)

    def grad_right(i, _):
        val = grad_of(s.dr[rows16(i), :], s.yr[rows16(i), :], s.bnr, valid_at(i)).astype(BF)
        s.gr[rows16(i), :] = val

        return 0

    tiles(16, grad_right)

    def back_one(h, _):
        cols = pl.ds(al(h * 256, 256), 256)
        acc = mm_nt(s.glb[...], s.wl[cols, :]) + mm_nt(s.gr[...], s.wr[cols, :])
        gz = s.d1[:, cols] * acc
        s.d1[:, cols] = gz
        xh = s.y1[:, cols] * s.bn0[2:3, cols] + s.bn0[3:4, cols]
        st[7][0:1, cols] = jnp.sum(gz, axis=0, keepdims=True)
        st[7][1:2, cols] = jnp.sum(gz * xh, axis=0, keepdims=True)
        return 0

    lax.fori_loop(0, 4, back_one, 0)
    ar_send(7)

    @pl.when(c == 1)
    def _():
        s.GA[myrows, :] = s.gr[...]

    cp_gr = to_sib(s.gr, s.GA.at[myrows])

    @pl.when(c == 0)
    def _():
        cp_gr.start()

    for hf in range(2):
        plane_second(0, hf)
    both_waits(cp_gr, 0)

    @pl.when(c == 1)
    def _():
        for k in (0, 1):
            piece(s.J2X, k, s.GA, s.st2)

    res = ar_recv(7)
    back_params(res, 0, s.bn0, 1024)

    def grad_one(i, _):
        val = grad_of(s.d1[rows16(i), :], s.y1[rows16(i), :], s.bn0, valid_at(i))
        low = val.astype(BF)
        s.G0[rows16(i), :] = low
        s.Gall[pl.ds(al(own8 * 256 + i * 16, 16), 16), :] = low
        return 0

    tiles(16, grad_one)

    halo_up(7, s.G0.at[pl.ds(0, 128)], s.G0.at[pl.ds(256, 128)])

    def g_block(core, batch, q):
        return s.Gall.at[pl.ds(al((core * 4 + batch) * 256, 256), 256), pl.ds(al(q * 256, 256), 256)]

    def g_direct(q, j):
        blk = g_block(c, b, q)
        return remote(blk, blk, s.gs.at[q, j - 1], s.grs.at[q, j - 1], (r, plane[j]))

    def g_forward(q, j):
        blk = g_block(c, plane[j], q)
        return remote(blk, blk, s.gfs.at[q, j], s.gfr.at[q, j], sib)

    is_tap8 = jnp.logical_and(c == 0, y == 0)
    has_plane2 = jnp.logical_not(is_tap8)

    for q in range(4):
        for j in (1, 2, 3):
            g_direct(q, j).start()
        g_forward(q, 0).start()
        if q == 3:

            @pl.when(c == 1)
            def _():
                for m in (1, 0):
                    for hf in range(2):
                        plane_start(1, hf, m)


    for dc in range(2):
        for j in range(4):
            if dc or j:
                idx = dc * 4 + j
                src8 = ((c + dc) % 2) * 4 + plane[j]
                for k in range(3):
                    dst = s.XG.at[k, :, pl.ds(al(src8 * 256, 256), 256)]
                    x_got = lambda: recv_wait(dst, s.xr.at[k, idx])
                    if k < 2:
                        x_got()
                    else:
                        pl.when(is_tap8)(x_got)

    def half_tile(ref, k, q, h):
        return ref.at[k, q, pl.ds(h * 128, 128)]

    def chain(zp, q, own, put, here):
        @pl.when(jnp.logical_and(here, jnp.logical_and(q >= 0, q < 4)))
        def _():
            val = own(q)

            def below(h):
                got = half_tile(s.zb, zp - 1, q, h)
                recv_wait(got, s.zur.at[zp, 2 * q + h])
                return got[...].astype(F32)

            def above(h):
                got = half_tile(s.za, zp, q, h)
                recv_wait(got, s.zdr.at[zp, 2 * q + h])
                return got[...].astype(F32)

            def mine(h):
                return val[h * 128 : h * 128 + 128]

            def up(h, v):
                part = half_tile(s.zs, zp, q, h)
                part[...] = v.astype(BF)
                there = half_tile(s.zb, zp - 1, q, h)
                remote(part, there, s.zus.at[zp, 2 * q + h], s.zur.at[zp, 2 * q + h], (r + 2, b)).start()

            def down(h, v):
                part = half_tile(s.zs, zp, q, h)
                part[...] = v.astype(BF)
                there = half_tile(s.za, zp, q, h)
                remote(part, there, s.zds.at[zp, 2 * q + h], s.zdr.at[zp, 2 * q + h], (r - 2, b)).start()

            def each(do):
                def both():
                    for h in range(2):
                        do(h)

                return both

            if zp > 0:
                pl.when(z == 0)(each(lambda h: up(h, mine(h))))
            if zp > 1:
                pl.when(jnp.logical_and(z > 0, z < zp))(each(lambda h: up(h, mine(h) + below(h))))
            if zp < 3:
                pl.when(z == 3)(each(lambda h: down(h, mine(h))))
            if zp < 2:
                pl.when(jnp.logical_and(z > zp, z < 3))(each(lambda h: down(h, mine(h) + above(h))))

            @pl.when(z == zp)
            def _():
                for h in range(2):
                    v = mine(h)
                    if zp > 0:
                        v = v + below(h)
                    if zp < 3:
                        v = v + above(h)
                    put(q, h, v)

    def put_down(q, h, v):
        for i in range(2):
            s.wgo[pl.ds(h * 1024 + 2 * q + i, 128, stride=8), :] = v[:, i * 128 : i * 128 + 128]

    def put_tile(q, h, v):
        base = (q // 2) * 1024 + h * 512 + (q % 2) * 2
        for i in range(2):
            s.wgo[pl.ds(base + i, 128, stride=4), :] = v[:, i * 128 : i * 128 + 128]

    def chain_drain(zp, q):
        for h in range(2):
            part = half_tile(s.zs, zp, q, h)
            if zp > 0:

                @pl.when(z < zp)
                def _():
                    pltpu.make_async_copy(part, part, s.zus.at[zp, 2 * q + h]).wait()

            if zp < 3:

                @pl.when(z > zp)
                def _():
                    pltpu.make_async_copy(part, part, s.zds.at[zp, 2 * q + h]).wait()

    def own_plane(stage, slots, q):
        rows = pl.ds(al((q // 2) * 256, 256), 256)
        cols = pl.ds(al((q % 2) * 256, 256), 256)
        v = stage[b, rows, cols].astype(F32)
        for m in (0, 2):
            v = v + slots[m, rows, cols].astype(F32)
        return v

    def own_down(k, q):
        return mm(s.XG[k], s.Gall[:, pl.ds(al(q * 256, 256), 256)])

    def shift_one(i, _):
        n = i % 8
        for h in range(2):
            cols = pl.ds(h * 512, 512)
            s.pad[n, 8:24, :] = s.G0[rows16(i), cols].astype(F32)
            s.Gp[rows16(i), cols] = s.pad[n, 9:25, :].astype(BF)
        return 0

    lax.fori_loop(0, 16, shift_one, 0)

    def back_conv(h, par):
        ch = pl.ds(al(h * 256, 256), 256)

        def part(src, row, tap):
            return mm_nt(src[pl.ds(row * 128, 256), :], s.wd[tap, ch, :])

        if par == 0:
            even = part(s.G0, 0, 4)
            odd = part(s.G0, 0, 5) + part(s.Gp, 0, 3)
        else:
            even = part(s.G0, 0, 7) + part(s.G0, 1, 1)
            odd = (part(s.G0, 0, 8) + part(s.Gp, 0, 6)) + (part(s.G0, 1, 2) + part(s.Gp, 1, 0))
        for q in range(2):
            s.igf[q, pl.ds(0, 256, stride=2), :] = even[:, q * 128 : q * 128 + 128]
            s.igf[q, pl.ds(1, 256, stride=2), :] = odd[:, q * 128 : q * 128 + 128]
        for rr in range(2):
            for q in range(2):
                s.inraw[2 * rr + par, :, :, pl.ds(al(h * 256 + q * 128, 128), 128)] = (
                    s.igf[q, rr * 256 : rr * 256 + 256, :].astype(BF).reshape(8, 32, 128)
                )

    left2 = jnp.logical_and(c == 0, y == 1)
    late2 = c == 1

    def step(slot, _):
        pl.when(slot < 2)(lambda: back_conv(slot, 0))

        @pl.when(slot == 0)
        def _():
            for hf in range(2):
                plane_got(0, hf, 0)
                plane_got(0, hf, 2)
            tiles4(job3, z == 0)

        @pl.when(jnp.logical_and(slot == 0, c == 0))
        def _():
            for hf in range(2):
                plane_got(1, hf, 0)
                plane_got(1, hf, 2)
            tiles4(job2, jnp.logical_and(left2, z % 3 == 0))

        @pl.when(slot < 4)
        def _():
            for j in (1, 2, 3):
                recv_wait(g_block(c, plane[j], slot), s.grs.at[slot, j - 1])
                g_forward(slot, j).start()
            for j in range(4):
                recv_wait(g_block(1 - c, plane[j], slot), s.gfr.at[slot, j])

        job0(slot - (3 - z), z > 0)
        job1(slot - jnp.where(z == 2, 1, 0), z != 1)
        tap8(slot - 2 * (z % 3), jnp.logical_and(is_tap8, z != 2))

        @pl.when(slot == 1)
        def _():
            tiles4(job3, z == 1)
            tiles4(job2, jnp.logical_and(left2, z == 1))

        pl.when(slot == 2)(lambda: tiles4(job3, z == 2))

        @pl.when(slot == 3)
        def _():
            halo_up_wait(7, s.G0.at[pl.ds(256, 128)])
            lax.fori_loop(16, 24, shift_one, 0)
            tiles4(job3, z == 3)

        @pl.when(jnp.logical_and(slot == 3, c == 1))
        def _():
            for hf in range(2):
                plane_second(1, hf)

        pl.when(jnp.logical_and(slot >= 3, slot < 5))(lambda: back_conv(slot - 3, 1))

        @pl.when(jnp.logical_and(slot == 4, c == 1))
        def _():
            for hf in range(2):
                plane_got(1, hf, 0)
                plane_got(1, hf, 2)
            tiles4(job2, jnp.logical_and(late2, z % 3 == 0))

        return 0

    def job0(q, here):
        chain(0, q, lambda q: own_down(0, q), put_down, here)

    def job1(q, here):
        chain(1, q, lambda q: own_down(1, q), put_down, here)

    def tap8(q, here):
        chain(2, q, lambda q: own_down(2, q), put_down, here)

    def job2(q, here):
        chain(2, q, lambda q: own_plane(s.st2, s.pr2, q), put_tile, here)

    def job3(q, here):
        chain(3, q, lambda q: own_plane(st3, s.pr3, q), put_tile, here)

    def tiles4(job, here):
        def body(q, _):
            job(q, here)
            return 0

        @pl.when(here)
        def _():
            lax.fori_loop(0, 4, body, 0)

    lax.fori_loop(0, 6, step, 0)
    tiles4(job1, z == 1)
    tiles4(job0, z == 0)
    tiles4(job2, jnp.logical_and(late2, z == 1))
    tiles4(job2, jnp.logical_and(has_plane2, z == 2))
    tiles4(tap8, jnp.logical_and(is_tap8, z == 2))
    store(s.wgo, wg_ref)
    for i in range(4):
        store(s.inraw.at[i], ig_ref.at[:, i])

    for q in range(4):
        for zp in range(4):
            chain_drain(zp, q)
        for j in (1, 2, 3):
            g_direct(q, j).wait_send()
        for j in range(4):
            g_forward(q, j).wait_send()
    for job in range(2):
        for hf in range(2):
            for m in range(3):
                plane_sent(job, hf, m)
    for cp in outs:
        cp.wait()


def hand_over(n, *refs):
    ins, outs, held = refs[:n], refs[n : 2 * n], refs[2 * n : 3 * n]
    sems = refs[3 * n]
    got = [pltpu.make_async_copy(ins[i], held[i], sems.at[0, i]) for i in range(n)]
    put = [pltpu.make_async_copy(held[i], outs[i], sems.at[1, i]) for i in range(n)]
    for cp in got:
        cp.start()
    for i in range(n):
        got[i].wait()
        put[i].start()
    for cp in put:
        cp.wait()


def fused_step(
    inputs, counts, down_weight, left_weight, right_weight, reduce_weight, spread_weight,
    norm_gains, norm_biases, running_mean, running_var, section_cotangent, block_cotangent,
):
    table = scratch_table()
    names = tuple(table)
    sds = jax.ShapeDtypeStruct
    row = (1, 3072)
    vmem = pl.BlockSpec(memory_space=pltpu.VMEM)
    smem = pl.BlockSpec(memory_space=pltpu.SMEM)
    hbm = pl.BlockSpec(memory_space=pl.ANY)
    outs = pl.pallas_call(
        functools.partial(fused_kernel, names, 13, 8),
        out_shape=(
            sds((8, 2, 16, 1024), BF),
            sds((8, 2, 16, 512), BF),
            sds((8, 4, 32, 512), BF),
            sds((2048, 128), F32),
            sds(row, F32),
            sds(row, F32),
            sds(row, F32),
            sds(row, F32),
        ),
        in_specs=[hbm, smem, hbm, hbm, hbm, hbm, hbm, vmem, vmem, vmem, vmem, hbm, hbm],
        out_specs=(hbm, hbm, hbm, hbm, vmem, vmem, vmem, vmem),
        scratch_shapes=list(table.values()),
        compiler_params=pltpu.CompilerParams(
            collective_id=0, has_side_effects=True, vmem_limit_bytes=64 * 2**20 - 2**16
        ),
        cost_estimate=pl.CostEstimate(flops=13 * 10**9, bytes_accessed=21 * 10**6, transcendentals=10**6),
    )(
        inputs, counts, down_weight.reshape((9,) + down_weight.shape[2:]), left_weight, right_weight,
        reduce_weight, spread_weight.reshape((9,) + spread_weight.shape[2:]),
        norm_gains.reshape(row), norm_biases.reshape(row), running_mean.reshape(row), running_var.reshape(row),
        section_cotangent, block_cotangent,
    )
    n = len(outs)
    so, bo, ig, wg, gg, bg, nm, nv = pl.pallas_call(
        functools.partial(hand_over, n),
        out_shape=tuple(sds(o.shape, o.dtype) for o in outs),
        in_specs=[hbm] * n,
        out_specs=(hbm,) * n,
        scratch_shapes=[pltpu.VMEM(o.shape, o.dtype) for o in outs] + [pltpu.SemaphoreType.DMA((2, n))],
        cost_estimate=pl.CostEstimate(flops=0, bytes_accessed=6 * 10**6, transcendentals=0),
    )(*outs)
    return (so, bo, ig, wg.reshape(-1), gg.reshape(-1), bg.reshape(-1), nm.reshape(-1), nv.reshape(-1))


def fits_fused(mesh):
    return dict(mesh.shape) == {"rows": 8, "batch": 4}


def solution(mesh):
    placed = (
        P("batch", "rows", None, None),
        P("batch"),
        P(),
        P(),
        P(),
        P(),
        P(),
        P(),
        P(),
        P(),
        P(),
        P("batch", "rows", None, None),
        P("batch", "rows", None, None),
    )
    return jax.shard_map(
        fused_step if fits_fused(mesh) else on_device,
        mesh=mesh,
        in_specs=placed,
        out_specs=(
            P("batch", "rows", None, None),
            P("batch", "rows", None, None),
            P("batch", "rows", None, None),
            P(("rows", "batch")),
            P(),
            P(),
            P(),
            P(),
        ),
        check_vma=False,
    )
```

```python
import functools
import types

import jax
import jax.numpy as jnp
from jax import lax
from jax.experimental import pallas as pl
from jax.experimental.pallas import tpu as pltpu
from jax.sharding import PartitionSpec as P

EPS = 1e-05
MOMENTUM = 0.1


def passed_along(block, axis, distance):
    devices = range(lax.axis_size(axis))
    route = [(i - distance, i) for i in devices if i - distance in devices]
    return lax.ppermute(block, axis, route)


def padded_2(block, sides, width):
    for axis, dim in sides:
        count = lax.axis_size(axis)
        forward = [(i, i + 1) for i in range(count - 1)]
        backward = [(target, source) for source, target in forward]
        low = lax.ppermute(
            lax.slice_in_dim(block, block.shape[dim] - width, None, axis=dim), axis, forward
        )
        high = lax.ppermute(lax.slice_in_dim(block, 0, width, axis=dim), axis, backward)
        block = jnp.concatenate([low, block, high], axis=dim)
    return block


def mish_act(values):
    return values * jnp.tanh(jax.nn.softplus(values))


def mish_back(before, grad_out):
    return jax.vjp(mish_act, before)[1](grad_out)[0]


def point_dot(left_op, right_op):
    return jnp.einsum("nhwc,cd->nhwd", left_op, right_op, preferred_element_type=jnp.float32)


def back_dot(left_op, right_op):
    return jnp.einsum("nhwd,cd->nhwc", left_op, right_op, preferred_element_type=jnp.float32)


def outer_dot(left_op, right_op):
    return jnp.einsum("nhwc,nhwd->cd", left_op, right_op, preferred_element_type=jnp.float32)


def norm_forward(values, valid_mask, gain_vec, offset, local_pixels):
    sum_first = jnp.sum(values * valid_mask, axis=(0, 1, 2))
    sum_second = jnp.sum(values * values * valid_mask, axis=(0, 1, 2))
    sum_first, sum_second, pixel_total = lax.psum(
        (sum_first, sum_second, local_pixels), ("rows", "batch")
    )
    batch_mean = sum_first / pixel_total
    batch_var = sum_second / pixel_total - batch_mean * batch_mean
    inv_std = lax.rsqrt(batch_var + EPS)
    normed = (values - batch_mean) * inv_std
    return (normed * gain_vec + offset, normed, inv_std, batch_mean, batch_var, pixel_total)


def norm_back(grad_out, normed, inv_std, gain_vec, valid_mask, pixel_total):
    bias_grad, gain_grad = lax.psum(
        (jnp.sum(grad_out, axis=(0, 1, 2)), jnp.sum(grad_out * normed, axis=(0, 1, 2))),
        ("rows", "batch"),
    )
    grad_in = (
        gain_vec
        * inv_std
        * (grad_out - valid_mask * (bias_grad + normed * gain_grad) / pixel_total)
    )
    return (grad_in, gain_grad, bias_grad)


def on_device(
    inputs,
    counts,
    down_weight,
    left_weight,
    right_weight,
    reduce_weight,
    spread_weight,
    norm_gains,
    norm_biases,
    running_mean,
    running_var,
    section_cotangent,
    block_cotangent,
):
    n_slots, row_in, col_in, in_width = inputs.shape
    row_out = row_in // 2
    col_out = col_in // 2
    section_width = down_weight.shape[3]
    branch_width = right_weight.shape[1]
    bounds = [
        0,
        section_width,
        section_width + branch_width,
        section_width + 2 * branch_width,
        section_width + 3 * branch_width,
        section_width + 4 * branch_width,
    ]
    valid_mask = (
        (jnp.arange(n_slots, dtype=jnp.int32) < counts[0])
        .astype(jnp.float32)
        .reshape(n_slots, 1, 1, 1)
    )
    local_pixels = jnp.sum(valid_mask) * float(row_out * col_out)

    def gain_at(bn_index):
        return norm_gains[bounds[bn_index] : bounds[bn_index + 1]]

    def norm_at(values, bn_index):
        return norm_forward(
            values,
            valid_mask,
            gain_at(bn_index),
            norm_biases[bounds[bn_index] : bounds[bn_index + 1]],
            local_pixels,
        )

    rim_row = passed_along(inputs[:, row_in - 1 :], "rows", 1)
    padded = jnp.pad(jnp.concatenate([rim_row, inputs], axis=1), ((0, 0), (0, 0), (1, 1), (0, 0)))
    taps = []
    first_out = jnp.zeros((n_slots, row_out, col_out, section_width), jnp.float32)
    for row_tap in range(3):
        for col_tap in range(3):
            window = padded[
                :, row_tap : row_tap + 2 * row_out : 2, col_tap : col_tap + 2 * col_out : 2, :
            ]
            taps.append(window)
            first_out = first_out + point_dot(window, down_weight[row_tap, col_tap])
    z_one, normed_one, inv_one, mean_one, var_one, pixel_total = norm_at(first_out, 0)
    act_one = mish_act(z_one).astype(jnp.bfloat16)
    z_left, normed_left, inv_left, mean_left, var_left, pixel_total = norm_at(
        point_dot(act_one, left_weight), 1
    )
    act_left = mish_act(z_left)
    z_right, normed_right, inv_right, mean_right, var_right, pixel_total = norm_at(
        point_dot(act_one, right_weight), 2
    )
    act_right = mish_act(z_right)
    right_low = act_right.astype(jnp.bfloat16)
    z_mid, normed_mid, inv_mid, mean_mid, var_mid, pixel_total = norm_at(
        point_dot(right_low, reduce_weight), 3
    )
    act_mid = mish_act(z_mid).astype(jnp.bfloat16)
    mid_halo = padded_2(act_mid, (("rows", 1),), 1)
    mid_pad = jnp.pad(mid_halo, ((0, 0), (0, 0), (1, 1), (0, 0)))
    fourth_out = jnp.zeros((n_slots, row_out, col_out, branch_width), jnp.float32)
    for row_tap in range(3):
        for col_tap in range(3):
            fourth_out = fourth_out + point_dot(
                mid_pad[:, row_tap : row_tap + row_out, col_tap : col_tap + col_out, :],
                spread_weight[row_tap, col_tap],
            )
    z_four, normed_four, inv_four, mean_four, var_four, pixel_total = norm_at(fourth_out, 4)
    act_four = mish_act(z_four)
    section_out = (valid_mask * jnp.concatenate([act_left, act_right], axis=3)).astype(jnp.bfloat16)
    block_out = (valid_mask * (act_right + act_four)).astype(jnp.bfloat16)
    section_grad = valid_mask * section_cotangent.astype(jnp.float32)
    block_grad = valid_mask * block_cotangent.astype(jnp.float32)
    grad_four, gain_four, bias_four = norm_back(
        mish_back(z_four, block_grad), normed_four, inv_four, gain_at(4), valid_mask, pixel_total
    )
    grad_four = grad_four.astype(jnp.bfloat16)
    grad_halo = padded_2(grad_four, (("rows", 1),), 1)
    grad_pad = jnp.pad(grad_halo, ((0, 0), (0, 0), (1, 1), (0, 0)))
    spread_taps = []
    mid_grad = jnp.zeros((n_slots, row_out, col_out, branch_width), jnp.float32)
    for row_tap in range(3):
        for col_tap in range(3):
            spread_taps.append(
                outer_dot(
                    mid_pad[:, row_tap : row_tap + row_out, col_tap : col_tap + col_out, :],
                    grad_four,
                )
            )
            mid_grad = mid_grad + back_dot(
                grad_pad[
                    :, 2 - row_tap : 2 - row_tap + row_out, 2 - col_tap : 2 - col_tap + col_out, :
                ],
                spread_weight[row_tap, col_tap],
            )
    spread_grad = jnp.stack(spread_taps).reshape(spread_weight.shape)
    grad_mid, gain_mid, bias_mid = norm_back(
        mish_back(z_mid, mid_grad), normed_mid, inv_mid, gain_at(3), valid_mask, pixel_total
    )
    grad_mid = grad_mid.astype(jnp.bfloat16)
    reduce_grad = outer_dot(right_low, grad_mid)
    right_total = section_grad[..., branch_width:] + block_grad + back_dot(grad_mid, reduce_weight)
    grad_right, gain_right, bias_right = norm_back(
        mish_back(z_right, right_total),
        normed_right,
        inv_right,
        gain_at(2),
        valid_mask,
        pixel_total,
    )
    grad_right = grad_right.astype(jnp.bfloat16)
    grad_left, gain_left, bias_left = norm_back(
        mish_back(z_left, section_grad[..., :branch_width]),
        normed_left,
        inv_left,
        gain_at(1),
        valid_mask,
        pixel_total,
    )
    grad_left = grad_left.astype(jnp.bfloat16)
    left_grad = outer_dot(act_one, grad_left)
    right_grad = outer_dot(act_one, grad_right)
    one_total = back_dot(grad_left, left_weight) + back_dot(grad_right, right_weight)
    grad_one, gain_one, bias_one = norm_back(
        mish_back(z_one, one_total), normed_one, inv_one, gain_at(0), valid_mask, pixel_total
    )
    grad_one = grad_one.astype(jnp.bfloat16)
    down_taps = []
    spread_back = jnp.zeros(padded.shape, jnp.float32)
    for row_tap in range(3):
        for col_tap in range(3):
            down_taps.append(outer_dot(taps[row_tap * 3 + col_tap], grad_one))
            spread_back = spread_back.at[
                :, row_tap : row_tap + 2 * row_out : 2, col_tap : col_tap + 2 * col_out : 2, :
            ].add(back_dot(grad_one, down_weight[row_tap, col_tap]))
    down_grad = jnp.stack(down_taps).reshape(down_weight.shape)
    back_rim = passed_along(
        spread_back[:, 0:1, 1 : col_in + 1].astype(jnp.bfloat16), "rows", -1
    ).astype(jnp.float32)
    input_grad = spread_back[:, 1:, 1 : col_in + 1]
    input_grad = input_grad.at[:, row_in - 1 :].add(back_rim)
    flat_grads = jnp.concatenate(
        [
            down_grad.reshape(-1),
            left_grad.reshape(-1),
            right_grad.reshape(-1),
            reduce_grad.reshape(-1),
            spread_grad.reshape(-1),
        ]
    )
    row_share = lax.psum_scatter(
        flat_grads.astype(jnp.bfloat16), "rows", scatter_dimension=0, tiled=True
    )
    weight_share = lax.psum_scatter(row_share, "batch", scatter_dimension=0, tiled=True).astype(
        jnp.float32
    )
    gain_grads = jnp.concatenate([gain_one, gain_left, gain_right, gain_mid, gain_four])
    bias_grads = jnp.concatenate([bias_one, bias_left, bias_right, bias_mid, bias_four])
    means_all = jnp.concatenate([mean_one, mean_left, mean_right, mean_mid, mean_four])
    vars_all = jnp.concatenate([var_one, var_left, var_right, var_mid, var_four])
    new_mean = (1.0 - MOMENTUM) * running_mean + MOMENTUM * means_all
    new_var = (1.0 - MOMENTUM) * running_var + MOMENTUM * vars_all * (
        pixel_total / (pixel_total - 1.0)
    )
    return (
        section_out,
        block_out,
        input_grad.astype(jnp.bfloat16),
        weight_share,
        gain_grads,
        bias_grads,
        new_mean,
        new_var,
    )


MESHID = pl.DeviceIdType.MESH
BF = jnp.bfloat16
F32 = jnp.float32
NT = (((1,), (1,)), ((), ()))


def mm(lhs, rhs):
    return jnp.dot(lhs, rhs, preferred_element_type=F32)


def mm_nt(lhs, rhs):
    return lax.dot_general(lhs, rhs, NT, preferred_element_type=F32)


def mish_parts(z):
    e = jnp.exp(jnp.minimum(z, 20.0))
    n = e * (e + 2.0)
    d = 1.0 / (n + 2.0)
    return e, d, n * d


def mish_of(z):
    return z * mish_parts(z)[2]


def mish_slope(z):
    e, d, t = mish_parts(z)
    return t + 4.0 * z * (e * (1.0 + e)) * (d * d)


def al(i, m):
    return pl.multiple_of(i, m)


def scratch_table():
    v = pltpu.VMEM
    dma = pltpu.SemaphoreType.DMA
    table = dict(
        inraw=v((5, 8, 32, 512), BF),
        tmpc=v((8, 4, 40, 128), F32),
        pad=v((8, 32, 512), F32),
        X=v((2304, 512), BF),
        xst=v((5, 512, 512), BF),
        XG=v((3, 256, 2048), BF),
        wd=v((9, 512, 1024), BF),
        wl=v((1024, 512), BF),
        wr=v((1024, 512), BF),
        wm=v((512, 512), BF),
        ws=v((9, 512, 512), BF),
        sc=v((2, 8, 16, 1024), BF),
        bc=v((4, 8, 16, 512), BF),
        so=v((2, 8, 16, 1024), BF),
        bo=v((2, 8, 16, 512), BF),
        y1=v((256, 1024), F32),
        d1=v((256, 1024), F32),
        act1=v((256, 1024), BF),
        yl=v((256, 512), F32),
        yr=v((256, 512), F32),
        gl=v((256, 512), F32),
        dr=v((256, 512), F32),
        actr=v((256, 512), F32),
        rlow=v((256, 512), BF),
        ym=v((512, 512), F32),
        dm=v((256, 512), F32),
        y4=v((512, 512), F32),
        g4=v((512, 512), F32),
        gm=v((256, 512), BF),
        gr=v((256, 512), BF),
        glb=v((256, 512), BF),
        GA=v((512, 512), BF),
        GB=v((512, 512), BF),
        G4=v((512, 512), BF),
        J2X=v((4, 512, 512), BF),
        MT=v((4, 512, 512), BF),
        st2=v((4, 512, 512), BF),
        pr2=v((3, 512, 512), BF),
        pr3=v((3, 512, 512), BF),
        Gall=v((2048, 1024), BF),
        G0=v((384, 1024), BF),
        Gp=v((256 + 128, 1024), BF),
        igf=v((2, 512, 128), F32),
        zb=v((3, 4, 256, 256), BF),
        za=v((3, 4, 256, 256), BF),
        zs=v((4, 4, 256, 256), BF),
        wgo=v((2048, 128), F32),
        bn0=v((8, 1024), F32),
        bnl=v((8, 512), F32),
        bnr=v((8, 512), F32),
        bnm=v((8, 512), F32),
        bn4=v((8, 512), F32),
        tot=v((1, 1024), F32),
        ld=dma((32,)),
        ldo=dma((16,)),
        hs=dma((12,)),
        hr=dma((12,)),
        cs=dma((8,)),
        cr=dma((8,)),
        as_=dma((8,)),
        ar_=dma((8,)),
        xs=dma((3, 8)),
        xr=dma((3, 8)),
        bs=dma((12,)),
        br=dma((12,)),
        ps=dma((2, 2, 3)),
        pr=dma((2, 2, 3)),
        gs=dma((4, 3)),
        grs=dma((4, 3)),
        gfs=dma((4, 4)),
        gfr=dma((4, 4)),
        zus=dma((4, 8)),
        zur=dma((4, 8)),
        zds=dma((4, 8)),
        zdr=dma((4, 8)),
    )
    widths = AR_WIDTHS
    for k, w in enumerate(widths):
        table["ar_st%d" % k] = v((2, w), F32)
        table["ar_ct%d" % k] = v((2, w), F32)
        table["ar_ab%d" % k] = v((16, 2, w), F32)
    return table


AR_WIDTHS = (1152, 1024, 512, 1024, 512, 512, 512, 1024)


def fused_kernel(names, n_in, n_out, *refs):
    (in_ref, cnt_ref, wd_ref, wl_ref, wr_ref, wm_ref, ws_ref, gain_ref, bias_ref, rm_ref, rv_ref,
     sc_ref, bc_ref) = refs[:n_in]
    (so_ref, bo_ref, ig_ref, wg_ref, gg_ref, bg_ref, nm_ref, nv_ref) = refs[n_in : n_in + n_out]
    s = types.SimpleNamespace(**dict(zip(names, refs[n_in + n_out :])))
    st = [getattr(s, "ar_st%d" % k) for k in range(8)]
    ct = [getattr(s, "ar_ct%d" % k) for k in range(8)]
    ab = [getattr(s, "ar_ab%d" % k) for k in range(8)]

    r = lax.axis_index("rows")
    b = lax.axis_index("batch")
    z = r // 2
    c = r % 2
    y = b // 2
    x = b % 2
    chip = z * 4 + b
    sib = (r + 1 - 2 * c, b)
    own8 = c * 4 + b
    first = r == 0
    last = r == 7
    plane = [b, b + 1 - 2 * x, b + 2 - 4 * y, 3 - b]

    def remote(src, dst, ss, rs, dev):
        return pltpu.make_async_remote_copy(
            src_ref=src, dst_ref=dst, send_sem=ss, recv_sem=rs, device_id=dev, device_id_type=MESHID
        )

    def recv_wait(dst, rs):
        pltpu.make_async_copy(dst, dst, rs).wait()

    bar = pltpu.get_barrier_semaphore()
    for i in range(8):
        for j in range(4):
            if i or j:
                pl.semaphore_signal(
                    bar, inc=1, device_id=((r + i) % 8, (b + j) % 4), device_id_type=MESHID
                )

    loads = {}

    def load(name, src, dst):
        cp = pltpu.make_async_copy(src, dst, s.ld.at[len(loads)])
        cp.start()
        loads[name] = cp

    for i in range(4):
        load("in%d" % i, in_ref.at[:, i], s.inraw.at[1 + i])
    for t in (3, 4, 5, 6, 7, 8, 0, 1, 2):
        load("wd%d" % t, wd_ref.at[t], s.wd.at[t])
    load("wl", wl_ref, s.wl)
    load("wr", wr_ref, s.wr)
    load("wm", wm_ref, s.wm)
    for i in range(2):
        load("sc%d" % i, sc_ref.at[:, i], s.sc.at[i])
        load("bc%d" % i, bc_ref.at[:, i], s.bc.at[1 + i])
    for i in range(3):
        load("ws%d" % i, ws_ref.at[pl.ds(3 * i, 3)], s.ws.at[pl.ds(3 * i, 3)])

    for n in range(8):
        for q in range(4):
            s.tmpc[n, q, 0:8, :] = jnp.zeros((8, 128), F32)
        s.pad[n, 0:8, :] = jnp.zeros((8, 512), F32)
        s.pad[n, 24:32, :] = jnp.zeros((8, 512), F32)

    @pl.when(first)
    def _():
        s.inraw[0] = jnp.zeros((8, 32, 512), BF)
        s.bc[0] = jnp.zeros((8, 16, 512), BF)
        s.ym[0:128, :] = jnp.zeros((128, 512), F32)
        s.y4[0:128, :] = jnp.zeros((128, 512), F32)

    @pl.when(last)
    def _():
        s.bc[3] = jnp.zeros((8, 16, 512), BF)
        s.ym[384:512, :] = jnp.zeros((128, 512), F32)
        s.y4[384:512, :] = jnp.zeros((128, 512), F32)
        s.G0[256:384, :] = jnp.zeros((128, 1024), BF)

    nxt = (r + 1, b)
    prv = (r - 1, b)

    def halo_down(k, src, dst):
        @pl.when(r < 7)
        def _():
            remote(src, dst, s.hs.at[k], s.hr.at[k], nxt).start()

    def halo_up(k, src, dst):
        @pl.when(r > 0)
        def _():
            remote(src, dst, s.hs.at[k], s.hr.at[k], prv).start()

    def halo_down_wait(k, dst):
        @pl.when(r < 7)
        def _():
            pltpu.make_async_copy(dst, dst, s.hs.at[k]).wait()

        @pl.when(r > 0)
        def _():
            recv_wait(dst, s.hr.at[k])

    def halo_up_wait(k, dst):
        @pl.when(r > 0)
        def _():
            pltpu.make_async_copy(dst, dst, s.hs.at[k]).wait()

        @pl.when(r < 7)
        def _():
            recv_wait(dst, s.hr.at[k])

    count = cnt_ref[0]
    vs = [(jnp.int32(n) < count).astype(F32) for n in range(8)]

    def ar_send(k):
        cp = remote(st[k], ct[k], s.cs.at[k], s.cr.at[k], sib)
        cp.start()
        cp.wait()
        ab[k][chip] = st[k][...] + ct[k][...]
        for j in range(1, 16):
            dev = (((z + j // 4) % 4) * 2 + c, (b + j % 4) % 4)
            remote(ab[k].at[chip], ab[k].at[chip], s.as_.at[k], s.ar_.at[k], dev).start()

    def ar_recv(k):
        part = ab[k].at[pl.ds(0, 15)]
        pltpu.make_async_copy(part, part, s.ar_.at[k]).wait()
        pltpu.make_async_copy(part, part, s.as_.at[k]).wait()
        out = ab[k][0]
        for j in range(1, 16):
            out = out + ab[k][j]
        return out

    def colstats(acc, k, col, width):
        a = acc.reshape(2, 8, 16, width)
        t1 = jnp.zeros((16, width), F32)
        t2 = jnp.zeros((16, width), F32)
        for n in range(8):
            p = a[0, n]
            q = a[1, n]
            t1 = t1 + (p + q) * vs[n]
            t2 = t2 + (p * p + q * q) * vs[n]
        st[k][0:1, pl.ds(col, width)] = jnp.sum(t1, axis=0, keepdims=True)
        st[k][1:2, pl.ds(col, width)] = jnp.sum(t2, axis=0, keepdims=True)

    def rows_loop(count_, body, init=0, unroll=2):
        return lax.fori_loop(0, count_, body, init, unroll=unroll)

    def rows16(i):
        return pl.ds(al(i * 16, 16), 16)

    def deinterleave(slot):
        targets = [(i, rr) for rr in range(2) for i in range(3) if i + 2 * rr == slot]

        def body(n, _):
            for q in range(4):
                s.tmpc[n, q, 8:40, :] = s.inraw[slot, n, :, q * 128 : q * 128 + 128].astype(F32)
            for j in range(3):
                for q in range(4):
                    val = s.tmpc[n, q, pl.ds(7 + j, 16, stride=2), :].astype(BF)
                    for i, rr in targets:
                        s.X[pl.ds(al((3 * i + j) * 256 + rr * 128 + n * 16, 16), 16), q * 128 : q * 128 + 128] = val
            return 0

        lax.fori_loop(0, 8, body, 0)

    for i in range(4):
        loads["in%d" % i].wait()
        deinterleave(1 + i)
    pl.semaphore_wait(bar, 31)
    halo_down(0, in_ref.at[:, 3], s.inraw.at[0])
    halo_down(1, bc_ref.at[:, 1], s.bc.at[0])
    halo_up(2, bc_ref.at[:, 0], s.bc.at[3])
    for t in (3, 4, 5, 6, 7, 8):
        loads["wd%d" % t].wait()

    def conv_a(n, _):
        cols = pl.ds(al(n * 256, 256), 256)
        acc = mm(s.X[3 * 256 : 4 * 256, :], s.wd[3, :, cols])
        for t in range(4, 9):
            acc = acc + mm(s.X[t * 256 : t * 256 + 256, :], s.wd[t, :, cols])
        s.y1[:, cols] = acc
        return 0

    lax.fori_loop(0, 4, conv_a, 0)
    halo_down_wait(0, s.inraw.at[0])
    deinterleave(0)
    for t in (0, 1, 2):
        loads["wd%d" % t].wait()
    st[0][:, 1024:1152] = jnp.zeros((2, 128), F32) + count.astype(F32) * 32.0

    def conv_b(n, _):
        col = al(n * 256, 256)
        cols = pl.ds(col, 256)
        acc = s.y1[:, cols]
        for t in range(3):
            acc = acc + mm(s.X[t * 256 : t * 256 + 256, :], s.wd[t, :, cols])
        s.y1[:, cols] = acc
        colstats(acc, 0, col, 256)
        return 0

    lax.fori_loop(0, 4, conv_b, 0)
    ar_send(0)

    def xpose(t, _):
        for q in range(4):
            s.xst[t // 2, q * 128 : q * 128 + 128, pl.ds(al((t % 2) * 256, 256), 256)] = s.X[
                pl.ds(al(t * 256, 256), 256), q * 128 : q * 128 + 128
            ].T
        return 0

    lax.fori_loop(0, 9, xpose, 0)

    def x_copy(dc, j, k):
        cc = (c + dc) % 2
        bb = plane[j]
        yy = bb // 2
        xx = bb % 2
        half = pl.ds(al(xx * 256, 256), 256)
        mine = pl.ds(al(own8 * 256, 256), 256)
        tap = 2 * cc + yy + 4 * k if k < 2 else 8
        src = s.xst.at[tap // 2, half, pl.ds(al((tap % 2) * 256, 256), 256)]
        dst = s.XG.at[k, :, mine]
        idx = dc * 4 + j
        if dc == 0 and j == 0:
            return pltpu.make_async_copy(src, dst, s.xs.at[k, idx])
        return remote(src, dst, s.xs.at[k, idx], s.xr.at[k, idx], (z * 2 + cc, bb))

    def x_when(dc, j, k, do):
        if k < 2:
            do()
        else:
            pl.when(jnp.logical_and((c + dc) % 2 == 0, plane[j] // 2 == 0))(do)

    def x_start(js, ks):
        for k in ks:
            for dc in range(2):
                for j in js:
                    x_when(dc, j, k, lambda: x_copy(dc, j, k).start())

    x_start((1, 2), (0,))
    x_start((0,), (0, 1, 2))

    def norm_params(k, res, lo, bn, width):
        g = gain_ref[0:1, pl.ds(lo, width)]
        o = bias_ref[0:1, pl.ds(lo, width)]
        inv_t = s.tot[0:1, 0:width]
        mean = res[0:1] * inv_t
        var = res[1:2] * inv_t - mean * mean
        inv = lax.rsqrt(var + EPS)
        a = g * inv
        bn[0:1, :] = a
        bn[1:2, :] = o - mean * a
        bn[2:3, :] = inv
        bn[3:4, :] = -mean * inv
        nm_ref[0:1, pl.ds(lo, width)] = (1.0 - MOMENTUM) * rm_ref[0:1, pl.ds(lo, width)] + MOMENTUM * mean
        t = 1.0 / inv_t
        nv_ref[0:1, pl.ds(lo, width)] = (1.0 - MOMENTUM) * rv_ref[0:1, pl.ds(lo, width)] + MOMENTUM * var * (
            t / (t - 1.0)
        )

    res = ar_recv(0)
    s.tot[0:1, :] = jnp.broadcast_to(1.0 / res[0:1, 1024:1025], (1, 1024))
    norm_params(0, res[:, 0:1024], 0, s.bn0, 1024)

    def act_one(i, _):
        zv = s.y1[rows16(i), :] * s.bn0[0:1, :] + s.bn0[1:2, :]
        s.act1[rows16(i), :] = mish_of(zv).astype(BF)
        return 0

    rows_loop(16, act_one)
    loads["wl"].wait()
    loads["wr"].wait()

    for h in range(2):
        cols = pl.ds(h * 256, 256)
        acc = mm(s.act1[...], s.wl[:, cols])
        s.yl[:, cols] = acc
        colstats(acc, 1, h * 256, 256)
        acc = mm(s.act1[...], s.wr[:, cols])
        s.yr[:, cols] = acc
        colstats(acc, 1, 512 + h * 256, 256)
    ar_send(1)
    x_start((1, 2), (1,))

    def slope_one(i, _):
        zv = s.y1[rows16(i), :] * s.bn0[0:1, :] + s.bn0[1:2, :]
        s.d1[rows16(i), :] = mish_slope(zv)
        return 0

    rows_loop(16, slope_one)
    mycols = pl.ds(al(c * 256, 256), 256)

    def xpose_act(h, _):
        for q in range(4):
            blk = s.act1[:, pl.ds(al(h * 512 + q * 128, 128), 128)]
            s.J2X[2 - 2 * c + h, pl.ds(q * 128, 128), mycols] = blk.T
        return 0

    lax.fori_loop(0, 2, xpose_act, 0)
    pair = []

    def to_sib(src, dst):
        k = len(pair)
        cp = remote(src, dst, s.bs.at[k], s.br.at[k], sib)
        pair.append(cp)
        return cp

    cp_act = to_sib(s.J2X.at[pl.ds(2 - 2 * c, 2), :, mycols], s.J2X.at[pl.ds(2 * c, 2), :, mycols])
    cp_act.start()

    res = ar_recv(1)
    norm_params(1, res[:, 0:512], 1024, s.bnl, 512)
    norm_params(2, res[:, 512:1024], 1536, s.bnr, 512)

    def act_right(i, _):
        zv = s.yr[rows16(i), :] * s.bnr[0:1, :] + s.bnr[1:2, :]
        e, d, t = mish_parts(zv)
        a = zv * t
        s.actr[rows16(i), :] = a
        s.rlow[rows16(i), :] = a.astype(BF)
        s.dr[rows16(i), :] = t + 4.0 * zv * (e * (1.0 + e)) * (d * d)
        return 0

    rows_loop(16, act_right)
    loads["wm"].wait()
    for h in range(2):
        cols = pl.ds(h * 256, 256)
        acc = mm(s.rlow[...], s.wm[:, cols])
        s.ym[128:384, cols] = acc
        colstats(acc, 2, h * 256, 256)
    ar_send(2)
    halo_down(3, s.ym.at[pl.ds(256, 128)], s.ym.at[pl.ds(0, 128)])
    halo_up(4, s.ym.at[pl.ds(128, 128)], s.ym.at[pl.ds(384, 128)])
    x_start((3,), (0,))

    loads["sc0"].wait()
    loads["sc1"].wait()

    def valid_at(i):
        return ((i % 8) < count).astype(F32)

    def left_branch(i, carry):
        t1, t2 = carry
        v = valid_at(i)
        yv = s.yl[rows16(i), :]
        zv = yv * s.bnl[0:1, :] + s.bnl[1:2, :]
        e, d, t = mish_parts(zv)
        s.so[i // 8, i % 8, :, 0:512] = (zv * t * v).astype(BF)
        s.so[i // 8, i % 8, :, 512:1024] = (s.actr[rows16(i), :] * v).astype(BF)
        gz = (t + 4.0 * zv * (e * (1.0 + e)) * (d * d)) * (s.sc[i // 8, i % 8, :, 0:512].astype(F32) * v)
        s.gl[rows16(i), :] = gz
        gx = gz * (yv * s.bnl[2:3, :] + s.bnl[3:4, :])
        return t1 + gz, t2 + gx

    zero16 = jnp.zeros((16, 512), F32)
    t1, t2 = rows_loop(16, left_branch, (zero16, zero16), unroll=1)
    st[3][0:1, 512:1024] = jnp.sum(t1, axis=0, keepdims=True)
    st[3][1:2, 512:1024] = jnp.sum(t2, axis=0, keepdims=True)
    outs = []

    def store(src, dst):
        cp = pltpu.make_async_copy(src, dst, s.ldo.at[len(outs)])
        cp.start()
        outs.append(cp)

    for i in range(2):
        store(s.so.at[i], so_ref.at[:, i])
    for q in range(4):
        s.J2X[2 * c, pl.ds(q * 128, 128), mycols] = s.rlow[:, q * 128 : q * 128 + 128].T
    cp_low = to_sib(s.J2X.at[0, :, mycols], s.J2X.at[2, :, mycols])

    @pl.when(c == 0)
    def _():
        cp_low.start()

    res = ar_recv(2)
    norm_params(3, res, 2048, s.bnm, 512)
    halo_down_wait(3, s.ym.at[pl.ds(0, 128)])
    halo_up_wait(4, s.ym.at[pl.ds(384, 128)])

    def edge_at(i):
        lo = jnp.logical_and(i < 8, first)
        hi = jnp.logical_and(i >= 24, last)
        return 1.0 - jnp.logical_or(lo, hi).astype(F32)

    def windows(i, val):
        n = i % 8
        s.pad[n, 8:24, :] = val
        for k in range(3):
            rows = pl.ds(al(k * 512 + i * 16, 16), 16)
            s.X[rows, :] = (val if k == 1 else s.pad[n, 7 + k : 23 + k, :]).astype(BF)

    def act_mid(i, _):
        zv = s.ym[rows16(i), :] * s.bnm[0:1, :] + s.bnm[1:2, :]
        windows(i, mish_of(zv) * edge_at(i))
        return 0

    rows_loop(32, act_mid)
    for i in range(3):
        loads["ws%d" % i].wait()

    def conv_four(h, _):
        col = al(h * 256, 256)
        cols = pl.ds(col, 256)
        acc = None
        for t in range(9):
            part = mm(s.X[pl.ds((t % 3) * 512 + (t // 3) * 128, 256), :], s.ws[t, :, cols])
            acc = part if acc is None else acc + part
        s.y4[pl.ds(128, 256), cols] = acc
        colstats(acc, 3, col, 256)
        return 0

    lax.fori_loop(0, 2, conv_four, 0)
    ar_send(3)
    halo_down(5, s.y4.at[pl.ds(256, 128)], s.y4.at[pl.ds(0, 128)])
    halo_up(6, s.y4.at[pl.ds(128, 128)], s.y4.at[pl.ds(384, 128)])
    x_start((3,), (1,))

    def slope_mid(i, _):
        zv = s.ym[pl.ds(al(128 + i * 16, 16), 16), :] * s.bnm[0:1, :] + s.bnm[1:2, :]
        s.dm[rows16(i), :] = mish_slope(zv)
        return 0

    rows_loop(16, slope_mid)

    def window_t(tap, dst, k):
        base = pl.ds(al((tap % 3) * 512 + (tap // 3) * 128, 128), 256)
        for q in range(4):
            dst[k, pl.ds(q * 128, 128), mycols] = s.X[base, q * 128 : q * 128 + 128].T

    def xpose_mid(k, _):
        window_t(1 + 4 * c + k, s.MT, k)
        window_t(5 - 4 * c + k, s.st2, k)
        return 0

    lax.fori_loop(0, 4, xpose_mid, 0)
    window_t(0 * c, s.J2X, 1 + 2 * c)
    cp_mt = to_sib(s.st2.at[:, :, mycols], s.MT.at[:, :, mycols])
    cp_mt.start()
    cp_m0 = to_sib(s.J2X.at[1, :, mycols], s.J2X.at[3, :, mycols])

    @pl.when(c == 0)
    def _():
        cp_m0.start()

    loads["bc0"].wait()
    loads["bc1"].wait()
    halo_down_wait(1, s.bc.at[0])
    halo_up_wait(2, s.bc.at[3])

    def back_params(res, lo, bn, width):
        inv_t = s.tot[0:1, 0:width]
        bg_ref[0:1, pl.ds(lo, width)] = res[0:1]
        gg_ref[0:1, pl.ds(lo, width)] = res[1:2]
        bn[4:5, :] = res[0:1] * inv_t
        bn[5:6, :] = res[1:2] * inv_t

    def grad_of(gz, yv, bn, v):
        xh = yv * bn[2:3, :] + bn[3:4, :]
        return bn[0:1, :] * (gz - v * (bn[4:5, :] + xh * bn[5:6, :]))

    res = ar_recv(3)
    norm_params(4, res[:, 0:512], 2560, s.bn4, 512)
    back_params(res[:, 512:1024], 1024, s.bnl, 512)

    def norm_four(i, carry):
        t1, t2 = carry
        v = valid_at(i)
        rows = pl.ds(al(128 + i * 16, 16), 16)
        yv = s.y4[rows, :]
        zv = yv * s.bn4[0:1, :] + s.bn4[1:2, :]
        e, d, t = mish_parts(zv)
        s.bo[i // 8, i % 8] = ((zv * t + s.actr[rows16(i), :]) * v).astype(BF)
        gz = (t + 4.0 * zv * (e * (1.0 + e)) * (d * d)) * (s.bc[1 + i // 8, i % 8].astype(F32) * v)
        s.g4[rows, :] = gz
        gx = gz * (yv * s.bn4[2:3, :] + s.bn4[3:4, :])
        return t1 + gz, t2 + gx

    t1, t2 = rows_loop(16, norm_four, (zero16, zero16), unroll=1)
    st[4][0:1, :] = jnp.sum(t1, axis=0, keepdims=True)
    st[4][1:2, :] = jnp.sum(t2, axis=0, keepdims=True)
    ar_send(4)
    x_start((1, 2, 3), (2,))
    myrows = pl.ds(al(c * 256, 256), 256)
    st3 = s.xst

    def grad_left(i, _):
        val = grad_of(s.gl[rows16(i), :], s.yl[rows16(i), :], s.bnl, valid_at(i)).astype(BF)
        s.glb[rows16(i), :] = val
        s.GA[pl.ds(al(c * 256 + i * 16, 16), 16), :] = val
        return 0

    rows_loop(16, grad_left)
    cp_ga = to_sib(s.glb, s.GA.at[myrows])

    @pl.when(c == 1)
    def _():
        cp_ga.start()

    def both_waits(cp, sender):
        pl.when(c == sender)(cp.wait_send)
        pl.when(c != sender)(cp.wait_recv)

    def half_of(ref, k, hf):
        return ref.at[k, pl.ds(hf * 256, 256)]

    def owned(job, j):
        return True if job == 0 else jnp.logical_or(c == 1, plane[j] // 2 == 1)

    def when_owned(job, j, do):
        if job == 0:
            do()
        else:
            pl.when(owned(job, j))(do)

    def plane_copy(job, hf, m):
        stage, slots = ((st3, s.pr3), (s.st2, s.pr2))[job]
        near, far = ((1, 2), (2, 1))[hf]
        src = (near, 3, far)[m]
        to = (near, near, far)[m]
        cp = remote(
            half_of(stage, plane[src], hf), half_of(slots, m, hf), s.ps.at[job, hf, m], s.pr.at[job, hf, m],
            (r, plane[to]),
        )
        return cp, src, (0, far, 0)[m]

    def plane_start(job, hf, m):
        cp, src, _ = plane_copy(job, hf, m)
        when_owned(job, src, cp.start)

    def plane_got(job, hf, m):
        cp, _, mine_at = plane_copy(job, hf, m)
        when_owned(job, mine_at, cp.wait_recv)

    def plane_sent(job, hf, m):
        cp, src, _ = plane_copy(job, hf, m)
        when_owned(job, src, cp.wait_send)

    def plane_second(job, hf):
        stage, slots = ((st3, s.pr3), (s.st2, s.pr2))[job]
        far = (2, 1)[hf]
        plane_got(job, hf, 1)

        def add():
            def body(i, _):
                rows = pl.ds(al(hf * 256 + i * 16, 16), 16)
                k = plane[far]
                stage[k, rows, :] = (stage[k, rows, :].astype(F32) + slots[1, rows, :].astype(F32)).astype(BF)
                return 0

            lax.fori_loop(0, 16, body, 0)

        when_owned(job, far, add)
        plane_start(job, hf, 2)

    def piece(lhs, k, rhs, stage):
        def body(i, _):
            rows = pl.ds(al((i // 2) * 256, 256), 256)
            cols = pl.ds(al((i % 2) * 256, 256), 256)
            stage[k, rows, cols] = mm(lhs[k, rows, :], rhs[:, cols]).astype(BF)
            return 0

        lax.fori_loop(0, 4, body, 0)

    cp_act.wait()
    cp_mt.wait()
    both_waits(cp_ga, 1)

    @pl.when(c == 0)
    def _():
        for k in (2, 3):
            piece(s.J2X, k, s.GA, s.st2)
        for m in (1, 0):
            for hf in range(2):
                plane_start(1, hf, m)

    for i in range(2):
        store(s.bo.at[i], bo_ref.at[:, i])

    halo_down_wait(5, s.y4.at[pl.ds(0, 128)])
    halo_up_wait(6, s.y4.at[pl.ds(384, 128)])

    def halo_four(k, _):
        i = k + 16 * (k // 8)
        v = valid_at(i)
        zv = s.y4[rows16(i), :] * s.bn4[0:1, :] + s.bn4[1:2, :]
        s.g4[rows16(i), :] = mish_slope(zv) * (s.bc[i // 8, i % 8].astype(F32) * v)
        return 0

    rows_loop(16, halo_four)

    res = ar_recv(4)
    back_params(res, 2560, s.bn4, 512)

    def grad_four(i, _):
        v = valid_at(i) * edge_at(i)
        windows(i, grad_of(s.g4[rows16(i), :], s.y4[rows16(i), :], s.bn4, v).astype(BF).astype(F32))
        return 0

    rows_loop(32, grad_four)

    def back_four(h, _):
        col = al(h * 256, 256)
        acc = None
        for t in range(9):
            part = mm_nt(
                s.X[pl.ds((2 - t % 3) * 512 + (2 - t // 3) * 128, 256), :], s.ws[t, pl.ds(col, 256), :]
            )
            acc = part if acc is None else acc + part
        cols = pl.ds(col, 256)
        gz = s.dm[:, cols] * acc
        s.dm[:, cols] = gz
        xh = s.ym[pl.ds(128, 256), cols] * s.bnm[2:3, cols] + s.bnm[3:4, cols]
        st[5][0:1, cols] = jnp.sum(gz, axis=0, keepdims=True)
        st[5][1:2, cols] = jnp.sum(gz * xh, axis=0, keepdims=True)
        return 0

    lax.fori_loop(0, 2, back_four, 0)
    ar_send(5)

    s.G4[myrows, :] = s.X[640:896, :]
    cp_g4 = to_sib(s.G4.at[myrows], s.G4.at[myrows])
    cp_g4.start()
    both_waits(cp_low, 0)
    both_waits(cp_m0, 0)
    cp_g4.wait()

    for k in range(3):
        for dc in range(2):
            for j in range(4):
                cp = x_copy(dc, j, k)
                x_when(dc, j, k, cp.wait if dc == 0 and j == 0 else cp.wait_send)

    def piece3(j):
        piece(s.MT, plane[j], s.G4, st3)

    piece3(3)
    for hf in range(2):
        plane_start(0, hf, 1)

    @pl.when(c == 0)
    def _():
        for hf in range(2):
            plane_second(1, hf)

    piece3(1)
    piece3(2)

    res = ar_recv(5)
    back_params(res, 2048, s.bnm, 512)

    def grad_mid(i, _):
        val = grad_of(
            s.dm[rows16(i), :], s.ym[pl.ds(al(128 + i * 16, 16), 16), :], s.bnm, valid_at(i)
        ).astype(BF)
        s.gm[rows16(i), :] = val
        s.GB[pl.ds(al(c * 256 + i * 16, 16), 16), :] = val
        return 0

    rows_loop(16, grad_mid)

    def back_mid(h, _):
        col = al(h * 256, 256)
        cols = pl.ds(col, 256)
        acc = mm_nt(s.gm[...], s.wm[cols, :]).reshape(2, 8, 16, 256)
        t1 = jnp.zeros((16, 256), F32)
        t2 = jnp.zeros((16, 256), F32)
        for rr in range(2):
            for n in range(8):
                rows = pl.ds(rr * 128 + n * 16, 16)
                cot = s.sc[rr, n, :, pl.ds(al(512 + h * 256, 256), 256)].astype(F32) + s.bc[
                    1 + rr, n, :, cols
                ].astype(F32)
                gz = s.dr[rows, cols] * (acc[rr, n] + cot * vs[n])
                s.dr[rows, cols] = gz
                t1 = t1 + gz
                t2 = t2 + gz * (s.yr[rows, cols] * s.bnr[2:3, cols] + s.bnr[3:4, cols])
        st[6][0:1, cols] = jnp.sum(t1, axis=0, keepdims=True)
        st[6][1:2, cols] = jnp.sum(t2, axis=0, keepdims=True)
        return 0

    lax.fori_loop(0, 2, back_mid, 0)
    ar_send(6)

    cp_gb = to_sib(s.gm, s.GB.at[myrows])

    @pl.when(c == 0)
    def _():
        cp_gb.start()

    for hf in range(2):
        plane_second(0, hf)
    piece3(0)
    both_waits(cp_gb, 0)

    @pl.when(c == 1)
    def _():
        piece(s.J2X, 3, s.G4, s.st2)
        piece(s.J2X, 2, s.GB, s.st2)

    res = ar_recv(6)
    back_params(res, 1536, s.bnr, 512)

    def grad_right(i, _):
        val = grad_of(s.dr[rows16(i), :], s.yr[rows16(i), :], s.bnr, valid_at(i)).astype(BF)
        s.gr[rows16(i), :] = val

        return 0

    rows_loop(16, grad_right)

    def back_one(h, _):
        cols = pl.ds(al(h * 256, 256), 256)
        acc = mm_nt(s.glb[...], s.wl[cols, :]) + mm_nt(s.gr[...], s.wr[cols, :])
        gz = s.d1[:, cols] * acc
        s.d1[:, cols] = gz
        xh = s.y1[:, cols] * s.bn0[2:3, cols] + s.bn0[3:4, cols]
        st[7][0:1, cols] = jnp.sum(gz, axis=0, keepdims=True)
        st[7][1:2, cols] = jnp.sum(gz * xh, axis=0, keepdims=True)
        return 0

    lax.fori_loop(0, 4, back_one, 0)
    ar_send(7)

    @pl.when(c == 1)
    def _():
        s.GA[myrows, :] = s.gr[...]

    cp_gr = to_sib(s.gr, s.GA.at[myrows])

    @pl.when(c == 0)
    def _():
        cp_gr.start()

    for hf in range(2):
        plane_start(0, hf, 0)
    both_waits(cp_gr, 0)

    @pl.when(c == 1)
    def _():
        for k in (0, 1):
            piece(s.J2X, k, s.GA, s.st2)

    res = ar_recv(7)
    back_params(res, 0, s.bn0, 1024)

    def grad_one(i, _):
        val = grad_of(s.d1[rows16(i), :], s.y1[rows16(i), :], s.bn0, valid_at(i))
        low = val.astype(BF)
        s.G0[rows16(i), :] = low
        s.Gall[pl.ds(al(own8 * 256 + i * 16, 16), 16), :] = low
        return 0

    rows_loop(16, grad_one)

    halo_up(7, s.G0.at[pl.ds(0, 128)], s.G0.at[pl.ds(256, 128)])

    def g_block(core, batch, q):
        return s.Gall.at[pl.ds(al((core * 4 + batch) * 256, 256), 256), pl.ds(al(q * 256, 256), 256)]

    def g_direct(q, j):
        blk = g_block(c, b, q)
        return remote(blk, blk, s.gs.at[q, j - 1], s.grs.at[q, j - 1], (r, plane[j]))

    def g_forward(q, j):
        blk = g_block(c, plane[j], q)
        return remote(blk, blk, s.gfs.at[q, j], s.gfr.at[q, j], sib)

    is_tap8 = jnp.logical_and(c == 0, y == 0)
    has_plane2 = jnp.logical_not(is_tap8)

    for q in range(4):
        for j in (1, 2, 3):
            g_direct(q, j).start()
        g_forward(q, 0).start()
        if q == 3:

            @pl.when(c == 1)
            def _():
                for m in (1, 0):
                    for hf in range(2):
                        plane_start(1, hf, m)


    for dc in range(2):
        for j in range(4):
            if dc or j:
                idx = dc * 4 + j
                src8 = ((c + dc) % 2) * 4 + plane[j]
                for k in range(3):
                    dst = s.XG.at[k, :, pl.ds(al(src8 * 256, 256), 256)]
                    x_got = lambda: recv_wait(dst, s.xr.at[k, idx])
                    if k < 2:
                        x_got()
                    else:
                        pl.when(is_tap8)(x_got)

    def half_tile(ref, k, q, h):
        return ref.at[k, q, pl.ds(h * 128, 128)]

    def chain(zp, q, own, put, here):
        @pl.when(jnp.logical_and(here, jnp.logical_and(q >= 0, q < 4)))
        def _():
            val = own(q)

            def below(h):
                got = half_tile(s.zb, zp - 1, q, h)
                recv_wait(got, s.zur.at[zp, 2 * q + h])
                return got[...].astype(F32)

            def above(h):
                got = half_tile(s.za, zp, q, h)
                recv_wait(got, s.zdr.at[zp, 2 * q + h])
                return got[...].astype(F32)

            def mine(h):
                return val[h * 128 : h * 128 + 128]

            def up(h, v):
                part = half_tile(s.zs, zp, q, h)
                part[...] = v.astype(BF)
                there = half_tile(s.zb, zp - 1, q, h)
                remote(part, there, s.zus.at[zp, 2 * q + h], s.zur.at[zp, 2 * q + h], (r + 2, b)).start()

            def down(h, v):
                part = half_tile(s.zs, zp, q, h)
                part[...] = v.astype(BF)
                there = half_tile(s.za, zp, q, h)
                remote(part, there, s.zds.at[zp, 2 * q + h], s.zdr.at[zp, 2 * q + h], (r - 2, b)).start()

            def each(do):
                def both():
                    for h in range(2):
                        do(h)

                return both

            if zp > 0:
                pl.when(z == 0)(each(lambda h: up(h, mine(h))))
            if zp > 1:
                pl.when(jnp.logical_and(z > 0, z < zp))(each(lambda h: up(h, mine(h) + below(h))))
            if zp < 3:
                pl.when(z == 3)(each(lambda h: down(h, mine(h))))
            if zp < 2:
                pl.when(jnp.logical_and(z > zp, z < 3))(each(lambda h: down(h, mine(h) + above(h))))

            @pl.when(z == zp)
            def _():
                for h in range(2):
                    v = mine(h)
                    if zp > 0:
                        v = v + below(h)
                    if zp < 3:
                        v = v + above(h)
                    put(q, h, v)

    def put_down(q, h, v):
        for i in range(2):
            s.wgo[pl.ds(h * 1024 + 2 * q + i, 128, stride=8), :] = v[:, i * 128 : i * 128 + 128]

    def put_tile(q, h, v):
        base = (q // 2) * 1024 + h * 512 + (q % 2) * 2
        for i in range(2):
            s.wgo[pl.ds(base + i, 128, stride=4), :] = v[:, i * 128 : i * 128 + 128]

    def chain_drain(zp, q):
        for h in range(2):
            part = half_tile(s.zs, zp, q, h)
            if zp > 0:

                @pl.when(z < zp)
                def _():
                    pltpu.make_async_copy(part, part, s.zus.at[zp, 2 * q + h]).wait()

            if zp < 3:

                @pl.when(z > zp)
                def _():
                    pltpu.make_async_copy(part, part, s.zds.at[zp, 2 * q + h]).wait()

    def own_plane(stage, slots, q):
        rows = pl.ds(al((q // 2) * 256, 256), 256)
        cols = pl.ds(al((q % 2) * 256, 256), 256)
        v = stage[b, rows, cols].astype(F32)
        for m in (0, 2):
            v = v + slots[m, rows, cols].astype(F32)
        return v

    def own_down(k, q):
        return mm(s.XG[k], s.Gall[:, pl.ds(al(q * 256, 256), 256)])

    def shift_one(i, _):
        n = i % 8
        for h in range(2):
            cols = pl.ds(h * 512, 512)
            s.pad[n, 8:24, :] = s.G0[rows16(i), cols].astype(F32)
            s.Gp[rows16(i), cols] = s.pad[n, 9:25, :].astype(BF)
        return 0

    lax.fori_loop(0, 16, shift_one, 0)

    def back_conv(h, par):
        ch = pl.ds(al(h * 256, 256), 256)

        def part(src, row, tap):
            return mm_nt(src[pl.ds(row * 128, 256), :], s.wd[tap, ch, :])

        if par == 0:
            even = part(s.G0, 0, 4)
            odd = part(s.G0, 0, 5) + part(s.Gp, 0, 3)
        else:
            even = part(s.G0, 0, 7) + part(s.G0, 1, 1)
            odd = (part(s.G0, 0, 8) + part(s.Gp, 0, 6)) + (part(s.G0, 1, 2) + part(s.Gp, 1, 0))
        for q in range(2):
            s.igf[q, pl.ds(0, 256, stride=2), :] = even[:, q * 128 : q * 128 + 128]
            s.igf[q, pl.ds(1, 256, stride=2), :] = odd[:, q * 128 : q * 128 + 128]
        for rr in range(2):
            for q in range(2):
                s.inraw[2 * rr + par, :, :, pl.ds(al(h * 256 + q * 128, 128), 128)] = (
                    s.igf[q, rr * 256 : rr * 256 + 256, :].astype(BF).reshape(8, 32, 128)
                )

    left2 = jnp.logical_and(c == 0, y == 1)
    late2 = c == 1

    def step(slot, _):
        pl.when(slot < 2)(lambda: back_conv(slot, 0))

        @pl.when(slot == 0)
        def _():
            for hf in range(2):
                plane_got(0, hf, 0)
                plane_got(0, hf, 2)
            run_tiles(job3, z == 0, 0, 4)

        @pl.when(jnp.logical_and(slot == 0, c == 0))
        def _():
            for hf in range(2):
                plane_got(1, hf, 0)
                plane_got(1, hf, 2)
            run_tiles(job2, jnp.logical_and(left2, z % 3 == 0), 0, 4)

        @pl.when(slot < 4)
        def _():
            for j in (1, 2, 3):
                recv_wait(g_block(c, plane[j], slot), s.grs.at[slot, j - 1])
                g_forward(slot, j).start()
            for j in range(4):
                recv_wait(g_block(1 - c, plane[j], slot), s.gfr.at[slot, j])

        job0(slot - (3 - z), z > 0)
        job1(slot - jnp.where(z == 0, 0, 4 - z), z != 1)
        tap8(slot - 2 * z, jnp.logical_and(is_tap8, z < 2))
        pl.when(jnp.logical_and(slot >= 1, slot < 3))(lambda: run_tiles(job3, z == 1, 2 * slot - 2, 2))
        pl.when(jnp.logical_and(slot >= 3, slot < 5))(lambda: run_tiles(job3, z == 2, 2 * slot - 6, 2))
        pl.when(slot == 3)(lambda: run_tiles(job2, jnp.logical_and(left2, z == 1), 0, 4))

        @pl.when(slot == 3)
        def _():
            halo_up_wait(7, s.G0.at[pl.ds(256, 128)])
            lax.fori_loop(16, 24, shift_one, 0)

        @pl.when(jnp.logical_and(slot == 3, c == 1))
        def _():
            for hf in range(2):
                plane_second(1, hf)

        pl.when(jnp.logical_and(slot >= 3, slot < 5))(lambda: back_conv(slot - 3, 1))

        @pl.when(jnp.logical_and(slot == 4, c == 1))
        def _():
            for hf in range(2):
                plane_got(1, hf, 0)
                plane_got(1, hf, 2)
            run_tiles(job2, jnp.logical_and(late2, z % 3 == 0), 0, 4)

        return 0

    def job0(q, here):
        chain(0, q, lambda q: own_down(0, q), put_down, here)

    def job1(q, here):
        chain(1, q, lambda q: own_down(1, q), put_down, here)

    def tap8(q, here):
        chain(2, q, lambda q: own_down(2, q), put_down, here)

    def job2(q, here):
        chain(2, q, lambda q: own_plane(s.st2, s.pr2, q), put_tile, here)

    def job3(q, here):
        chain(3, q, lambda q: own_plane(st3, s.pr3, q), put_tile, here)

    def run_tiles(job, here, first, n):
        def body(q, _):
            job(first + q, here)
            return 0

        @pl.when(here)
        def _():
            lax.fori_loop(0, n, body, 0)

    lax.fori_loop(0, 6, step, 0)
    run_tiles(tap8, jnp.logical_and(is_tap8, z == 3), 0, 4)
    run_tiles(job1, z == 1, 0, 4)
    run_tiles(job0, z == 0, 0, 4)
    run_tiles(job2, jnp.logical_and(late2, z == 1), 0, 4)
    run_tiles(job3, z == 3, 0, 4)
    run_tiles(job2, jnp.logical_and(has_plane2, z == 2), 0, 4)
    run_tiles(tap8, jnp.logical_and(is_tap8, z == 2), 0, 4)
    store(s.wgo, wg_ref)
    for i in range(4):
        store(s.inraw.at[i], ig_ref.at[:, i])

    for q in range(4):
        for zp in range(4):
            chain_drain(zp, q)
        for j in (1, 2, 3):
            g_direct(q, j).wait_send()
        for j in range(4):
            g_forward(q, j).wait_send()
    for job in range(2):
        for hf in range(2):
            for m in range(3):
                plane_sent(job, hf, m)
    for cp in outs:
        cp.wait()


def hand_over(n, *refs):
    ins, outs, held = refs[:n], refs[n : 2 * n], refs[2 * n : 3 * n]
    sems = refs[3 * n]
    got = [pltpu.make_async_copy(ins[i], held[i], sems.at[0, i]) for i in range(n)]
    put = [pltpu.make_async_copy(held[i], outs[i], sems.at[1, i]) for i in range(n)]
    for cp in got:
        cp.start()
    for i in range(n):
        got[i].wait()
        put[i].start()
    for cp in put:
        cp.wait()


def fused_step(
    inputs, counts, down_weight, left_weight, right_weight, reduce_weight, spread_weight,
    norm_gains, norm_biases, running_mean, running_var, section_cotangent, block_cotangent,
):
    table = scratch_table()
    names = tuple(table)
    sds = jax.ShapeDtypeStruct
    row = (1, 3072)
    vmem = pl.BlockSpec(memory_space=pltpu.VMEM)
    smem = pl.BlockSpec(memory_space=pltpu.SMEM)
    hbm = pl.BlockSpec(memory_space=pl.ANY)
    outs = pl.pallas_call(
        functools.partial(fused_kernel, names, 13, 8),
        out_shape=(
            sds((8, 2, 16, 1024), BF),
            sds((8, 2, 16, 512), BF),
            sds((8, 4, 32, 512), BF),
            sds((2048, 128), F32),
            sds(row, F32),
            sds(row, F32),
            sds(row, F32),
            sds(row, F32),
        ),
        in_specs=[hbm, smem, hbm, hbm, hbm, hbm, hbm, vmem, vmem, vmem, vmem, hbm, hbm],
        out_specs=(hbm, hbm, hbm, hbm, vmem, vmem, vmem, vmem),
        scratch_shapes=list(table.values()),
        compiler_params=pltpu.CompilerParams(
            collective_id=0, has_side_effects=True, vmem_limit_bytes=64 * 2**20 - 2**16
        ),
        cost_estimate=pl.CostEstimate(flops=13 * 10**9, bytes_accessed=21 * 10**6, transcendentals=10**6),
    )(
        inputs, counts, down_weight.reshape((9,) + down_weight.shape[2:]), left_weight, right_weight,
        reduce_weight, spread_weight.reshape((9,) + spread_weight.shape[2:]),
        norm_gains.reshape(row), norm_biases.reshape(row), running_mean.reshape(row), running_var.reshape(row),
        section_cotangent, block_cotangent,
    )
    n = len(outs)
    so, bo, ig, wg, gg, bg, nm, nv = pl.pallas_call(
        functools.partial(hand_over, n),
        out_shape=tuple(sds(o.shape, o.dtype) for o in outs),
        in_specs=[hbm] * n,
        out_specs=(hbm,) * n,
        scratch_shapes=[pltpu.VMEM(o.shape, o.dtype) for o in outs] + [pltpu.SemaphoreType.DMA((2, n))],
        cost_estimate=pl.CostEstimate(flops=0, bytes_accessed=6 * 10**6, transcendentals=0),
    )(*outs)
    return (so, bo, ig, wg.reshape(-1), gg.reshape(-1), bg.reshape(-1), nm.reshape(-1), nv.reshape(-1))


def fits_fused(mesh):
    return dict(mesh.shape) == {"rows": 8, "batch": 4}


def solution(mesh):
    placed = (
        P("batch", "rows", None, None),
        P("batch"),
        P(),
        P(),
        P(),
        P(),
        P(),
        P(),
        P(),
        P(),
        P(),
        P("batch", "rows", None, None),
        P("batch", "rows", None, None),
    )
    return jax.shard_map(
        fused_step if fits_fused(mesh) else on_device,
        mesh=mesh,
        in_specs=placed,
        out_specs=(
            P("batch", "rows", None, None),
            P("batch", "rows", None, None),
            P("batch", "rows", None, None),
            P(("rows", "batch")),
            P(),
            P(),
            P(),
            P(),
        ),
        check_vma=False,
    )
```

```python
import functools
import types

import jax
import jax.numpy as jnp
from jax import lax
from jax.experimental import pallas as pl
from jax.experimental.pallas import tpu as pltpu
from jax.sharding import PartitionSpec as P

EPS = 1e-05
MOMENTUM = 0.1


def passed_along(block, axis, distance):
    devices = range(lax.axis_size(axis))
    route = [(i - distance, i) for i in devices if i - distance in devices]
    return lax.ppermute(block, axis, route)


def padded_2(block, sides, width):
    for axis, dim in sides:
        count = lax.axis_size(axis)
        forward = [(i, i + 1) for i in range(count - 1)]
        backward = [(target, source) for source, target in forward]
        low = lax.ppermute(
            lax.slice_in_dim(block, block.shape[dim] - width, None, axis=dim), axis, forward
        )
        high = lax.ppermute(lax.slice_in_dim(block, 0, width, axis=dim), axis, backward)
        block = jnp.concatenate([low, block, high], axis=dim)
    return block


def mish_act(values):
    return values * jnp.tanh(jax.nn.softplus(values))


def mish_back(before, grad_out):
    return jax.vjp(mish_act, before)[1](grad_out)[0]


def point_dot(left_op, right_op):
    return jnp.einsum("nhwc,cd->nhwd", left_op, right_op, preferred_element_type=jnp.float32)


def back_dot(left_op, right_op):
    return jnp.einsum("nhwd,cd->nhwc", left_op, right_op, preferred_element_type=jnp.float32)


def outer_dot(left_op, right_op):
    return jnp.einsum("nhwc,nhwd->cd", left_op, right_op, preferred_element_type=jnp.float32)


def norm_forward(values, valid_mask, gain_vec, offset, local_pixels):
    sum_first = jnp.sum(values * valid_mask, axis=(0, 1, 2))
    sum_second = jnp.sum(values * values * valid_mask, axis=(0, 1, 2))
    sum_first, sum_second, pixel_total = lax.psum(
        (sum_first, sum_second, local_pixels), ("rows", "batch")
    )
    batch_mean = sum_first / pixel_total
    batch_var = sum_second / pixel_total - batch_mean * batch_mean
    inv_std = lax.rsqrt(batch_var + EPS)
    normed = (values - batch_mean) * inv_std
    return (normed * gain_vec + offset, normed, inv_std, batch_mean, batch_var, pixel_total)


def norm_back(grad_out, normed, inv_std, gain_vec, valid_mask, pixel_total):
    bias_grad, gain_grad = lax.psum(
        (jnp.sum(grad_out, axis=(0, 1, 2)), jnp.sum(grad_out * normed, axis=(0, 1, 2))),
        ("rows", "batch"),
    )
    grad_in = (
        gain_vec
        * inv_std
        * (grad_out - valid_mask * (bias_grad + normed * gain_grad) / pixel_total)
    )
    return (grad_in, gain_grad, bias_grad)


def on_device(
    inputs,
    counts,
    down_weight,
    left_weight,
    right_weight,
    reduce_weight,
    spread_weight,
    norm_gains,
    norm_biases,
    running_mean,
    running_var,
    section_cotangent,
    block_cotangent,
):
    n_slots, row_in, col_in, in_width = inputs.shape
    row_out = row_in // 2
    col_out = col_in // 2
    section_width = down_weight.shape[3]
    branch_width = right_weight.shape[1]
    bounds = [
        0,
        section_width,
        section_width + branch_width,
        section_width + 2 * branch_width,
        section_width + 3 * branch_width,
        section_width + 4 * branch_width,
    ]
    valid_mask = (
        (jnp.arange(n_slots, dtype=jnp.int32) < counts[0])
        .astype(jnp.float32)
        .reshape(n_slots, 1, 1, 1)
    )
    local_pixels = jnp.sum(valid_mask) * float(row_out * col_out)

    def gain_at(bn_index):
        return norm_gains[bounds[bn_index] : bounds[bn_index + 1]]

    def norm_at(values, bn_index):
        return norm_forward(
            values,
            valid_mask,
            gain_at(bn_index),
            norm_biases[bounds[bn_index] : bounds[bn_index + 1]],
            local_pixels,
        )

    rim_row = passed_along(inputs[:, row_in - 1 :], "rows", 1)
    padded = jnp.pad(jnp.concatenate([rim_row, inputs], axis=1), ((0, 0), (0, 0), (1, 1), (0, 0)))
    taps = []
    first_out = jnp.zeros((n_slots, row_out, col_out, section_width), jnp.float32)
    for row_tap in range(3):
        for col_tap in range(3):
            window = padded[
                :, row_tap : row_tap + 2 * row_out : 2, col_tap : col_tap + 2 * col_out : 2, :
            ]
            taps.append(window)
            first_out = first_out + point_dot(window, down_weight[row_tap, col_tap])
    z_one, normed_one, inv_one, mean_one, var_one, pixel_total = norm_at(first_out, 0)
    act_one = mish_act(z_one).astype(jnp.bfloat16)
    z_left, normed_left, inv_left, mean_left, var_left, pixel_total = norm_at(
        point_dot(act_one, left_weight), 1
    )
    act_left = mish_act(z_left)
    z_right, normed_right, inv_right, mean_right, var_right, pixel_total = norm_at(
        point_dot(act_one, right_weight), 2
    )
    act_right = mish_act(z_right)
    right_low = act_right.astype(jnp.bfloat16)
    z_mid, normed_mid, inv_mid, mean_mid, var_mid, pixel_total = norm_at(
        point_dot(right_low, reduce_weight), 3
    )
    act_mid = mish_act(z_mid).astype(jnp.bfloat16)
    mid_halo = padded_2(act_mid, (("rows", 1),), 1)
    mid_pad = jnp.pad(mid_halo, ((0, 0), (0, 0), (1, 1), (0, 0)))
    fourth_out = jnp.zeros((n_slots, row_out, col_out, branch_width), jnp.float32)
    for row_tap in range(3):
        for col_tap in range(3):
            fourth_out = fourth_out + point_dot(
                mid_pad[:, row_tap : row_tap + row_out, col_tap : col_tap + col_out, :],
                spread_weight[row_tap, col_tap],
            )
    z_four, normed_four, inv_four, mean_four, var_four, pixel_total = norm_at(fourth_out, 4)
    act_four = mish_act(z_four)
    section_out = (valid_mask * jnp.concatenate([act_left, act_right], axis=3)).astype(jnp.bfloat16)
    block_out = (valid_mask * (act_right + act_four)).astype(jnp.bfloat16)
    section_grad = valid_mask * section_cotangent.astype(jnp.float32)
    block_grad = valid_mask * block_cotangent.astype(jnp.float32)
    grad_four, gain_four, bias_four = norm_back(
        mish_back(z_four, block_grad), normed_four, inv_four, gain_at(4), valid_mask, pixel_total
    )
    grad_four = grad_four.astype(jnp.bfloat16)
    grad_halo = padded_2(grad_four, (("rows", 1),), 1)
    grad_pad = jnp.pad(grad_halo, ((0, 0), (0, 0), (1, 1), (0, 0)))
    spread_taps = []
    mid_grad = jnp.zeros((n_slots, row_out, col_out, branch_width), jnp.float32)
    for row_tap in range(3):
        for col_tap in range(3):
            spread_taps.append(
                outer_dot(
                    mid_pad[:, row_tap : row_tap + row_out, col_tap : col_tap + col_out, :],
                    grad_four,
                )
            )
            mid_grad = mid_grad + back_dot(
                grad_pad[
                    :, 2 - row_tap : 2 - row_tap + row_out, 2 - col_tap : 2 - col_tap + col_out, :
                ],
                spread_weight[row_tap, col_tap],
            )
    spread_grad = jnp.stack(spread_taps).reshape(spread_weight.shape)
    grad_mid, gain_mid, bias_mid = norm_back(
        mish_back(z_mid, mid_grad), normed_mid, inv_mid, gain_at(3), valid_mask, pixel_total
    )
    grad_mid = grad_mid.astype(jnp.bfloat16)
    reduce_grad = outer_dot(right_low, grad_mid)
    right_total = section_grad[..., branch_width:] + block_grad + back_dot(grad_mid, reduce_weight)
    grad_right, gain_right, bias_right = norm_back(
        mish_back(z_right, right_total),
        normed_right,
        inv_right,
        gain_at(2),
        valid_mask,
        pixel_total,
    )
    grad_right = grad_right.astype(jnp.bfloat16)
    grad_left, gain_left, bias_left = norm_back(
        mish_back(z_left, section_grad[..., :branch_width]),
        normed_left,
        inv_left,
        gain_at(1),
        valid_mask,
        pixel_total,
    )
    grad_left = grad_left.astype(jnp.bfloat16)
    left_grad = outer_dot(act_one, grad_left)
    right_grad = outer_dot(act_one, grad_right)
    one_total = back_dot(grad_left, left_weight) + back_dot(grad_right, right_weight)
    grad_one, gain_one, bias_one = norm_back(
        mish_back(z_one, one_total), normed_one, inv_one, gain_at(0), valid_mask, pixel_total
    )
    grad_one = grad_one.astype(jnp.bfloat16)
    down_taps = []
    spread_back = jnp.zeros(padded.shape, jnp.float32)
    for row_tap in range(3):
        for col_tap in range(3):
            down_taps.append(outer_dot(taps[row_tap * 3 + col_tap], grad_one))
            spread_back = spread_back.at[
                :, row_tap : row_tap + 2 * row_out : 2, col_tap : col_tap + 2 * col_out : 2, :
            ].add(back_dot(grad_one, down_weight[row_tap, col_tap]))
    down_grad = jnp.stack(down_taps).reshape(down_weight.shape)
    back_rim = passed_along(
        spread_back[:, 0:1, 1 : col_in + 1].astype(jnp.bfloat16), "rows", -1
    ).astype(jnp.float32)
    input_grad = spread_back[:, 1:, 1 : col_in + 1]
    input_grad = input_grad.at[:, row_in - 1 :].add(back_rim)
    flat_grads = jnp.concatenate(
        [
            down_grad.reshape(-1),
            left_grad.reshape(-1),
            right_grad.reshape(-1),
            reduce_grad.reshape(-1),
            spread_grad.reshape(-1),
        ]
    )
    row_share = lax.psum_scatter(
        flat_grads.astype(jnp.bfloat16), "rows", scatter_dimension=0, tiled=True
    )
    weight_share = lax.psum_scatter(row_share, "batch", scatter_dimension=0, tiled=True).astype(
        jnp.float32
    )
    gain_grads = jnp.concatenate([gain_one, gain_left, gain_right, gain_mid, gain_four])
    bias_grads = jnp.concatenate([bias_one, bias_left, bias_right, bias_mid, bias_four])
    means_all = jnp.concatenate([mean_one, mean_left, mean_right, mean_mid, mean_four])
    vars_all = jnp.concatenate([var_one, var_left, var_right, var_mid, var_four])
    new_mean = (1.0 - MOMENTUM) * running_mean + MOMENTUM * means_all
    new_var = (1.0 - MOMENTUM) * running_var + MOMENTUM * vars_all * (
        pixel_total / (pixel_total - 1.0)
    )
    return (
        section_out,
        block_out,
        input_grad.astype(jnp.bfloat16),
        weight_share,
        gain_grads,
        bias_grads,
        new_mean,
        new_var,
    )


MESHID = pl.DeviceIdType.MESH
BF = jnp.bfloat16
F32 = jnp.float32
NT = (((1,), (1,)), ((), ()))


def mm(lhs, rhs):
    return jnp.dot(lhs, rhs, preferred_element_type=F32)


def mm_nt(lhs, rhs):
    return lax.dot_general(lhs, rhs, NT, preferred_element_type=F32)


def mish_parts(z):
    e = jnp.exp(jnp.minimum(z, 20.0))
    n = e * (e + 2.0)
    d = 1.0 / (n + 2.0)
    return e, d, n * d


def mish_of(z):
    return z * mish_parts(z)[2]


def mish_slope(z):
    e, d, t = mish_parts(z)
    return t + 4.0 * z * (e * (1.0 + e)) * (d * d)


def al(i, m):
    return pl.multiple_of(i, m)


def scratch_table():
    v = pltpu.VMEM
    dma = pltpu.SemaphoreType.DMA
    table = dict(
        inraw=v((5, 8, 32, 512), BF),
        tmpc=v((8, 4, 40, 128), F32),
        pad=v((8, 32, 512), F32),
        X=v((2304, 512), BF),
        xst=v((5, 512, 512), BF),
        XG=v((3, 256, 2048), BF),
        wd=v((9, 512, 1024), BF),
        wl=v((1024, 512), BF),
        wr=v((1024, 512), BF),
        wm=v((512, 512), BF),
        ws=v((9, 512, 512), BF),
        sc=v((2, 8, 16, 1024), BF),
        bc=v((4, 8, 16, 512), BF),
        so=v((2, 8, 16, 1024), BF),
        bo=v((2, 8, 16, 512), BF),
        y1=v((256, 1024), F32),
        d1=v((256, 1024), F32),
        act1=v((256, 1024), BF),
        yl=v((256, 512), F32),
        yr=v((256, 512), F32),
        gl=v((256, 512), F32),
        dr=v((256, 512), F32),
        actr=v((256, 512), F32),
        rlow=v((256, 512), BF),
        ym=v((512, 512), F32),
        dm=v((256, 512), F32),
        y4=v((512, 512), F32),
        g4=v((512, 512), F32),
        gm=v((256, 512), BF),
        gr=v((256, 512), BF),
        glb=v((256, 512), BF),
        GA=v((512, 512), BF),
        GB=v((512, 512), BF),
        G4=v((512, 512), BF),
        J2X=v((4, 512, 512), BF),
        MT=v((4, 512, 512), BF),
        st2=v((4, 512, 512), BF),
        pr2=v((3, 512, 512), BF),
        pr3=v((3, 512, 512), BF),
        Gall=v((2048, 1024), BF),
        G0=v((384, 1024), BF),
        Gp=v((256 + 128, 1024), BF),
        igf=v((2, 512, 128), F32),
        zb=v((3, 4, 256, 256), BF),
        za=v((3, 4, 256, 256), BF),
        zs=v((4, 4, 256, 256), BF),
        wgo=v((2048, 128), F32),
        bn0=v((8, 1024), F32),
        bnl=v((8, 512), F32),
        bnr=v((8, 512), F32),
        bnm=v((8, 512), F32),
        bn4=v((8, 512), F32),
        tot=v((1, 1024), F32),
        ld=dma((32,)),
        ldo=dma((16,)),
        hs=dma((12,)),
        hr=dma((12,)),
        cs=dma((8,)),
        cr=dma((8,)),
        as_=dma((8,)),
        ar_=dma((8,)),
        xs=dma((3, 8)),
        xr=dma((3, 8)),
        bs=dma((12,)),
        br=dma((12,)),
        ps=dma((2, 2, 3)),
        pr=dma((2, 2, 3)),
        gs=dma((4, 3)),
        grs=dma((4, 3)),
        gfs=dma((4, 4)),
        gfr=dma((4, 4)),
        zus=dma((4, 8)),
        zur=dma((4, 8)),
        zds=dma((4, 8)),
        zdr=dma((4, 8)),
    )
    widths = AR_WIDTHS
    for k, w in enumerate(widths):
        table["ar_st%d" % k] = v((2, w), F32)
        table["ar_ct%d" % k] = v((2, w), F32)
        table["ar_ab%d" % k] = v((16, 2, w), F32)
    return table


AR_WIDTHS = (1152, 1024, 512, 1024, 512, 512, 512, 1024)


def fused_kernel(names, n_in, n_out, *refs):
    (in_ref, cnt_ref, wd_ref, wl_ref, wr_ref, wm_ref, ws_ref, gain_ref, bias_ref, rm_ref, rv_ref,
     sc_ref, bc_ref) = refs[:n_in]
    (so_ref, bo_ref, ig_ref, wg_ref, gg_ref, bg_ref, nm_ref, nv_ref) = refs[n_in : n_in + n_out]
    s = types.SimpleNamespace(**dict(zip(names, refs[n_in + n_out :])))
    st = [getattr(s, "ar_st%d" % k) for k in range(8)]
    ct = [getattr(s, "ar_ct%d" % k) for k in range(8)]
    ab = [getattr(s, "ar_ab%d" % k) for k in range(8)]

    r = lax.axis_index("rows")
    b = lax.axis_index("batch")
    z = r // 2
    c = r % 2
    y = b // 2
    x = b % 2
    chip = z * 4 + b
    sib = (r + 1 - 2 * c, b)
    own8 = c * 4 + b
    first = r == 0
    last = r == 7
    plane = [b, b + 1 - 2 * x, b + 2 - 4 * y, 3 - b]

    def remote(src, dst, ss, rs, dev):
        return pltpu.make_async_remote_copy(
            src_ref=src, dst_ref=dst, send_sem=ss, recv_sem=rs, device_id=dev, device_id_type=MESHID
        )

    def recv_wait(dst, rs):
        pltpu.make_async_copy(dst, dst, rs).wait()

    bar = pltpu.get_barrier_semaphore()
    for i in range(8):
        for j in range(4):
            if i or j:
                pl.semaphore_signal(
                    bar, inc=1, device_id=((r + i) % 8, (b + j) % 4), device_id_type=MESHID
                )

    loads = {}

    def load(name, src, dst):
        cp = pltpu.make_async_copy(src, dst, s.ld.at[len(loads)])
        cp.start()
        loads[name] = cp

    for i in range(4):
        load("in%d" % i, in_ref.at[:, i], s.inraw.at[1 + i])
    for t in (3, 4, 5, 6, 7, 8, 0, 1, 2):
        load("wd%d" % t, wd_ref.at[t], s.wd.at[t])
    load("wl", wl_ref, s.wl)
    load("wr", wr_ref, s.wr)
    load("wm", wm_ref, s.wm)
    for i in range(2):
        load("sc%d" % i, sc_ref.at[:, i], s.sc.at[i])
        load("bc%d" % i, bc_ref.at[:, i], s.bc.at[1 + i])
    for i in range(3):
        load("ws%d" % i, ws_ref.at[pl.ds(3 * i, 3)], s.ws.at[pl.ds(3 * i, 3)])

    for n in range(8):
        for q in range(4):
            s.tmpc[n, q, 0:8, :] = jnp.zeros((8, 128), F32)
        s.pad[n, 0:8, :] = jnp.zeros((8, 512), F32)
        s.pad[n, 24:32, :] = jnp.zeros((8, 512), F32)

    @pl.when(first)
    def _():
        s.inraw[0] = jnp.zeros((8, 32, 512), BF)
        s.bc[0] = jnp.zeros((8, 16, 512), BF)
        s.ym[0:128, :] = jnp.zeros((128, 512), F32)
        s.y4[0:128, :] = jnp.zeros((128, 512), F32)

    @pl.when(last)
    def _():
        s.bc[3] = jnp.zeros((8, 16, 512), BF)
        s.ym[384:512, :] = jnp.zeros((128, 512), F32)
        s.y4[384:512, :] = jnp.zeros((128, 512), F32)
        s.G0[256:384, :] = jnp.zeros((128, 1024), BF)

    nxt = (r + 1, b)
    prv = (r - 1, b)

    def halo_down(k, src, dst):
        @pl.when(r < 7)
        def _():
            remote(src, dst, s.hs.at[k], s.hr.at[k], nxt).start()

    def halo_up(k, src, dst):
        @pl.when(r > 0)
        def _():
            remote(src, dst, s.hs.at[k], s.hr.at[k], prv).start()

    def halo_down_wait(k, dst):
        @pl.when(r < 7)
        def _():
            pltpu.make_async_copy(dst, dst, s.hs.at[k]).wait()

        @pl.when(r > 0)
        def _():
            recv_wait(dst, s.hr.at[k])

    def halo_up_wait(k, dst):
        @pl.when(r > 0)
        def _():
            pltpu.make_async_copy(dst, dst, s.hs.at[k]).wait()

        @pl.when(r < 7)
        def _():
            recv_wait(dst, s.hr.at[k])

    count = cnt_ref[0]
    vs = [(jnp.int32(n) < count).astype(F32) for n in range(8)]

    def ar_send(k):
        cp = remote(st[k], ct[k], s.cs.at[k], s.cr.at[k], sib)
        cp.start()
        cp.wait()
        ab[k][chip] = st[k][...] + ct[k][...]
        for j in range(1, 16):
            dev = (((z + j // 4) % 4) * 2 + c, (b + j % 4) % 4)
            remote(ab[k].at[chip], ab[k].at[chip], s.as_.at[k], s.ar_.at[k], dev).start()

    def ar_recv(k):
        part = ab[k].at[pl.ds(0, 15)]
        pltpu.make_async_copy(part, part, s.ar_.at[k]).wait()
        pltpu.make_async_copy(part, part, s.as_.at[k]).wait()
        out = ab[k][0]
        for j in range(1, 16):
            out = out + ab[k][j]
        return out

    def colstats(acc, k, col, width):
        a = acc.reshape(2, 8, 16, width)
        t1 = jnp.zeros((16, width), F32)
        t2 = jnp.zeros((16, width), F32)
        for n in range(8):
            p = a[0, n]
            q = a[1, n]
            t1 = t1 + (p + q) * vs[n]
            t2 = t2 + (p * p + q * q) * vs[n]
        st[k][0:1, pl.ds(col, width)] = jnp.sum(t1, axis=0, keepdims=True)
        st[k][1:2, pl.ds(col, width)] = jnp.sum(t2, axis=0, keepdims=True)

    def rows_loop(count_, body, init=0, unroll=2):
        return lax.fori_loop(0, count_, body, init, unroll=unroll)

    def rows16(i):
        return pl.ds(al(i * 16, 16), 16)

    def deinterleave(slot):
        targets = [(i, rr) for rr in range(2) for i in range(3) if i + 2 * rr == slot]

        def body(n, _):
            for q in range(4):
                s.tmpc[n, q, 8:40, :] = s.inraw[slot, n, :, q * 128 : q * 128 + 128].astype(F32)
            for j in range(3):
                for q in range(4):
                    val = s.tmpc[n, q, pl.ds(7 + j, 16, stride=2), :].astype(BF)
                    for i, rr in targets:
                        s.X[pl.ds(al((3 * i + j) * 256 + rr * 128 + n * 16, 16), 16), q * 128 : q * 128 + 128] = val
            return 0

        lax.fori_loop(0, 8, body, 0)

    for i in range(4):
        loads["in%d" % i].wait()
        deinterleave(1 + i)
    pl.semaphore_wait(bar, 31)
    halo_down(0, in_ref.at[:, 3], s.inraw.at[0])
    halo_down(1, bc_ref.at[:, 1], s.bc.at[0])
    halo_up(2, bc_ref.at[:, 0], s.bc.at[3])
    for t in (3, 4, 5, 6, 7, 8):
        loads["wd%d" % t].wait()

    def conv_a(n, _):
        cols = pl.ds(al(n * 256, 256), 256)
        acc = mm(s.X[3 * 256 : 4 * 256, :], s.wd[3, :, cols])
        for t in range(4, 9):
            acc = acc + mm(s.X[t * 256 : t * 256 + 256, :], s.wd[t, :, cols])
        s.y1[:, cols] = acc
        return 0

    lax.fori_loop(0, 4, conv_a, 0)
    halo_down_wait(0, s.inraw.at[0])
    deinterleave(0)
    for t in (0, 1, 2):
        loads["wd%d" % t].wait()
    st[0][:, 1024:1152] = jnp.zeros((2, 128), F32) + count.astype(F32) * 32.0

    def conv_b(n, _):
        col = al(n * 256, 256)
        cols = pl.ds(col, 256)
        acc = s.y1[:, cols]
        for t in range(3):
            acc = acc + mm(s.X[t * 256 : t * 256 + 256, :], s.wd[t, :, cols])
        s.y1[:, cols] = acc
        colstats(acc, 0, col, 256)
        return 0

    lax.fori_loop(0, 4, conv_b, 0)
    ar_send(0)

    def xpose(t, _):
        for q in range(4):
            s.xst[t // 2, q * 128 : q * 128 + 128, pl.ds(al((t % 2) * 256, 256), 256)] = s.X[
                pl.ds(al(t * 256, 256), 256), q * 128 : q * 128 + 128
            ].T
        return 0

    lax.fori_loop(0, 9, xpose, 0)

    def x_copy(dc, j, k):
        cc = (c + dc) % 2
        bb = plane[j]
        yy = bb // 2
        xx = bb % 2
        half = pl.ds(al(xx * 256, 256), 256)
        mine = pl.ds(al(own8 * 256, 256), 256)
        tap = 2 * cc + yy + 4 * k if k < 2 else 8
        src = s.xst.at[tap // 2, half, pl.ds(al((tap % 2) * 256, 256), 256)]
        dst = s.XG.at[k, :, mine]
        idx = dc * 4 + j
        if dc == 0 and j == 0:
            return pltpu.make_async_copy(src, dst, s.xs.at[k, idx])
        return remote(src, dst, s.xs.at[k, idx], s.xr.at[k, idx], (z * 2 + cc, bb))

    def x_when(dc, j, k, do):
        if k < 2:
            do()
        else:
            pl.when(jnp.logical_and((c + dc) % 2 == 0, plane[j] // 2 == 0))(do)

    def x_start(js, ks):
        for k in ks:
            for dc in range(2):
                for j in js:
                    x_when(dc, j, k, lambda: x_copy(dc, j, k).start())

    x_start((1, 2), (0,))
    x_start((0,), (0, 1, 2))

    def norm_params(k, res, lo, bn, width):
        g = gain_ref[0:1, pl.ds(lo, width)]
        o = bias_ref[0:1, pl.ds(lo, width)]
        inv_t = s.tot[0:1, 0:width]
        mean = res[0:1] * inv_t
        var = res[1:2] * inv_t - mean * mean
        inv = lax.rsqrt(var + EPS)
        a = g * inv
        bn[0:1, :] = a
        bn[1:2, :] = o - mean * a
        bn[2:3, :] = inv
        bn[3:4, :] = -mean * inv
        nm_ref[0:1, pl.ds(lo, width)] = (1.0 - MOMENTUM) * rm_ref[0:1, pl.ds(lo, width)] + MOMENTUM * mean
        t = 1.0 / inv_t
        nv_ref[0:1, pl.ds(lo, width)] = (1.0 - MOMENTUM) * rv_ref[0:1, pl.ds(lo, width)] + MOMENTUM * var * (
            t / (t - 1.0)
        )

    res = ar_recv(0)
    s.tot[0:1, :] = jnp.broadcast_to(1.0 / res[0:1, 1024:1025], (1, 1024))
    norm_params(0, res[:, 0:1024], 0, s.bn0, 1024)

    def act_one(i, _):
        zv = s.y1[rows16(i), :] * s.bn0[0:1, :] + s.bn0[1:2, :]
        s.act1[rows16(i), :] = mish_of(zv).astype(BF)
        return 0

    rows_loop(16, act_one)
    loads["wl"].wait()
    loads["wr"].wait()

    for h in range(2):
        cols = pl.ds(h * 256, 256)
        acc = mm(s.act1[...], s.wl[:, cols])
        s.yl[:, cols] = acc
        colstats(acc, 1, h * 256, 256)
        acc = mm(s.act1[...], s.wr[:, cols])
        s.yr[:, cols] = acc
        colstats(acc, 1, 512 + h * 256, 256)
    ar_send(1)
    x_start((1, 2), (1,))

    def slope_one(i, _):
        zv = s.y1[rows16(i), :] * s.bn0[0:1, :] + s.bn0[1:2, :]
        s.d1[rows16(i), :] = mish_slope(zv)
        return 0

    rows_loop(16, slope_one)
    mycols = pl.ds(al(c * 256, 256), 256)

    def xpose_act(h, _):
        for q in range(4):
            blk = s.act1[:, pl.ds(al(h * 512 + q * 128, 128), 128)]
            s.J2X[2 - 2 * c + h, pl.ds(q * 128, 128), mycols] = blk.T
        return 0

    lax.fori_loop(0, 2, xpose_act, 0)
    pair = []

    def to_sib(src, dst):
        k = len(pair)
        cp = remote(src, dst, s.bs.at[k], s.br.at[k], sib)
        pair.append(cp)
        return cp

    cp_act = to_sib(s.J2X.at[pl.ds(2 - 2 * c, 2), :, mycols], s.J2X.at[pl.ds(2 * c, 2), :, mycols])
    cp_act.start()

    res = ar_recv(1)
    norm_params(1, res[:, 0:512], 1024, s.bnl, 512)
    norm_params(2, res[:, 512:1024], 1536, s.bnr, 512)

    def act_right(i, _):
        zv = s.yr[rows16(i), :] * s.bnr[0:1, :] + s.bnr[1:2, :]
        e, d, t = mish_parts(zv)
        a = zv * t
        s.actr[rows16(i), :] = a
        s.rlow[rows16(i), :] = a.astype(BF)
        s.dr[rows16(i), :] = t + 4.0 * zv * (e * (1.0 + e)) * (d * d)
        return 0

    rows_loop(16, act_right)
    loads["wm"].wait()
    for h in range(2):
        cols = pl.ds(h * 256, 256)
        acc = mm(s.rlow[...], s.wm[:, cols])
        s.ym[128:384, cols] = acc
        colstats(acc, 2, h * 256, 256)
    ar_send(2)
    halo_down(3, s.ym.at[pl.ds(256, 128)], s.ym.at[pl.ds(0, 128)])
    halo_up(4, s.ym.at[pl.ds(128, 128)], s.ym.at[pl.ds(384, 128)])
    x_start((3,), (0,))

    loads["sc0"].wait()
    loads["sc1"].wait()

    def valid_at(i):
        return ((i % 8) < count).astype(F32)

    def left_branch(i, carry):
        t1, t2 = carry
        v = valid_at(i)
        yv = s.yl[rows16(i), :]
        zv = yv * s.bnl[0:1, :] + s.bnl[1:2, :]
        e, d, t = mish_parts(zv)
        s.so[i // 8, i % 8, :, 0:512] = (zv * t * v).astype(BF)
        s.so[i // 8, i % 8, :, 512:1024] = (s.actr[rows16(i), :] * v).astype(BF)
        gz = (t + 4.0 * zv * (e * (1.0 + e)) * (d * d)) * (s.sc[i // 8, i % 8, :, 0:512].astype(F32) * v)
        s.gl[rows16(i), :] = gz
        gx = gz * (yv * s.bnl[2:3, :] + s.bnl[3:4, :])
        return t1 + gz, t2 + gx

    zero16 = jnp.zeros((16, 512), F32)
    t1, t2 = rows_loop(16, left_branch, (zero16, zero16), unroll=1)
    st[3][0:1, 512:1024] = jnp.sum(t1, axis=0, keepdims=True)
    st[3][1:2, 512:1024] = jnp.sum(t2, axis=0, keepdims=True)
    outs = []

    def store(src, dst):
        cp = pltpu.make_async_copy(src, dst, s.ldo.at[len(outs)])
        cp.start()
        outs.append(cp)

    for i in range(2):
        store(s.so.at[i], so_ref.at[:, i])
    for q in range(4):
        s.J2X[2 * c, pl.ds(q * 128, 128), mycols] = s.rlow[:, q * 128 : q * 128 + 128].T
    cp_low = to_sib(s.J2X.at[0, :, mycols], s.J2X.at[2, :, mycols])

    @pl.when(c == 0)
    def _():
        cp_low.start()

    res = ar_recv(2)
    norm_params(3, res, 2048, s.bnm, 512)
    halo_down_wait(3, s.ym.at[pl.ds(0, 128)])
    halo_up_wait(4, s.ym.at[pl.ds(384, 128)])

    def edge_at(i):
        lo = jnp.logical_and(i < 8, first)
        hi = jnp.logical_and(i >= 24, last)
        return 1.0 - jnp.logical_or(lo, hi).astype(F32)

    def windows(i, val):
        n = i % 8
        s.pad[n, 8:24, :] = val
        for k in range(3):
            rows = pl.ds(al(k * 512 + i * 16, 16), 16)
            s.X[rows, :] = (val if k == 1 else s.pad[n, 7 + k : 23 + k, :]).astype(BF)

    def act_mid(i, _):
        zv = s.ym[rows16(i), :] * s.bnm[0:1, :] + s.bnm[1:2, :]
        windows(i, mish_of(zv) * edge_at(i))
        return 0

    rows_loop(32, act_mid)
    for i in range(3):
        loads["ws%d" % i].wait()

    def conv_four(h, _):
        col = al(h * 256, 256)
        cols = pl.ds(col, 256)
        acc = None
        for t in range(9):
            part = mm(s.X[pl.ds((t % 3) * 512 + (t // 3) * 128, 256), :], s.ws[t, :, cols])
            acc = part if acc is None else acc + part
        s.y4[pl.ds(128, 256), cols] = acc
        colstats(acc, 3, col, 256)
        return 0

    lax.fori_loop(0, 2, conv_four, 0)
    ar_send(3)
    halo_down(5, s.y4.at[pl.ds(256, 128)], s.y4.at[pl.ds(0, 128)])
    halo_up(6, s.y4.at[pl.ds(128, 128)], s.y4.at[pl.ds(384, 128)])
    x_start((3,), (1,))

    def slope_mid(i, _):
        zv = s.ym[pl.ds(al(128 + i * 16, 16), 16), :] * s.bnm[0:1, :] + s.bnm[1:2, :]
        s.dm[rows16(i), :] = mish_slope(zv)
        return 0

    rows_loop(16, slope_mid)

    def window_t(tap, dst, k):
        base = pl.ds(al((tap % 3) * 512 + (tap // 3) * 128, 128), 256)
        for q in range(4):
            dst[k, pl.ds(q * 128, 128), mycols] = s.X[base, q * 128 : q * 128 + 128].T

    def xpose_mid(k, _):
        window_t(1 + 4 * c + k, s.MT, k)
        window_t(5 - 4 * c + k, s.st2, k)
        return 0

    lax.fori_loop(0, 4, xpose_mid, 0)
    window_t(0 * c, s.J2X, 1 + 2 * c)
    cp_mt = to_sib(s.st2.at[:, :, mycols], s.MT.at[:, :, mycols])
    cp_mt.start()
    cp_m0 = to_sib(s.J2X.at[1, :, mycols], s.J2X.at[3, :, mycols])

    @pl.when(c == 0)
    def _():
        cp_m0.start()

    loads["bc0"].wait()
    loads["bc1"].wait()
    halo_down_wait(1, s.bc.at[0])
    halo_up_wait(2, s.bc.at[3])

    def back_params(res, lo, bn, width):
        inv_t = s.tot[0:1, 0:width]
        bg_ref[0:1, pl.ds(lo, width)] = res[0:1]
        gg_ref[0:1, pl.ds(lo, width)] = res[1:2]
        bn[4:5, :] = res[0:1] * inv_t
        bn[5:6, :] = res[1:2] * inv_t

    def grad_of(gz, yv, bn, v):
        xh = yv * bn[2:3, :] + bn[3:4, :]
        return bn[0:1, :] * (gz - v * (bn[4:5, :] + xh * bn[5:6, :]))

    res = ar_recv(3)
    norm_params(4, res[:, 0:512], 2560, s.bn4, 512)
    back_params(res[:, 512:1024], 1024, s.bnl, 512)

    def norm_four(i, carry):
        t1, t2 = carry
        v = valid_at(i)
        rows = pl.ds(al(128 + i * 16, 16), 16)
        yv = s.y4[rows, :]
        zv = yv * s.bn4[0:1, :] + s.bn4[1:2, :]
        e, d, t = mish_parts(zv)
        s.bo[i // 8, i % 8] = ((zv * t + s.actr[rows16(i), :]) * v).astype(BF)
        gz = (t + 4.0 * zv * (e * (1.0 + e)) * (d * d)) * (s.bc[1 + i // 8, i % 8].astype(F32) * v)
        s.g4[rows, :] = gz
        gx = gz * (yv * s.bn4[2:3, :] + s.bn4[3:4, :])
        return t1 + gz, t2 + gx

    t1, t2 = rows_loop(16, norm_four, (zero16, zero16), unroll=1)
    st[4][0:1, :] = jnp.sum(t1, axis=0, keepdims=True)
    st[4][1:2, :] = jnp.sum(t2, axis=0, keepdims=True)
    ar_send(4)
    x_start((1, 2, 3), (2,))
    myrows = pl.ds(al(c * 256, 256), 256)
    st3 = s.xst

    def grad_left(i, _):
        val = grad_of(s.gl[rows16(i), :], s.yl[rows16(i), :], s.bnl, valid_at(i)).astype(BF)
        s.glb[rows16(i), :] = val
        s.GA[pl.ds(al(c * 256 + i * 16, 16), 16), :] = val
        return 0

    rows_loop(16, grad_left)
    cp_ga = to_sib(s.glb, s.GA.at[myrows])

    @pl.when(c == 1)
    def _():
        cp_ga.start()

    def both_waits(cp, sender):
        pl.when(c == sender)(cp.wait_send)
        pl.when(c != sender)(cp.wait_recv)

    def half_of(ref, k, hf):
        return ref.at[k, pl.ds(hf * 256, 256)]

    def owned(job, j):
        return True if job == 0 else jnp.logical_or(c == 1, plane[j] // 2 == 1)

    def when_owned(job, j, do):
        if job == 0:
            do()
        else:
            pl.when(owned(job, j))(do)

    def plane_copy(job, hf, m):
        stage, slots = ((st3, s.pr3), (s.st2, s.pr2))[job]
        near, far = ((1, 2), (2, 1))[hf]
        src = (near, 3, far)[m]
        to = (near, near, far)[m]
        cp = remote(
            half_of(stage, plane[src], hf), half_of(slots, m, hf), s.ps.at[job, hf, m], s.pr.at[job, hf, m],
            (r, plane[to]),
        )
        return cp, src, (0, far, 0)[m]

    def plane_start(job, hf, m):
        cp, src, _ = plane_copy(job, hf, m)
        when_owned(job, src, cp.start)

    def plane_got(job, hf, m):
        cp, _, mine_at = plane_copy(job, hf, m)
        when_owned(job, mine_at, cp.wait_recv)

    def plane_sent(job, hf, m):
        cp, src, _ = plane_copy(job, hf, m)
        when_owned(job, src, cp.wait_send)

    def plane_second(job, hf):
        stage, slots = ((st3, s.pr3), (s.st2, s.pr2))[job]
        far = (2, 1)[hf]
        plane_got(job, hf, 1)

        def add():
            def body(i, _):
                rows = pl.ds(al(hf * 256 + i * 16, 16), 16)
                k = plane[far]
                stage[k, rows, :] = (stage[k, rows, :].astype(F32) + slots[1, rows, :].astype(F32)).astype(BF)
                return 0

            lax.fori_loop(0, 16, body, 0)

        when_owned(job, far, add)
        plane_start(job, hf, 2)

    def piece(lhs, k, rhs, stage):
        def body(i, _):
            rows = pl.ds(al((i // 2) * 256, 256), 256)
            cols = pl.ds(al((i % 2) * 256, 256), 256)
            stage[k, rows, cols] = mm(lhs[k, rows, :], rhs[:, cols]).astype(BF)
            return 0

        lax.fori_loop(0, 4, body, 0)

    cp_act.wait()
    cp_mt.wait()
    both_waits(cp_ga, 1)

    @pl.when(c == 0)
    def _():
        for k in (2, 3):
            piece(s.J2X, k, s.GA, s.st2)
        for m in (1, 0):
            for hf in range(2):
                plane_start(1, hf, m)

    for i in range(2):
        store(s.bo.at[i], bo_ref.at[:, i])

    halo_down_wait(5, s.y4.at[pl.ds(0, 128)])
    halo_up_wait(6, s.y4.at[pl.ds(384, 128)])

    def halo_four(k, _):
        i = k + 16 * (k // 8)
        v = valid_at(i)
        zv = s.y4[rows16(i), :] * s.bn4[0:1, :] + s.bn4[1:2, :]
        s.g4[rows16(i), :] = mish_slope(zv) * (s.bc[i // 8, i % 8].astype(F32) * v)
        return 0

    rows_loop(16, halo_four)

    res = ar_recv(4)
    back_params(res, 2560, s.bn4, 512)

    def grad_four(i, _):
        v = valid_at(i) * edge_at(i)
        windows(i, grad_of(s.g4[rows16(i), :], s.y4[rows16(i), :], s.bn4, v).astype(BF).astype(F32))
        return 0

    rows_loop(32, grad_four)

    def back_four(h, _):
        col = al(h * 256, 256)
        acc = None
        for t in range(9):
            part = mm_nt(
                s.X[pl.ds((2 - t % 3) * 512 + (2 - t // 3) * 128, 256), :], s.ws[t, pl.ds(col, 256), :]
            )
            acc = part if acc is None else acc + part
        cols = pl.ds(col, 256)
        gz = s.dm[:, cols] * acc
        s.dm[:, cols] = gz
        xh = s.ym[pl.ds(128, 256), cols] * s.bnm[2:3, cols] + s.bnm[3:4, cols]
        st[5][0:1, cols] = jnp.sum(gz, axis=0, keepdims=True)
        st[5][1:2, cols] = jnp.sum(gz * xh, axis=0, keepdims=True)
        return 0

    lax.fori_loop(0, 2, back_four, 0)
    ar_send(5)

    s.G4[myrows, :] = s.X[640:896, :]
    cp_g4 = to_sib(s.G4.at[myrows], s.G4.at[myrows])
    cp_g4.start()
    both_waits(cp_low, 0)
    both_waits(cp_m0, 0)
    cp_g4.wait()

    for k in range(3):
        for dc in range(2):
            for j in range(4):
                cp = x_copy(dc, j, k)
                x_when(dc, j, k, cp.wait if dc == 0 and j == 0 else cp.wait_send)

    def piece3(j):
        piece(s.MT, plane[j], s.G4, st3)

    piece3(3)
    for hf in range(2):
        plane_start(0, hf, 1)

    @pl.when(c == 0)
    def _():
        for hf in range(2):
            plane_second(1, hf)

    piece3(1)
    piece3(2)

    res = ar_recv(5)
    back_params(res, 2048, s.bnm, 512)

    def grad_mid(i, _):
        val = grad_of(
            s.dm[rows16(i), :], s.ym[pl.ds(al(128 + i * 16, 16), 16), :], s.bnm, valid_at(i)
        ).astype(BF)
        s.gm[rows16(i), :] = val
        s.GB[pl.ds(al(c * 256 + i * 16, 16), 16), :] = val
        return 0

    rows_loop(16, grad_mid)

    def back_mid(h, _):
        col = al(h * 256, 256)
        cols = pl.ds(col, 256)
        acc = mm_nt(s.gm[...], s.wm[cols, :]).reshape(2, 8, 16, 256)
        t1 = jnp.zeros((16, 256), F32)
        t2 = jnp.zeros((16, 256), F32)
        for rr in range(2):
            for n in range(8):
                rows = pl.ds(rr * 128 + n * 16, 16)
                cot = s.sc[rr, n, :, pl.ds(al(512 + h * 256, 256), 256)].astype(F32) + s.bc[
                    1 + rr, n, :, cols
                ].astype(F32)
                gz = s.dr[rows, cols] * (acc[rr, n] + cot * vs[n])
                s.dr[rows, cols] = gz
                t1 = t1 + gz
                t2 = t2 + gz * (s.yr[rows, cols] * s.bnr[2:3, cols] + s.bnr[3:4, cols])
        st[6][0:1, cols] = jnp.sum(t1, axis=0, keepdims=True)
        st[6][1:2, cols] = jnp.sum(t2, axis=0, keepdims=True)
        return 0

    lax.fori_loop(0, 2, back_mid, 0)
    ar_send(6)
    for hf in range(2):
        plane_second(0, hf)

    cp_gb = to_sib(s.gm, s.GB.at[myrows])

    @pl.when(c == 0)
    def _():
        cp_gb.start()

    piece3(0)
    both_waits(cp_gb, 0)

    @pl.when(c == 1)
    def _():
        piece(s.J2X, 3, s.G4, s.st2)
        piece(s.J2X, 2, s.GB, s.st2)

    res = ar_recv(6)
    back_params(res, 1536, s.bnr, 512)

    def grad_right(i, _):
        val = grad_of(s.dr[rows16(i), :], s.yr[rows16(i), :], s.bnr, valid_at(i)).astype(BF)
        s.gr[rows16(i), :] = val

        return 0

    rows_loop(16, grad_right)

    def back_one(h, _):
        cols = pl.ds(al(h * 256, 256), 256)
        acc = mm_nt(s.glb[...], s.wl[cols, :]) + mm_nt(s.gr[...], s.wr[cols, :])
        gz = s.d1[:, cols] * acc
        s.d1[:, cols] = gz
        xh = s.y1[:, cols] * s.bn0[2:3, cols] + s.bn0[3:4, cols]
        st[7][0:1, cols] = jnp.sum(gz, axis=0, keepdims=True)
        st[7][1:2, cols] = jnp.sum(gz * xh, axis=0, keepdims=True)
        return 0

    lax.fori_loop(0, 4, back_one, 0)
    ar_send(7)
    for hf in range(2):
        plane_start(0, hf, 0)

    @pl.when(c == 1)
    def _():
        s.GA[myrows, :] = s.gr[...]

    cp_gr = to_sib(s.gr, s.GA.at[myrows])

    @pl.when(c == 0)
    def _():
        cp_gr.start()

    both_waits(cp_gr, 0)

    @pl.when(c == 1)
    def _():
        for k in (0, 1):
            piece(s.J2X, k, s.GA, s.st2)

    res = ar_recv(7)
    back_params(res, 0, s.bn0, 1024)

    def grad_one(i, _):
        val = grad_of(s.d1[rows16(i), :], s.y1[rows16(i), :], s.bn0, valid_at(i))
        low = val.astype(BF)
        s.G0[rows16(i), :] = low
        s.Gall[pl.ds(al(own8 * 256 + i * 16, 16), 16), :] = low
        return 0

    rows_loop(16, grad_one)

    halo_up(7, s.G0.at[pl.ds(0, 128)], s.G0.at[pl.ds(256, 128)])

    def g_block(core, batch, q):
        return s.Gall.at[pl.ds(al((core * 4 + batch) * 256, 256), 256), pl.ds(al(q * 256, 256), 256)]

    def g_direct(q, j):
        blk = g_block(c, b, q)
        return remote(blk, blk, s.gs.at[q, j - 1], s.grs.at[q, j - 1], (r, plane[j]))

    def g_forward(q, j):
        blk = g_block(c, plane[j], q)
        return remote(blk, blk, s.gfs.at[q, j], s.gfr.at[q, j], sib)

    is_tap8 = jnp.logical_and(c == 0, y == 0)
    has_plane2 = jnp.logical_not(is_tap8)

    for q in range(4):
        for j in (1, 2, 3):
            g_direct(q, j).start()
        g_forward(q, 0).start()
        if q == 3:

            @pl.when(c == 1)
            def _():
                for m in (1, 0):
                    for hf in range(2):
                        plane_start(1, hf, m)


    for dc in range(2):
        for j in range(4):
            if dc or j:
                idx = dc * 4 + j
                src8 = ((c + dc) % 2) * 4 + plane[j]
                for k in range(3):
                    dst = s.XG.at[k, :, pl.ds(al(src8 * 256, 256), 256)]
                    x_got = lambda: recv_wait(dst, s.xr.at[k, idx])
                    if k < 2:
                        x_got()
                    else:
                        pl.when(is_tap8)(x_got)

    def half_tile(ref, k, q, h):
        return ref.at[k, q, pl.ds(h * 128, 128)]

    def chain(zp, q, own, put, here):
        @pl.when(jnp.logical_and(here, jnp.logical_and(q >= 0, q < 4)))
        def _():
            val = own(q)

            def below(h):
                got = half_tile(s.zb, zp - 1, q, h)
                recv_wait(got, s.zur.at[zp, 2 * q + h])
                return got[...].astype(F32)

            def above(h):
                got = half_tile(s.za, zp, q, h)
                recv_wait(got, s.zdr.at[zp, 2 * q + h])
                return got[...].astype(F32)

            def mine(h):
                return val[h * 128 : h * 128 + 128]

            def up(h, v):
                part = half_tile(s.zs, zp, q, h)
                part[...] = v.astype(BF)
                there = half_tile(s.zb, zp - 1, q, h)
                remote(part, there, s.zus.at[zp, 2 * q + h], s.zur.at[zp, 2 * q + h], (r + 2, b)).start()

            def down(h, v):
                part = half_tile(s.zs, zp, q, h)
                part[...] = v.astype(BF)
                there = half_tile(s.za, zp, q, h)
                remote(part, there, s.zds.at[zp, 2 * q + h], s.zdr.at[zp, 2 * q + h], (r - 2, b)).start()

            def each(do):
                def both():
                    for h in range(2):
                        do(h)

                return both

            if zp > 0:
                pl.when(z == 0)(each(lambda h: up(h, mine(h))))
            if zp > 1:
                pl.when(jnp.logical_and(z > 0, z < zp))(each(lambda h: up(h, mine(h) + below(h))))
            if zp < 3:
                pl.when(z == 3)(each(lambda h: down(h, mine(h))))
            if zp < 2:
                pl.when(jnp.logical_and(z > zp, z < 3))(each(lambda h: down(h, mine(h) + above(h))))

            @pl.when(z == zp)
            def _():
                for h in range(2):
                    v = mine(h)
                    if zp > 0:
                        v = v + below(h)
                    if zp < 3:
                        v = v + above(h)
                    put(q, h, v)

    def put_down(q, h, v):
        for i in range(2):
            s.wgo[pl.ds(h * 1024 + 2 * q + i, 128, stride=8), :] = v[:, i * 128 : i * 128 + 128]

    def put_tile(q, h, v):
        base = (q // 2) * 1024 + h * 512 + (q % 2) * 2
        for i in range(2):
            s.wgo[pl.ds(base + i, 128, stride=4), :] = v[:, i * 128 : i * 128 + 128]

    def chain_drain(zp, q):
        for h in range(2):
            part = half_tile(s.zs, zp, q, h)
            if zp > 0:

                @pl.when(z < zp)
                def _():
                    pltpu.make_async_copy(part, part, s.zus.at[zp, 2 * q + h]).wait()

            if zp < 3:

                @pl.when(z > zp)
                def _():
                    pltpu.make_async_copy(part, part, s.zds.at[zp, 2 * q + h]).wait()

    def own_plane(stage, slots, q):
        rows = pl.ds(al((q // 2) * 256, 256), 256)
        cols = pl.ds(al((q % 2) * 256, 256), 256)
        v = stage[b, rows, cols].astype(F32)
        for m in (0, 2):
            v = v + slots[m, rows, cols].astype(F32)
        return v

    def own_down(k, q):
        return mm(s.XG[k], s.Gall[:, pl.ds(al(q * 256, 256), 256)])

    def shift_one(i, _):
        n = i % 8
        for h in range(2):
            cols = pl.ds(h * 512, 512)
            s.pad[n, 8:24, :] = s.G0[rows16(i), cols].astype(F32)
            s.Gp[rows16(i), cols] = s.pad[n, 9:25, :].astype(BF)
        return 0

    lax.fori_loop(0, 16, shift_one, 0)

    def back_conv(h, par):
        ch = pl.ds(al(h * 256, 256), 256)

        def part(src, row, tap):
            return mm_nt(src[pl.ds(row * 128, 256), :], s.wd[tap, ch, :])

        if par == 0:
            even = part(s.G0, 0, 4)
            odd = part(s.G0, 0, 5) + part(s.Gp, 0, 3)
        else:
            even = part(s.G0, 0, 7) + part(s.G0, 1, 1)
            odd = (part(s.G0, 0, 8) + part(s.Gp, 0, 6)) + (part(s.G0, 1, 2) + part(s.Gp, 1, 0))
        for q in range(2):
            s.igf[q, pl.ds(0, 256, stride=2), :] = even[:, q * 128 : q * 128 + 128]
            s.igf[q, pl.ds(1, 256, stride=2), :] = odd[:, q * 128 : q * 128 + 128]
        for rr in range(2):
            for q in range(2):
                s.inraw[2 * rr + par, :, :, pl.ds(al(h * 256 + q * 128, 128), 128)] = (
                    s.igf[q, rr * 256 : rr * 256 + 256, :].astype(BF).reshape(8, 32, 128)
                )

    left2 = jnp.logical_and(c == 0, y == 1)
    late2 = c == 1

    def step(slot, _):
        pl.when(slot < 2)(lambda: back_conv(slot, 0))

        @pl.when(slot == 0)
        def _():
            for hf in range(2):
                plane_got(0, hf, 0)
                plane_got(0, hf, 2)
            run_tiles(job3, z == 0, 0, 4)

        @pl.when(jnp.logical_and(slot == 0, c == 0))
        def _():
            for hf in range(2):
                plane_got(1, hf, 0)
                plane_got(1, hf, 2)
            run_tiles(job2, jnp.logical_and(left2, z % 3 == 0), 0, 4)

        @pl.when(slot < 4)
        def _():
            for j in (1, 2, 3):
                recv_wait(g_block(c, plane[j], slot), s.grs.at[slot, j - 1])
                g_forward(slot, j).start()
            for j in range(4):
                recv_wait(g_block(1 - c, plane[j], slot), s.gfr.at[slot, j])

        job0(slot - (3 - z), z > 0)
        job1(slot - jnp.where(z == 0, 0, 4 - z), z != 1)
        tap8(slot - 2 * z, jnp.logical_and(is_tap8, z < 2))
        pl.when(jnp.logical_and(slot >= 1, slot < 3))(lambda: run_tiles(job3, z == 1, 2 * slot - 2, 2))
        pl.when(jnp.logical_and(slot >= 3, slot < 5))(lambda: run_tiles(job3, z == 2, 2 * slot - 6, 2))
        pl.when(slot == 3)(lambda: run_tiles(job2, jnp.logical_and(left2, z == 1), 0, 4))

        @pl.when(slot == 3)
        def _():
            halo_up_wait(7, s.G0.at[pl.ds(256, 128)])
            lax.fori_loop(16, 24, shift_one, 0)

        @pl.when(jnp.logical_and(slot == 3, c == 1))
        def _():
            for hf in range(2):
                plane_second(1, hf)

        pl.when(jnp.logical_and(slot >= 3, slot < 5))(lambda: back_conv(slot - 3, 1))

        @pl.when(jnp.logical_and(slot == 4, c == 1))
        def _():
            for hf in range(2):
                plane_got(1, hf, 0)
                plane_got(1, hf, 2)
            run_tiles(job2, jnp.logical_and(late2, z % 3 == 0), 0, 4)

        return 0

    def job0(q, here):
        chain(0, q, lambda q: own_down(0, q), put_down, here)

    def job1(q, here):
        chain(1, q, lambda q: own_down(1, q), put_down, here)

    def tap8(q, here):
        chain(2, q, lambda q: own_down(2, q), put_down, here)

    def job2(q, here):
        chain(2, q, lambda q: own_plane(s.st2, s.pr2, q), put_tile, here)

    def job3(q, here):
        chain(3, q, lambda q: own_plane(st3, s.pr3, q), put_tile, here)

    def run_tiles(job, here, first, n):
        def body(q, _):
            job(first + q, here)
            return 0

        @pl.when(here)
        def _():
            lax.fori_loop(0, n, body, 0)

    lax.fori_loop(0, 6, step, 0)
    for i in range(4):
        store(s.inraw.at[i], ig_ref.at[:, i])
    run_tiles(tap8, jnp.logical_and(is_tap8, z == 3), 0, 4)
    run_tiles(job1, z == 1, 0, 4)
    run_tiles(job0, z == 0, 0, 4)
    run_tiles(job2, jnp.logical_and(late2, z == 1), 0, 4)
    run_tiles(job3, z == 3, 0, 4)
    run_tiles(job2, jnp.logical_and(has_plane2, z == 2), 0, 4)
    run_tiles(tap8, jnp.logical_and(is_tap8, z == 2), 0, 4)
    store(s.wgo, wg_ref)

    for q in range(4):
        for zp in range(4):
            chain_drain(zp, q)
        for j in (1, 2, 3):
            g_direct(q, j).wait_send()
        for j in range(4):
            g_forward(q, j).wait_send()
    for job in range(2):
        for hf in range(2):
            for m in range(3):
                plane_sent(job, hf, m)
    for cp in outs:
        cp.wait()


def hand_over(n, *refs):
    ins, outs, held = refs[:n], refs[n : 2 * n], refs[2 * n : 3 * n]
    sems = refs[3 * n]
    got = [pltpu.make_async_copy(ins[i], held[i], sems.at[0, i]) for i in range(n)]
    put = [pltpu.make_async_copy(held[i], outs[i], sems.at[1, i]) for i in range(n)]
    for cp in got:
        cp.start()
    for i in range(n):
        got[i].wait()
        put[i].start()
    for cp in put:
        cp.wait()


def fused_step(
    inputs, counts, down_weight, left_weight, right_weight, reduce_weight, spread_weight,
    norm_gains, norm_biases, running_mean, running_var, section_cotangent, block_cotangent,
):
    table = scratch_table()
    names = tuple(table)
    sds = jax.ShapeDtypeStruct
    row = (1, 3072)
    vmem = pl.BlockSpec(memory_space=pltpu.VMEM)
    smem = pl.BlockSpec(memory_space=pltpu.SMEM)
    hbm = pl.BlockSpec(memory_space=pl.ANY)
    outs = pl.pallas_call(
        functools.partial(fused_kernel, names, 13, 8),
        out_shape=(
            sds((8, 2, 16, 1024), BF),
            sds((8, 2, 16, 512), BF),
            sds((8, 4, 32, 512), BF),
            sds((2048, 128), F32),
            sds(row, F32),
            sds(row, F32),
            sds(row, F32),
            sds(row, F32),
        ),
        in_specs=[hbm, smem, hbm, hbm, hbm, hbm, hbm, vmem, vmem, vmem, vmem, hbm, hbm],
        out_specs=(hbm, hbm, hbm, hbm, vmem, vmem, vmem, vmem),
        scratch_shapes=list(table.values()),
        compiler_params=pltpu.CompilerParams(
            collective_id=0, has_side_effects=True, vmem_limit_bytes=64 * 2**20 - 2**16
        ),
        cost_estimate=pl.CostEstimate(flops=13 * 10**9, bytes_accessed=21 * 10**6, transcendentals=10**6),
    )(
        inputs, counts, down_weight.reshape((9,) + down_weight.shape[2:]), left_weight, right_weight,
        reduce_weight, spread_weight.reshape((9,) + spread_weight.shape[2:]),
        norm_gains.reshape(row), norm_biases.reshape(row), running_mean.reshape(row), running_var.reshape(row),
        section_cotangent, block_cotangent,
    )
    n = len(outs)
    so, bo, ig, wg, gg, bg, nm, nv = pl.pallas_call(
        functools.partial(hand_over, n),
        out_shape=tuple(sds(o.shape, o.dtype) for o in outs),
        in_specs=[hbm] * n,
        out_specs=(hbm,) * n,
        scratch_shapes=[pltpu.VMEM(o.shape, o.dtype) for o in outs] + [pltpu.SemaphoreType.DMA((2, n))],
        cost_estimate=pl.CostEstimate(flops=0, bytes_accessed=6 * 10**6, transcendentals=0),
    )(*outs)
    return (so, bo, ig, wg.reshape(-1), gg.reshape(-1), bg.reshape(-1), nm.reshape(-1), nv.reshape(-1))


def fits_fused(mesh):
    return dict(mesh.shape) == {"rows": 8, "batch": 4}


def solution(mesh):
    placed = (
        P("batch", "rows", None, None),
        P("batch"),
        P(),
        P(),
        P(),
        P(),
        P(),
        P(),
        P(),
        P(),
        P(),
        P("batch", "rows", None, None),
        P("batch", "rows", None, None),
    )
    return jax.shard_map(
        fused_step if fits_fused(mesh) else on_device,
        mesh=mesh,
        in_specs=placed,
        out_specs=(
            P("batch", "rows", None, None),
            P("batch", "rows", None, None),
            P("batch", "rows", None, None),
            P(("rows", "batch")),
            P(),
            P(),
            P(),
            P(),
        ),
        check_vma=False,
    )
```
